32 devices in a mesh: dp: 8 (over z, x), tensor: 4 (over y, core).
Axes of the slice: x: 2, y: 2, z: 4, core: 2. Of those that a mesh axis runs over, the one named last changes fastest.
Arguments:
- prompt_in: bfloat16 [8192, 1024], P('dp'), may hold values from -6 to 6
- cont_in: bfloat16 [2048, 1024], P('dp'), may hold values from -6 to 6
- prompt_cot: bfloat16 [8192, 1024], P('dp'), may hold values from -6 to 6
- cont_cot: bfloat16 [2048, 1024], P('dp'), may hold values from -6 to 6
- group_of: int32 [16], replicated, may hold values from 0 to 7, as said below
- offsets: int32 [16], replicated, may hold values from 512 to 1024, as said below
- ln1_gain: bfloat16 [1024], replicated, may hold values from 0.5 to 1.5
- ln1_bias: bfloat16 [1024], replicated, may hold values from -4 to 4
- ln2_gain: bfloat16 [1024], replicated, may hold values from 0.5 to 1.5
- ln2_bias: bfloat16 [1024], replicated, may hold values from -4 to 4
- qkv_weight: bfloat16 [1024, 3072], P(None, 'tensor'), may hold values from -0.25 to 0.25
- qkv_bias: bfloat16 [3072], P('tensor'), may hold values from -6 to 6
- dense_weight: bfloat16 [1024, 1024], P('tensor'), may hold values from -2 to 2
- dense_bias: bfloat16 [1024], replicated, may hold values from -4 to 4
- fc1_weight: bfloat16 [1024, 4096], P(None, 'tensor'), may hold values from -0.1875 to 0.1875
- fc1_bias: bfloat16 [4096], P('tensor'), may hold values from -6 to 6
- fc2_weight: bfloat16 [4096, 1024], P('tensor'), may hold values from -0.09375 to 0.09375
- fc2_bias: bfloat16 [1024], replicated, may hold values from -4 to 4
Outputs:
- prompt_out: bfloat16 [8192, 1024], P('dp')
- cont_out: bfloat16 [2048, 1024], P('dp')
- prompt_grad: bfloat16 [8192, 1024], P('dp')
- cont_grad: bfloat16 [2048, 1024], P('dp')
- ln1_gain_grad: float32 [1024], replicated
- ln1_bias_grad: float32 [1024], replicated
- ln2_gain_grad: float32 [1024], replicated
- ln2_bias_grad: float32 [1024], replicated
- qkv_weight_grad: float32 [1024, 3072], P(None, 'tensor')
- qkv_bias_grad: float32 [3072], P('tensor')
- dense_weight_grad: float32 [1024, 1024], P('tensor')
- dense_bias_grad: float32 [1024], replicated
- fc1_weight_grad: float32 [1024, 4096], P(None, 'tensor')
- fc1_bias_grad: float32 [4096], P('tensor')
- fc2_weight_grad: float32 [4096, 1024], P('tensor')
- fc2_bias_grad: float32 [1024], replicated
The draws below stay inside these ranges and needn't reach their ends.
Inputs may be any that keep to these rules, and one draw needn't show every extreme that they name: `group_of`: each of the 8 groups is named by exactly 2 continuations. Continuation j sees the first offsets[j] tokens of its group's prompt, and its tokens stand at positions offsets[j] onward.
All inputs are finite; a program needn't handle non-finite values.
Results may differ from the reference program's by a relative error of at most 0.017.
The reference program's roundings to bfloat16 on the way count: a program that leaves them out, or rounds other values in their place, can miss the bound.
Values may be sent and summed in bfloat16 or wider, within the bound.
A program may use at most 256 MiB of HBM per device.

```python
import math
import jax
import jax.numpy as jnp
from jax import lax

D = 1024
HEADS = 16
HD = 64
ROT = 16
FF = 4096
PROMPT = 1024
CONT_LEN = 128
GROUPS = 8
CONTS = 16
N_TENSOR = 4


def draw_group_of(key, part):
    key = jax.random.fold_in(key, 3)
    return (jax.random.permutation(key, CONTS) % GROUPS).astype(jnp.int32)


def draw_offsets(key, part):
    key = jax.random.fold_in(key, 7)
    values = jax.random.randint(key, (CONTS,), PROMPT // 2, PROMPT + 1).astype(jnp.int32)
    return values.at[0].set(PROMPT).at[1].set(PROMPT // 2)


def shard_levels(stream_key, extent, shards, least, high):
    factor_of = 1.0
    for position, parts in shards:
        draws = jax.random.uniform(jax.random.fold_in(jax.random.fold_in(stream_key, 6), position), (parts,), jnp.float32, least / len(shards), high / len(shards))
        factor_of = factor_of * jnp.repeat(jnp.exp(draws), extent[position] // parts).reshape((-1,) + (1,) * (len(extent) - 1 - position))
    return factor_of


def centred(key, shape, width, limit, split=(), held_as=jnp.bfloat16):
    entries = jax.random.normal(key, shape, jnp.float32) * width
    if len(split) > 0:
        entries = shard_levels(key, shape, split, -0.22, 0.18) * entries
    return jnp.clip(entries, min=-limit, max=limit).astype(held_as)


def setup_inputs(seed: int = 0) -> dict:
    key_of = jax.random.split(jax.random.key(seed), 19)
    return {
        "prompt_in": centred(key_of[0], (GROUPS * PROMPT, D), 1.0, 6.0, ((0, 8),)),
        "cont_in": centred(key_of[1], (CONTS * CONT_LEN, D), 1.0, 6.0, ((0, 8),)),
        "prompt_cot": centred(key_of[2], (GROUPS * PROMPT, D), 1.0, 6.0, ((0, 8),)),
        "cont_cot": centred(key_of[3], (CONTS * CONT_LEN, D), 1.0, 6.0, ((0, 8),)),
        "group_of": draw_group_of(jax.random.fold_in(key_of[18], 71), 0),
        "offsets": draw_offsets(jax.random.fold_in(key_of[18], 71), 0),
        "ln1_gain": jnp.clip(1.0 + 0.1 * jax.random.normal(key_of[6], (D,), jnp.float32), 0.5, 1.5).astype(jnp.bfloat16),
        "ln1_bias": centred(key_of[7], (D,), 0.3, 4.0),
        "ln2_gain": jnp.clip(1.0 + 0.1 * jax.random.normal(key_of[8], (D,), jnp.float32), 0.5, 1.5).astype(jnp.bfloat16),
        "ln2_bias": centred(key_of[9], (D,), 0.3, 4.0),
        "qkv_weight": centred(key_of[10], (D, 3 * D), (D // 2) ** -0.5, 0.25, ((1, 4),)),
        "qkv_bias": centred(key_of[11], (3 * D,), 0.5, 6.0, ((0, 4),)),
        "dense_weight": centred(key_of[12], (D, D), (max(D // 128, 1)) ** -0.5, 2.0, ((0, 4),)),
        "dense_bias": centred(key_of[13], (D,), 0.3, 4.0),
        "fc1_weight": centred(key_of[14], (D, FF), D ** -0.5, 0.1875, ((1, 4),)),
        "fc1_bias": centred(key_of[15], (FF,), 0.5, 6.0, ((0, 4),)),
        "fc2_weight": centred(key_of[16], (FF, D), FF ** -0.5, 0.09375, ((0, 4),)),
        "fc2_bias": centred(key_of[17], (D,), 0.3, 4.0),
    }


@jax.custom_vjp
def low(v):
    return lax.optimization_barrier(v.astype(jnp.bfloat16)).astype(jnp.float32)

@jax.custom_vjp
def low_back(v):
    return v

def low_keep(v):
    return (low(v), None)

def low_pass(kept, grad):
    return (grad,)

def back_keep(v):
    return (v, None)

def back_low(kept, grad):
    return (low(grad),)
low.defvjp(low_keep, low_pass)
low_back.defvjp(back_keep, back_low)
eps_norm = 1e-05
masked_value = -1e+30
highest = lax.Precision.HIGHEST

def norm_rows(rows_in, gain_vec, shift_vec):
    row_mean = lax.optimization_barrier(jnp.mean(rows_in, axis=-1, keepdims=True))
    centered = rows_in - row_mean
    variance = lax.optimization_barrier(jnp.mean(centered * centered, axis=-1, keepdims=True))
    return centered * lax.rsqrt(variance + eps_norm) * gain_vec + shift_vec

def rotary_tables(positions):
    half_rot = ROT // 2
    frequencies = jnp.exp(-jnp.arange(half_rot, dtype=jnp.float32) * (2.0 * math.log(10000.0) / ROT))
    angles = positions.astype(jnp.float32)[:, None] * frequencies[None, :]
    angles = jnp.concatenate([angles, angles], axis=1)
    return (jnp.cos(angles), jnp.sin(angles))

def turn(rows_in, cos_table, sin_table):
    half_rot = ROT // 2
    rotated = rows_in[..., :ROT]
    swapped = jnp.concatenate([-rotated[..., half_rot:], rotated[..., :half_rot]], axis=-1)
    rotated = rotated * cos_table[:, None, :] + swapped * sin_table[:, None, :]
    return jnp.concatenate([rotated, rows_in[..., ROT:]], axis=-1)

def product(first_op, second_op):
    return jnp.dot(first_op, second_op, precision=highest, preferred_element_type=jnp.float32)

def reference(prompt_in, cont_in, prompt_cot, cont_cot, group_of, offsets, ln1_gain, ln1_bias, ln2_gain, ln2_bias, qkv_weight, qkv_bias, dense_weight, dense_bias, fc1_weight, fc1_bias, fc2_weight, fc2_bias):
    prompt_rows = GROUPS * PROMPT
    cont_rows = CONTS * CONT_LEN
    steps_along = jnp.arange(CONT_LEN, dtype=jnp.int32)
    positions = jnp.concatenate([jnp.tile(jnp.arange(PROMPT, dtype=jnp.int32), GROUPS), (offsets[:, None] + steps_along[None, :]).reshape(-1)])
    cos_table, sin_table = rotary_tables(positions)
    score_scale = 1.0 / math.sqrt(HD)
    head_cols = HEADS * HD // N_TENSOR
    unit_cols = FF // N_TENSOR
    prompt_mask = jnp.arange(PROMPT, dtype=jnp.int32)[:, None] >= jnp.arange(PROMPT, dtype=jnp.int32)[None, :]
    key_cols = jnp.arange(PROMPT + CONT_LEN, dtype=jnp.int32)
    cont_mask = jnp.where(key_cols[None, :] < PROMPT, key_cols[None, :] < PROMPT + 1, key_cols[None, :] - PROMPT <= steps_along[:, None])

    def prompt_attend(pieces):
        queries, key_rows, value_rows = pieces
        scores = low_back(jnp.einsum('qhd,khd->hqk', queries, key_rows, precision=highest) * score_scale)
        scores = jnp.where(prompt_mask[None], scores, masked_value)
        soft_probs = low(jax.nn.softmax(scores, axis=-1))
        return jnp.einsum('hqk,khd->qhd', soft_probs, value_rows, precision=highest)

    def forward(prompt_x, cont_x, gain_one, shift_one, gain_two, shift_two, weight_qkv, bias_qkv, weight_dense, bias_dense, weight_up, bias_up, weight_down, bias_down):
        rows_x = jnp.concatenate([prompt_x, cont_x], axis=0)
        row_count = rows_x.shape[0]
        h_one = low(norm_rows(rows_x, gain_one, shift_one))
        h_two = low(norm_rows(rows_x, gain_two, shift_two))
        qkv = low_back(product(h_one, weight_qkv) + bias_qkv).reshape(row_count, HEADS, 3, HD)
        queries = low(turn(qkv[:, :, 0], cos_table, sin_table))
        key_rows = low(turn(qkv[:, :, 1], cos_table, sin_table))
        value_rows = low(qkv[:, :, 2])
        prompt_keys = key_rows[:prompt_rows]
        prompt_values = value_rows[:prompt_rows]

        def cont_attend(pieces):
            queries_c, keys_c, values_c, group_id, offset = pieces
            keys_p = lax.dynamic_slice_in_dim(prompt_keys, group_id * PROMPT, PROMPT, 0)
            values_p = lax.dynamic_slice_in_dim(prompt_values, group_id * PROMPT, PROMPT, 0)
            keys_every = jnp.concatenate([keys_p, keys_c], axis=0)
            values_every = jnp.concatenate([values_p, values_c], axis=0)
            allowed = jnp.where(key_cols[None, :] < PROMPT, key_cols[None, :] < offset, cont_mask)
            scores = low_back(jnp.einsum('qhd,khd->hqk', queries_c, keys_every, precision=highest) * score_scale)
            scores = jnp.where(allowed[None], scores, masked_value)
            soft_probs = low(jax.nn.softmax(scores, axis=-1))
            return jnp.einsum('hqk,khd->qhd', soft_probs, values_every, precision=highest)
        shaped = (GROUPS, PROMPT, HEADS, HD)
        out_prompt = lax.map(jax.checkpoint(prompt_attend), (queries[:prompt_rows].reshape(shaped), prompt_keys.reshape(shaped), prompt_values.reshape(shaped)))
        cont_shape = (CONTS, CONT_LEN, HEADS, HD)
        out_cont = lax.map(jax.checkpoint(cont_attend), (queries[prompt_rows:].reshape(cont_shape), key_rows[prompt_rows:].reshape(cont_shape), value_rows[prompt_rows:].reshape(cont_shape), group_of, offsets))
        attended = jnp.concatenate([out_prompt.reshape(prompt_rows, HEADS * HD), out_cont.reshape(cont_rows, HEADS * HD)], axis=0)
        attended = low(low_back(attended))
        hidden = low_back(product(h_two, weight_up) + bias_up)
        gelu_out = low(jax.nn.gelu(hidden, approximate=False))
        result = rows_x + bias_dense + bias_down
        for shard_id in range(N_TENSOR):
            head_part = product(attended[:, shard_id * head_cols:(shard_id + 1) * head_cols], weight_dense[shard_id * head_cols:(shard_id + 1) * head_cols])
            unit_part = product(gelu_out[:, shard_id * unit_cols:(shard_id + 1) * unit_cols], weight_down[shard_id * unit_cols:(shard_id + 1) * unit_cols])
            result = result + low(head_part + unit_part)
        return (result[:prompt_rows], result[prompt_rows:])
    floats = tuple((a.astype(jnp.float32) for a in (prompt_in, cont_in, ln1_gain, ln1_bias, ln2_gain, ln2_bias, qkv_weight, qkv_bias, dense_weight, dense_bias, fc1_weight, fc1_bias, fc2_weight, fc2_bias)))
    outputs, pullback = jax.vjp(forward, *floats)
    gradients = pullback((prompt_cot.astype(jnp.float32), cont_cot.astype(jnp.float32)))
    return (outputs[0].astype(jnp.bfloat16), outputs[1].astype(jnp.bfloat16), gradients[0].astype(jnp.bfloat16), gradients[1].astype(jnp.bfloat16), gradients[2], gradients[3], gradients[4], gradients[5], gradients[6], gradients[7], gradients[8], gradients[9], gradients[10], gradients[11], gradients[12], gradients[13])
```

```python
import functools
import math

import jax
import jax.numpy as jnp
import numpy as np
from jax import lax
from jax.experimental import pallas as pl
from jax.experimental.pallas import tpu as pltpu
from jax.sharding import PartitionSpec as P

HD = 64
ROT = 16
CONT_LEN = 128
TILE = 256
CHUNK = 128
MEMBERS = 2

eps_norm = 1e-05
masked_value = -1e30
MESH = pl.DeviceIdType.MESH
bf16 = jnp.bfloat16
f32 = jnp.float32


def dot(a, b):
    return jnp.dot(a, b, preferred_element_type=f32)


def dot_nt(a, b):
    return lax.dot_general(a, b, (((1,), (1,)), ((), ())), preferred_element_type=f32)


def dot_tn(a, b):
    return lax.dot_general(a, b, (((0,), (0,)), ((), ())), preferred_element_type=f32)


def row_stats(x):
    centered = x - jnp.mean(x, axis=-1, keepdims=True)
    scale = lax.rsqrt(jnp.mean(centered * centered, axis=-1, keepdims=True) + eps_norm)
    return centered * scale, scale


def norm_pull(x, e):
    xhat, scale = row_stats(x)
    return scale * (
        e
        - jnp.mean(e, axis=-1, keepdims=True)
        - xhat * jnp.mean(e * xhat, axis=-1, keepdims=True)
    )


def gelu_and_slope(u):
    t = 1.0 / (1.0 + jnp.abs(u) * (0.3275911 / math.sqrt(2.0)))
    bell = jnp.exp(-0.5 * u * u)
    poly = t * (
        0.127414796
        + t * (-0.142248368 + t * (0.7107068705 + t * (-0.7265760135 + t * 0.5307027145)))
    )
    tail = poly * bell
    cdf = jnp.where(u >= 0, 1.0 - tail, tail)
    return u * cdf, cdf + u * bell * (1.0 / math.sqrt(2.0 * math.pi))


def rotary_table(length):
    half = ROT // 2
    frequencies = np.exp(
        -np.arange(half, dtype=np.float32) * np.float32(2.0 * math.log(10000.0) / ROT)
    ).astype(np.float32)
    angles = np.arange(length, dtype=np.float32)[:, None] * frequencies[None, :]
    angles = np.concatenate([angles, angles], axis=1).astype(np.float32)
    cos = np.ones((length, HD), np.float32)
    low = np.zeros((length, HD), np.float32)
    high = np.zeros((length, HD), np.float32)
    cos[:, :ROT] = np.cos(angles)
    low[:, :half] = -np.sin(angles)[:, :half]
    high[:, half:ROT] = np.sin(angles)[:, half:]
    return np.stack([np.concatenate([t, t], axis=1) for t in (cos, low, high)])


def ring_spot(device, n):
    odd = lax.rem(device, jnp.int32(2))
    half = lax.div(device, jnp.int32(2))
    return (1 - odd) * half + odd * (n - 1 - half)


def ring_device(spot, n):
    far = lax.div(spot, jnp.int32(n // 2))
    return (1 - far) * (2 * spot) + far * (2 * (n - 1 - spot) + 1)


def ring_neighbours(n):
    spot = ring_spot(lax.axis_index("dp"), n)
    after = ring_device(lax.rem(spot + 1, jnp.int32(n)), n)
    before = ring_device(lax.rem(spot + n - 1, jnp.int32(n)), n)
    return spot, after, before


def find_members(group_ref, wanted):
    count = group_ref.shape[0]
    first = jnp.int32(count)
    last = jnp.int32(-1)
    for j in range(count):
        hit = group_ref[j] == wanted
        first = jnp.minimum(first, jnp.where(hit, jnp.int32(j), jnp.int32(count)))
        last = jnp.maximum(last, jnp.where(hit, jnp.int32(j), jnp.int32(-1)))
    return jnp.minimum(first, count - 1), jnp.maximum(last, 0)


def meet(devices):
    barrier = pltpu.get_barrier_semaphore()
    for device in devices:
        pl.semaphore_signal(barrier, inc=1, device_id=device, device_id_type=MESH)
    pl.semaphore_wait(barrier, len(devices))


def remote(src, dst, send, recv, device):
    return pltpu.make_async_remote_copy(
        src_ref=src, dst_ref=dst, send_sem=send, recv_sem=recv, device_id=device, device_id_type=MESH
    )


def span(start, size, step):
    return pl.ds(pl.multiple_of(start, step), size)


def mlp_kernel(
    n_dp, n_tensor, group_ref, xp, xc, dp, dc, w1, w2, vecs,
    g_out, da_out, w1g_out, w2g_out, vec_out, picked_out,
    x_all, dy_all, w1_v, w2_v, g_all, h_all, du_all, da_all, w1g, w2g, ring,
    own_sem, load_sem, out_sem, send, recv,
):
    prompt_len, width = xp.shape
    cont_total = xc.shape[0]
    conts = cont_total // CONT_LEN
    rows = prompt_len + cont_total
    hidden = w1.shape[1]
    piece = CONT_LEN // n_tensor
    me_dp, me_t = lax.axis_index("dp"), lax.axis_index("tensor")
    spot, after, before = ring_neighbours(n_dp)

    own = [
        pltpu.make_async_copy(
            src.at[span(s * CONT_LEN + me_t * piece, piece, 16)], ring.at[spot, a, s], own_sem.at[a, s]
        )
        for a, src in enumerate((xc, dc))
        for s in range(conts)
    ]
    for c in own:
        c.start()
    loads = [
        pltpu.make_async_copy(src, dst, load_sem.at[i])
        for i, (src, dst) in enumerate(
            (
                (xp, x_all.at[pl.ds(0, prompt_len)]),
                (xc, x_all.at[pl.ds(prompt_len, cont_total)]),
                (w1, w1_v),
                (dp, dy_all.at[pl.ds(0, prompt_len)]),
                (dc, dy_all.at[pl.ds(prompt_len, cont_total)]),
                (w2, w2_v),
            )
        )
    ]
    for c in loads:
        c.start()
    meet([{"dp": after}, {"dp": before}])

    def steps(k):
        ahead = lax.rem(spot - k + n_dp, jnp.int32(n_dp))
        back = lax.rem(spot + k, jnp.int32(n_dp))
        return (
            remote(ring.at[ahead, 0], ring.at[ahead, 0], send.at[0, k], recv.at[0, k], {"dp": after}),
            remote(ring.at[back, 1], ring.at[back, 1], send.at[1, k], recv.at[1, k], {"dp": before}),
        )

    for c in own:
        c.wait()
    for c in steps(jnp.int32(0)):
        c.start()

    turns = rows // TILE + hidden // TILE
    per_turn = -(-(n_dp - 1) // turns)

    def tick(turn):
        def one(j, _):
            k = turn * per_turn + j

            @pl.when(k < n_dp - 1)
            def _():
                for c in steps(k):
                    c.wait()

            @pl.when(k < n_dp - 2)
            def _():
                for c in steps(k + 1):
                    c.start()

            return 0

        lax.fori_loop(0, per_turn, one, 0)

    for c in loads:
        c.wait()
    vec_out[...] = jnp.zeros_like(vec_out)
    gain, shift, bias = vecs[2:3], vecs[3:4], vecs[5:6, :hidden]

    def row_tile(i, _):
        at = span(i * TILE, TILE, TILE)
        xhat, _ = row_stats(x_all[at].astype(f32))
        h = (xhat * gain + shift).astype(bf16)
        h_all[at] = h
        dy = dy_all[at]
        for k in range(hidden // TILE):
            cols = slice(k * TILE, (k + 1) * TILE)
            u = dot(h, w1_v[:, cols]) + bias[:, cols]
            dg = dot_nt(dy, w2_v[cols, :])
            value, slope = gelu_and_slope(u)
            g_all[at, cols] = value.astype(bf16)
            du = (dg * slope).astype(bf16)
            du_all[at, cols] = du
            vec_out[3:4, cols] += jnp.sum(du.astype(f32), axis=0, keepdims=True)
        da = dot_nt(du_all[at], w1_v[...])
        da_all[at] = da.astype(bf16)
        xhat, _ = row_stats(x_all[at].astype(f32))
        vec_out[0:1] += jnp.sum(da * xhat, axis=0, keepdims=True)
        vec_out[1:2] += jnp.sum(da, axis=0, keepdims=True)
        vec_out[2:3] += jnp.sum(dy.astype(f32), axis=0, keepdims=True)
        tick(i)
        return 0

    lax.fori_loop(0, rows // TILE, row_tile, 0)
    outs = [
        pltpu.make_async_copy(src, dst, out_sem.at[i])
        for i, (src, dst) in enumerate(
            ((g_all, g_out), (da_all, da_out), (w2g, w2g_out), (w1g, w1g_out))
        )
    ]
    outs[0].start()
    outs[1].start()

    def down_tile(k, _):
        cols = span(k * TILE, TILE, TILE)
        w2g[cols, :] = dot_tn(g_all[:, cols], dy_all[...]).astype(bf16)
        tick(rows // TILE + k)
        return 0

    lax.fori_loop(0, hidden // TILE, down_tile, 0)
    outs[2].start()

    def up_tile(k, _):
        cols = span(k * TILE, TILE, TILE)
        w1g[cols, :] = dot_tn(h_all[:, cols], du_all[...]).astype(bf16)
        return 0

    lax.fori_loop(0, width // TILE, up_tile, 0)
    outs[3].start()

    for m, member in enumerate(find_members(group_ref, me_dp)):
        where = ring_spot(lax.div(member, jnp.int32(conts)), n_dp)
        slot = lax.rem(member, jnp.int32(conts))
        for a in range(2):
            picked_out[a, m] = ring[where, a, slot]
    for c in outs:
        c.wait()


def run_mlp(n_dp, n_tensor, group_of, xp, xc, dp, dc, w1, w2, vecs):
    prompt_len, width = xp.shape
    rows = prompt_len + xc.shape[0]
    conts = xc.shape[0] // CONT_LEN
    hidden = w1.shape[1]
    piece = CONT_LEN // n_tensor
    shape = jax.ShapeDtypeStruct
    hbm = pl.BlockSpec(memory_space=pl.ANY)
    vmem = pl.BlockSpec(memory_space=pltpu.VMEM)
    smem = pl.BlockSpec(memory_space=pltpu.SMEM)
    return pl.pallas_call(
        functools.partial(mlp_kernel, n_dp, n_tensor),
        out_shape=(
            shape((rows, hidden), bf16),
            shape((rows, width), bf16),
            shape((width, hidden), bf16),
            shape((hidden, width), bf16),
            shape((8, width), f32),
            shape((2, MEMBERS, piece, width), bf16),
        ),
        in_specs=[smem, hbm, hbm, hbm, hbm, hbm, hbm, vmem],
        out_specs=(hbm, hbm, hbm, hbm, vmem, vmem),
        scratch_shapes=[
            pltpu.VMEM((rows, width), bf16),
            pltpu.VMEM((rows, width), bf16),
            pltpu.VMEM((width, hidden), bf16),
            pltpu.VMEM((hidden, width), bf16),
            pltpu.VMEM((rows, hidden), bf16),
            pltpu.VMEM((rows, width), bf16),
            pltpu.VMEM((rows, hidden), bf16),
            pltpu.VMEM((rows, width), bf16),
            pltpu.VMEM((width, hidden), bf16),
            pltpu.VMEM((hidden, width), bf16),
            pltpu.VMEM((n_dp, 2, conts, piece, width), bf16),
            pltpu.SemaphoreType.DMA((2, conts)),
            pltpu.SemaphoreType.DMA((6,)),
            pltpu.SemaphoreType.DMA((4,)),
            pltpu.SemaphoreType.DMA((2, n_dp - 1)),
            pltpu.SemaphoreType.DMA((2, n_dp - 1)),
        ],
        compiler_params=pltpu.CompilerParams(
            collective_id=0, has_side_effects=True, vmem_limit_bytes=58 * 2**20
        ),
        cost_estimate=pl.CostEstimate(flops=14 * 10**9, bytes_accessed=20 * 10**6, transcendentals=10**6),
        name="mlp",
    )(group_of, xp, xc, dp, dc, w1, w2, vecs)


def attention_kernel(
    n_tensor, group_ref, offsets, picked, xp, dp, table, wqkv, wd, vecs,
    o_out, da_out, wqg_out, wdg_out, vec_out,
    x_all, dy_all, moved, h_all, tab, wqkv_v, wd_v, qs, ks, vs, dos, oh, dqs, dks, dvs, o_all, dqkv, da_all, wqg, wdg,
    load_sem, own_sem, y_send, y_recv, core_send, core_recv, out_sem,
):
    prompt_len, width = xp.shape
    conts = MEMBERS
    cont_total = conts * CONT_LEN
    rows = prompt_len + cont_total
    prompt_tiles = prompt_len // TILE
    local = wd.shape[0]
    heads = local // HD
    piece = CONT_LEN // n_tensor
    lines = n_tensor // 2
    table_len = table.shape[1]
    scale = 1.0 / math.sqrt(HD)
    me_dp, me_t = lax.axis_index("dp"), lax.axis_index("tensor")
    core = lax.rem(me_t, jnp.int32(2))
    sibling = me_t + 1 - 2 * core
    peers = [lax.rem(me_t + 2 * k, jnp.int32(n_tensor)) for k in range(1, lines)]

    mine = pltpu.make_async_copy(picked, moved.at[me_t], own_sem)
    mine.start()
    loads = [
        pltpu.make_async_copy(src, dst, load_sem.at[i])
        for i, (src, dst) in enumerate(
            (
                (xp, x_all.at[pl.ds(0, prompt_len)]),
                (wqkv, wqkv_v),
                (table, tab.at[:, pl.ds(0, table_len)]),
                (dp, dy_all.at[pl.ds(0, prompt_len)]),
                (wd, wd_v),
            )
        )
    ]
    for c in loads:
        c.start()
    meet([{"tensor": sibling}] + [{"tensor": p} for p in peers])
    mine.wait()
    over_y = [
        remote(moved.at[me_t], moved.at[me_t], y_send.at[k], y_recv.at[k], {"tensor": p})
        for k, p in enumerate(peers)
    ]
    over_core = [
        remote(
            moved.at[2 * j + core], moved.at[2 * j + core], core_send.at[j], core_recv.at[j], {"tensor": sibling}
        )
        for j in range(lines)
    ]
    for c in over_y:
        c.start()
    members = find_members(group_ref, me_dp)
    offs = [offsets[m] for m in members]
    for c in loads:
        c.wait()
    for m, off in enumerate(offs):
        for a in range(3):
            tab[a, table_len + m * CONT_LEN : table_len + (m + 1) * CONT_LEN, :] = tab[a, pl.ds(off, CONT_LEN), :]
    vec_out[...] = jnp.zeros_like(vec_out)
    gain, shift, bias = vecs[0:1], vecs[1:2], vecs[6:7, : 3 * local]
    lane = lax.broadcasted_iota(jnp.int32, (1, CHUNK), 1)

    def tables(start, c, sign):
        cos, low, high = (tab[a, pl.ds(start, TILE), :] for a in range(3))
        kinds = [(2 * c) % 3, (2 * c + 1) % 3]
        if 2 in kinds:
            turned = lane >= HD if kinds[0] == 2 else lane < HD
            cos = jnp.where(turned, cos, 1.0)
            low = jnp.where(turned, low, 0.0)
            high = jnp.where(turned, high, 0.0)
        return cos, low * sign, high * sign

    def turned(z, tabs):
        cos, low, high = tabs
        half = ROT // 2
        return z * cos + pltpu.roll(z, CHUNK - half, 1) * low + pltpu.roll(z, half, 1) * high

    def table_start(i):
        return pl.multiple_of(i * TILE + lax.div(i, jnp.int32(prompt_tiles)) * (table_len - prompt_len), CHUNK)

    def project(i, _):
        @pl.when(i == 1)
        def _():
            for c in over_y:
                c.wait()
            for c in over_core:
                c.start()

        @pl.when(i == prompt_tiles)
        def _():
            for c in over_core:
                c.wait()
            for q in range(n_tensor):
                for s in range(conts):
                    to = slice(prompt_len + s * CONT_LEN + q * piece, prompt_len + s * CONT_LEN + (q + 1) * piece)
                    x_all[to, :] = moved[q, 0, s]
                    dy_all[to, :] = moved[q, 1, s]

        at = span(i * TILE, TILE, TILE)
        xhat, _ = row_stats(x_all[at].astype(f32))
        h = (xhat * gain + shift).astype(bf16)
        h_all[at] = h
        for c in range(3 * local // CHUNK):
            cols = slice(c * CHUNK, (c + 1) * CHUNK)
            z = dot(h, wqkv_v[:, cols]) + bias[:, cols]
            z = turned(z, tables(table_start(i), c, 1.0)).astype(bf16)
            for part in range(2):
                head, kind = divmod(2 * c + part, 3)
                (qs, ks, vs)[kind][head, at] = z[:, part * HD : (part + 1) * HD]
        do = dot_nt(dy_all[at], wd_v[...]).astype(bf16)
        for head in range(heads):
            dos[head, at] = do[:, head * HD : (head + 1) * HD]
        return 0

    lax.fori_loop(0, rows // TILE, project, 0)

    query_lane = lax.broadcasted_iota(jnp.int32, (1, TILE), 1)
    reach = jnp.zeros((1, TILE), jnp.int32)
    for m, off in enumerate(offs):
        reach = jnp.where(lax.div(query_lane, jnp.int32(CONT_LEN)) == m, off, reach)

    def attend(head, _):
        for block in range(rows // TILE - 1, -1, -1):
            first = block * TILE
            seen = first + TILE
            at = slice(first, seen)
            q, do = qs[head, at], dos[head, at]
            k, v = ks[head, :seen], vs[head, :seen]
            s = dot_nt(k, q) * scale
            key = lax.broadcasted_iota(jnp.int32, (TILE, TILE), 0)
            query = lax.broadcasted_iota(jnp.int32, (TILE, TILE), 1)
            if block == prompt_tiles:
                key_row = lax.broadcasted_iota(jnp.int32, (prompt_len, TILE), 0)
                far = jnp.where(key_row < reach, s[:first], masked_value)
                same = lax.div(key, jnp.int32(CONT_LEN)) == lax.div(query, jnp.int32(CONT_LEN))
                near = jnp.where((key <= query) & same, s[first:], masked_value)
                s = jnp.concatenate([far, near], axis=0)
            else:
                near = jnp.where(key <= query, s[first:], masked_value)
                s = near if first == 0 else jnp.concatenate([s[:first], near], axis=0)
            p = jnp.exp(s - jnp.max(s, axis=0, keepdims=True))
            p = p * (1.0 / jnp.sum(p, axis=0, keepdims=True))
            low = p.astype(bf16)
            oh[head, at] = dot_tn(v, low).T.astype(bf16)
            dprob = dot_nt(v, do)
            delta = jnp.sum(p * dprob, axis=0, keepdims=True)
            ds = (p * (dprob - delta)).astype(bf16)
            dqs[head, at] = dot_tn(k, ds).T * scale
            dk = dot(ds, q) * scale
            dv = dot(low, do)
            if block == rows // TILE - 1:
                dks[head, :seen] = dk
                dvs[head, :seen] = dv
            else:
                dks[head, :seen] += dk
                dvs[head, :seen] += dv
        return 0

    lax.fori_loop(0, heads, attend, 0)

    def gather_back(i, _):
        at = span(i * TILE, TILE, TILE)
        for c in range(local // CHUNK):
            o_all[at, c * CHUNK : (c + 1) * CHUNK] = jnp.concatenate([oh[2 * c, at], oh[2 * c + 1, at]], axis=1)
        for c in range(3 * local // CHUNK):
            parts = []
            for part in range(2):
                head, kind = divmod(2 * c + part, 3)
                parts.append((dqs, dks, dvs)[kind][head, at])
            z = jnp.concatenate(parts, axis=1)
            z = turned(z, tables(table_start(i), c, -1.0)).astype(bf16)
            cols = slice(c * CHUNK, (c + 1) * CHUNK)
            dqkv[at, cols] = z
            vec_out[2:3, cols] += jnp.sum(z.astype(f32), axis=0, keepdims=True)
        da = dot_nt(dqkv[at], wqkv_v[...])
        da_all[at] = da.astype(bf16)
        xhat, _ = row_stats(x_all[at].astype(f32))
        vec_out[0:1] += jnp.sum(da * xhat, axis=0, keepdims=True)
        vec_out[1:2] += jnp.sum(da, axis=0, keepdims=True)
        return 0

    lax.fori_loop(0, rows // TILE, gather_back, 0)
    outs = [
        pltpu.make_async_copy(src, dst, out_sem.at[i])
        for i, (src, dst) in enumerate(
            ((o_all, o_out), (da_all, da_out), (wqg, wqg_out), (wdg, wdg_out))
        )
    ]
    outs[0].start()
    outs[1].start()

    def qkv_tile(k, _):
        cols = span(k * TILE, TILE, TILE)
        wqg[cols, :] = dot_tn(h_all[:, cols], dqkv[...]).astype(bf16)
        return 0

    lax.fori_loop(0, width // TILE, qkv_tile, 0)
    outs[2].start()
    wdg[...] = dot_tn(o_all[...], dy_all[...]).astype(bf16)
    outs[3].start()
    for c in outs:
        c.wait()


def run_attention(n_tensor, group_of, offsets, picked, xp, dp, wqkv, wd, vecs):
    prompt_len, width = xp.shape
    rows = prompt_len + MEMBERS * CONT_LEN
    local = wd.shape[0]
    heads = local // HD
    piece = CONT_LEN // n_tensor
    lines = n_tensor // 2
    table = jnp.asarray(rotary_table(prompt_len + CONT_LEN))
    table_rows = table.shape[1] + MEMBERS * CONT_LEN
    shape = jax.ShapeDtypeStruct
    hbm = pl.BlockSpec(memory_space=pl.ANY)
    vmem = pl.BlockSpec(memory_space=pltpu.VMEM)
    smem = pl.BlockSpec(memory_space=pltpu.SMEM)
    return pl.pallas_call(
        functools.partial(attention_kernel, n_tensor),
        out_shape=(
            shape((rows, local), bf16),
            shape((rows, width), bf16),
            shape((width, 3 * local), bf16),
            shape((local, width), bf16),
            shape((8, width), f32),
        ),
        in_specs=[smem, smem, hbm, hbm, hbm, hbm, hbm, hbm, vmem],
        out_specs=(hbm, hbm, hbm, hbm, vmem),
        scratch_shapes=[
            pltpu.VMEM((rows, width), bf16),
            pltpu.VMEM((rows, width), bf16),
            pltpu.VMEM((n_tensor, 2, MEMBERS, piece, width), bf16),
            pltpu.VMEM((rows, width), bf16),
            pltpu.VMEM((3, table_rows, CHUNK), f32),
            pltpu.VMEM((width, 3 * local), bf16),
            pltpu.VMEM((local, width), bf16),
        ]
        + [pltpu.VMEM((heads, rows, HD), bf16)] * 5
        + [pltpu.VMEM((heads, rows, HD), f32)] * 3
        + [
            pltpu.VMEM((rows, local), bf16),
            pltpu.VMEM((rows, 3 * local), bf16),
            pltpu.VMEM((rows, width), bf16),
            pltpu.VMEM((width, 3 * local), bf16),
            pltpu.VMEM((local, width), bf16),
            pltpu.SemaphoreType.DMA((5,)),
            pltpu.SemaphoreType.DMA,
            pltpu.SemaphoreType.DMA((lines - 1,)),
            pltpu.SemaphoreType.DMA((lines - 1,)),
            pltpu.SemaphoreType.DMA((lines,)),
            pltpu.SemaphoreType.DMA((lines,)),
            pltpu.SemaphoreType.DMA((4,)),
        ],
        compiler_params=pltpu.CompilerParams(
            collective_id=1, has_side_effects=True, vmem_limit_bytes=58 * 2**20
        ),
        cost_estimate=pl.CostEstimate(flops=20 * 10**9, bytes_accessed=20 * 10**6, transcendentals=4 * 10**6),
        name="attention",
    )(group_of, offsets, picked, xp, dp, table, wqkv, wd, vecs)


def tail_kernel(
    n_dp, n_tensor, group_ref, xp, xc, dp, dc, picked, o, g, da1, da2, wd, w2, vecs, vec1, vec2,
    out_p, out_c, grad_p, grad_c, vec_out,
    part, rc, sy, ry, o_v, g_v, wd_v, w2_v, xq, dyq, xm, xh, dyh, keep_y, keep_d, ag, ring, fin,
    small, small_core, small_y, small_ring,
    load_sem, part_sem, rc_send, rc_recv, ry_send, ry_recv, ag_send, ag_recv, agc_send, agc_recv,
    ring_send, ring_recv, sc_send, sc_recv, sy_send, sy_recv, fin_send, fin_recv, finc_send, finc_recv,
    out_sem, outc_sem,
):
    prompt_len, width = xp.shape
    cont_total = xc.shape[0]
    conts = MEMBERS
    piece = CONT_LEN // n_tensor
    lines = n_tensor // 2
    quarter = prompt_len // n_tensor
    few = conts * piece
    me_dp, me_t = lax.axis_index("dp"), lax.axis_index("tensor")
    core = lax.rem(me_t, jnp.int32(2))
    line = lax.div(me_t, jnp.int32(2))
    sibling = me_t + 1 - 2 * core
    peers = [lax.rem(me_t + 2 * k, jnp.int32(n_tensor)) for k in range(1, lines)]
    spot, after, before = ring_neighbours(n_dp)
    base_one, base_two, base_y = 4 * few, 4 * few + quarter, 4 * few + 2 * quarter
    group_rows = (slice(0, base_one), slice(base_one, base_y), slice(base_y, base_y + quarter))

    loads = [
        (o, o_v), (wd, wd_v), (g, g_v), (w2, w2_v),
        (xp.at[span(me_t * quarter, quarter, 16)], xq),
        (dp.at[span(me_t * quarter, quarter, 16)], dyq),
        (picked.at[0], xm),
    ]
    for s in range(conts):
        loads.append((xc.at[span(s * CONT_LEN + me_t * piece, piece, 16)], xh.at[s]))
        loads.append((dc.at[span(s * CONT_LEN + me_t * piece, piece, 16)], dyh.at[s]))
    loads = [pltpu.make_async_copy(src, dst, load_sem.at[i]) for i, (src, dst) in enumerate(loads)]
    fills = []
    for q in range(n_tensor):
        pairs = [
            (da1.at[pl.ds(q * quarter, quarter)], part.at[q, pl.ds(base_one, quarter)]),
            (da2.at[pl.ds(q * quarter, quarter)], part.at[q, pl.ds(base_two, quarter)]),
        ]
        for s in range(conts):
            from_rows = pl.ds(prompt_len + s * CONT_LEN + q * piece, piece)
            pairs.append((da1.at[from_rows], part.at[q, pl.ds(2 * few + s * piece, piece)]))
            pairs.append((da2.at[from_rows], part.at[q, pl.ds(3 * few + s * piece, piece)]))
        fills += [pltpu.make_async_copy(src, dst, part_sem.at[q, i]) for i, (src, dst) in enumerate(pairs)]
    for c in loads[:4]:
        c.start()
    for c in fills:
        c.start()
    for c in loads[4:]:
        c.start()
    meet([{"tensor": sibling}] + [{"tensor": p} for p in peers] + [{"dp": after}, {"dp": before}])

    small[0:2] = vec2[0:2]
    small[2:4] = vec1[0:2]
    small[4:6] = vec1[2:4]
    small[6:7] = vec2[2:3]
    small[7:8] = jnp.zeros((1, width), f32)
    small_to_core = remote(small, small_core, sc_send, sc_recv, {"tensor": sibling})
    small_to_core.start()

    for c in loads[:4]:
        c.wait()
    o_cont = dot(o_v[prompt_len:], wd_v[...]).astype(bf16)
    g_cont = dot(g_v[prompt_len:], w2_v[...]).astype(bf16)
    for q in range(n_tensor):
        for s in range(conts):
            from_rows = slice(s * CONT_LEN + q * piece, s * CONT_LEN + (q + 1) * piece)
            part[q, s * piece : (s + 1) * piece] = o_cont[from_rows]
            part[q, few + s * piece : few + (s + 1) * piece] = g_cont[from_rows]
    for c in fills:
        c.wait()

    def to_core(n):
        return [
            remote(
                part.at[2 * j + 1 - core, group_rows[n]], rc.at[j, group_rows[n]],
                rc_send.at[n, j], rc_recv.at[n, j], {"tensor": sibling},
            )
            for j in range(lines)
        ]

    def to_line(n):
        return [
            remote(
                sy.at[k, group_rows[n]], ry.at[k, group_rows[n]], ry_send.at[n, k], ry_recv.at[n, k], {"tensor": p}
            )
            for k, p in enumerate(peers)
        ]

    for c in to_core(0) + to_core(1):
        c.start()

    def outputs(q, _):
        at = span(q * quarter, quarter, quarter)
        total = dot(o_v[at], wd_v[...]) + dot(g_v[at], w2_v[...])
        part[q, group_rows[2]] = total.astype(bf16)
        return 0

    lax.fori_loop(0, n_tensor, outputs, 0)
    for c in to_core(2):
        c.start()

    small_to_core.wait()
    row = lax.broadcasted_iota(jnp.int32, (8, 1), 0)
    small_y[line] = small[...] + jnp.where(row < 4, small_core[...], 0.0)
    small_to_line = [
        remote(small_y.at[line], small_y.at[line], sy_send.at[k], sy_recv.at[k], {"tensor": p})
        for k, p in enumerate(peers)
    ]
    for c in small_to_line:
        c.start()
    for n in range(3):
        for c in to_core(n):
            c.wait()
        for k in range(1, lines):
            j = lax.rem(line + k, jnp.int32(lines))
            sy[k - 1, group_rows[n]] = (
                part[2 * j + core, group_rows[n]].astype(f32) + rc[j, group_rows[n]].astype(f32)
            ).astype(bf16)
        for c in to_line(n):
            c.start()

    for c in loads[4:]:
        c.wait()

    def summed(start, size):
        at = pl.ds(start, size)
        total = part[me_t, at].astype(f32) + rc[line, at].astype(f32)
        for k in range(lines - 1):
            total = total + ry[k, at].astype(f32)
        return total

    gain_one, gain_two = vecs[0:1], vecs[2:3]
    bias = vecs[4:5]
    for c in to_line(0):
        c.wait()
    for s in range(conts):
        ring[spot, 0, s] = summed(s * piece, piece).astype(bf16)
        pulled = norm_pull(xm[s].astype(f32), summed(2 * few + s * piece, piece) * gain_one)
        ring[spot, 1, s] = pulled.astype(bf16)
        home = xh[s].astype(f32)
        keep_y[s] = home + summed(few + s * piece, piece) + bias
        keep_d[s] = dyh[s].astype(f32) + norm_pull(home, summed(3 * few + s * piece, piece) * gain_two)
    for c in small_to_line:
        c.wait()
    reduced = small_y[0]
    for j in range(1, lines):
        reduced = reduced + small_y[j]
    small_ring[spot] = jnp.where(row < 4, reduced, small[...])

    def steps(k):
        ahead = lax.rem(spot - k + n_dp, jnp.int32(n_dp))
        back = lax.rem(spot + k, jnp.int32(n_dp))
        return (
            remote(ring.at[ahead, 0], ring.at[ahead, 0], ring_send.at[0, k], ring_recv.at[0, k], {"dp": after}),
            remote(ring.at[back, 1], ring.at[back, 1], ring_send.at[1, k], ring_recv.at[1, k], {"dp": before}),
            remote(
                small_ring.at[ahead], small_ring.at[ahead], ring_send.at[2, k], ring_recv.at[2, k], {"dp": after}
            ),
        )

    def tick(k, _):
        for c in steps(k):
            c.start()
        for c in steps(k):
            c.wait()
        return 0

    lax.fori_loop(0, n_dp - 1, tick, 0)
    total = small_ring[0]
    for j in range(1, n_dp):
        total = total + small_ring[j]
    vec_out[...] = total

    def gather_line(a):
        return [
            remote(ag.at[me_t, a], ag.at[me_t, a], ag_send.at[a, k], ag_recv.at[a, k], {"tensor": p})
            for k, p in enumerate(peers)
        ]

    def gather_core(a):
        return [
            remote(
                ag.at[2 * j + core, a], ag.at[2 * j + core, a], agc_send.at[a, j], agc_recv.at[a, j],
                {"tensor": sibling},
            )
            for j in range(lines)
        ]

    for c in to_line(1):
        c.wait()
    e = summed(base_one, quarter) * gain_one + summed(base_two, quarter) * gain_two
    ag[me_t, 1] = (dyq[...].astype(f32) + norm_pull(xq[...].astype(f32), e)).astype(bf16)
    for c in gather_line(1):
        c.start()
    for c in to_line(2):
        c.wait()
    ag[me_t, 0] = (xq[...].astype(f32) + summed(base_y, quarter) + bias).astype(bf16)
    for c in gather_line(0):
        c.start()

    for s in range(conts):
        mine = me_dp * conts + s
        group = group_ref[mine]
        first, _ = find_members(group_ref, group)
        slot = jnp.where(first == mine, jnp.int32(0), jnp.int32(1))
        where = ring_spot(group, n_dp)
        fin[me_t, 0, s] = (keep_y[s] + ring[where, 0, slot].astype(f32)).astype(bf16)
        fin[me_t, 1, s] = (keep_d[s] + ring[where, 1, slot].astype(f32)).astype(bf16)
    fin_line = [
        remote(fin.at[me_t], fin.at[me_t], fin_send.at[k], fin_recv.at[k], {"tensor": p})
        for k, p in enumerate(peers)
    ]
    fin_core = [
        remote(
            fin.at[2 * j + core], fin.at[2 * j + core], finc_send.at[j], finc_recv.at[j], {"tensor": sibling}
        )
        for j in range(lines)
    ]
    for c in fin_line:
        c.start()
    for a in (1, 0):
        for c in gather_line(a):
            c.wait()
        for c in gather_core(a):
            c.start()
    for c in fin_line:
        c.wait()
    for c in fin_core:
        c.start()
    outs = []
    for a, dst in ((1, grad_p), (0, out_p)):
        for c in gather_core(a):
            c.wait()
        for q in range(n_tensor):
            outs.append(
                pltpu.make_async_copy(ag.at[q, a], dst.at[pl.ds(q * quarter, quarter)], out_sem.at[a, q])
            )
            outs[-1].start()
    for c in fin_core:
        c.wait()
    for a, dst in ((1, grad_c), (0, out_c)):
        for q in range(n_tensor):
            for s in range(conts):
                outs.append(
                    pltpu.make_async_copy(
                        fin.at[q, a, s], dst.at[pl.ds(s * CONT_LEN + q * piece, piece)], outc_sem.at[a, q, s]
                    )
                )
                outs[-1].start()
    for c in outs:
        c.wait()


def run_tail(n_dp, n_tensor, group_of, xp, xc, dp, dc, picked, o, g, da1, da2, wd, w2, vecs, vec1, vec2):
    prompt_len, width = xp.shape
    cont_total = xc.shape[0]
    conts = MEMBERS
    piece = CONT_LEN // n_tensor
    lines = n_tensor // 2
    quarter = prompt_len // n_tensor
    stack = 4 * conts * piece + 3 * quarter
    shape = jax.ShapeDtypeStruct
    hbm = pl.BlockSpec(memory_space=pl.ANY)
    vmem = pl.BlockSpec(memory_space=pltpu.VMEM)
    smem = pl.BlockSpec(memory_space=pltpu.SMEM)
    sem = pltpu.SemaphoreType.DMA
    return pl.pallas_call(
        functools.partial(tail_kernel, n_dp, n_tensor),
        out_shape=(
            shape(xp.shape, bf16),
            shape(xc.shape, bf16),
            shape(xp.shape, bf16),
            shape(xc.shape, bf16),
            shape((8, width), f32),
        ),
        in_specs=[smem] + [hbm] * 11 + [vmem] * 3,
        out_specs=(hbm, hbm, hbm, hbm, vmem),
        scratch_shapes=[
            pltpu.VMEM((n_tensor, stack, width), bf16),
            pltpu.VMEM((lines, stack, width), bf16),
            pltpu.VMEM((lines - 1, stack, width), bf16),
            pltpu.VMEM((lines - 1, stack, width), bf16),
            pltpu.VMEM(o.shape, bf16),
            pltpu.VMEM(g.shape, bf16),
            pltpu.VMEM(wd.shape, bf16),
            pltpu.VMEM(w2.shape, bf16),
            pltpu.VMEM((quarter, width), bf16),
            pltpu.VMEM((quarter, width), bf16),
            pltpu.VMEM((conts, piece, width), bf16),
            pltpu.VMEM((conts, piece, width), bf16),
            pltpu.VMEM((conts, piece, width), bf16),
            pltpu.VMEM((conts, piece, width), f32),
            pltpu.VMEM((conts, piece, width), f32),
            pltpu.VMEM((n_tensor, 2, quarter, width), bf16),
            pltpu.VMEM((n_dp, 2, conts, piece, width), bf16),
            pltpu.VMEM((n_tensor, 2, conts, piece, width), bf16),
            pltpu.VMEM((8, width), f32),
            pltpu.VMEM((8, width), f32),
            pltpu.VMEM((lines, 8, width), f32),
            pltpu.VMEM((n_dp, 8, width), f32),
            sem((7 + 2 * conts,)),
            sem((n_tensor, 2 + 2 * conts)),
            sem((3, lines)),
            sem((3, lines)),
            sem((3, lines - 1)),
            sem((3, lines - 1)),
            sem((2, lines - 1)),
            sem((2, lines - 1)),
            sem((2, lines)),
            sem((2, lines)),
            sem((3, n_dp - 1)),
            sem((3, n_dp - 1)),
            sem,
            sem,
            sem((lines - 1,)),
            sem((lines - 1,)),
            sem((lines - 1,)),
            sem((lines - 1,)),
            sem((lines,)),
            sem((lines,)),
            sem((2, n_tensor)),
            sem((2, n_tensor, conts)),
        ],
        compiler_params=pltpu.CompilerParams(
            collective_id=2, has_side_effects=True, vmem_limit_bytes=58 * 2**20
        ),
        cost_estimate=pl.CostEstimate(flops=20 * 10**9, bytes_accessed=30 * 10**6, transcendentals=0),
        name="tail",
    )(group_of, xp, xc, dp, dc, picked, o, g, da1, da2, wd, w2, vecs, vec1, vec2)


def per_device(
    n_dp, n_tensor,
    prompt_in, cont_in, prompt_cot, cont_cot, group_of, offsets, ln1_gain, ln1_bias, ln2_gain, ln2_bias,
    qkv_weight, qkv_bias, dense_weight, dense_bias, fc1_weight, fc1_bias, fc2_weight, fc2_bias,
):
    width = prompt_in.shape[1]
    hidden = fc1_weight.shape[1]
    local3 = qkv_weight.shape[1]

    def row(v):
        return jnp.pad(v.astype(f32), (0, width - v.shape[0]))

    vecs = jnp.stack(
        [
            row(ln1_gain), row(ln1_bias), row(ln2_gain), row(ln2_bias),
            row(dense_bias.astype(f32) + fc2_bias.astype(f32)), row(fc1_bias), row(qkv_bias),
            jnp.zeros((width,), f32),
        ]
    )
    g, da2, w1g, w2g, vec1, picked = run_mlp(
        n_dp, n_tensor, group_of, prompt_in, cont_in, prompt_cot, cont_cot, fc1_weight, fc2_weight, vecs
    )
    w1g, w2g = lax.psum((w1g, w2g), "dp")
    o, da1, wqg, wdg, vec2 = run_attention(
        n_tensor, group_of, offsets, picked, prompt_in, prompt_cot, qkv_weight, dense_weight, vecs
    )
    wqg, wdg = lax.psum((wqg, wdg), "dp")
    out_p, out_c, grad_p, grad_c, total = run_tail(
        n_dp, n_tensor, group_of, prompt_in, cont_in, prompt_cot, cont_cot, picked, o, g, da1, da2,
        dense_weight, fc2_weight, vecs, vec1, vec2,
    )
    return (
        out_p, out_c, grad_p, grad_c,
        total[0], total[1], total[2], total[3],
        wqg.astype(f32), total[6, :local3],
        wdg.astype(f32), total[4],
        w1g.astype(f32), total[5, :hidden],
        w2g.astype(f32), total[4],
    )


def solution(mesh):
    rows, whole, columns, segment, depth = P("dp", None), P(), P(None, "tensor"), P("tensor"), P("tensor", None)
    return jax.shard_map(
        functools.partial(per_device, mesh.shape["dp"], mesh.shape["tensor"]),
        mesh=mesh,
        in_specs=(
            rows, rows, rows, rows, whole, whole, whole, whole, whole, whole,
            columns, segment, depth, whole, columns, segment, depth, whole,
        ),
        out_specs=(
            rows, rows, rows, rows, whole, whole, whole, whole,
            columns, segment, depth, whole, columns, segment, depth, whole,
        ),
        check_vma=False,
    )
```

```python
import functools
import math

import jax
import jax.numpy as jnp
import numpy as np
from jax import lax
from jax.experimental import pallas as pl
from jax.experimental.pallas import tpu as pltpu
from jax.sharding import PartitionSpec as P

HD = 64
ROT = 16
CONT_LEN = 128
TILE = 256
CHUNK = 128
MEMBERS = 2

eps_norm = 1e-05
masked_value = -1e30
MESH = pl.DeviceIdType.MESH
bf16 = jnp.bfloat16
f32 = jnp.float32


def dot(a, b):
    return jnp.dot(a, b, preferred_element_type=f32)


def dot_nt(a, b):
    return lax.dot_general(a, b, (((1,), (1,)), ((), ())), preferred_element_type=f32)


def dot_tn(a, b):
    return lax.dot_general(a, b, (((0,), (0,)), ((), ())), preferred_element_type=f32)


def row_stats(x):
    centered = x - jnp.mean(x, axis=-1, keepdims=True)
    scale = lax.rsqrt(jnp.mean(centered * centered, axis=-1, keepdims=True) + eps_norm)
    return centered * scale, scale


def norm_pull(x, e):
    xhat, scale = row_stats(x)
    return scale * (
        e
        - jnp.mean(e, axis=-1, keepdims=True)
        - xhat * jnp.mean(e * xhat, axis=-1, keepdims=True)
    )


def gelu_and_slope(u):
    t = 1.0 / (1.0 + jnp.abs(u) * (0.3275911 / math.sqrt(2.0)))
    bell = jnp.exp(-0.5 * u * u)
    poly = t * (
        0.127414796
        + t * (-0.142248368 + t * (0.7107068705 + t * (-0.7265760135 + t * 0.5307027145)))
    )
    tail = poly * bell
    cdf = jnp.where(u >= 0, 1.0 - tail, tail)
    return u * cdf, cdf + u * bell * (1.0 / math.sqrt(2.0 * math.pi))


def rotary_table(length):
    half = ROT // 2
    frequencies = np.exp(
        -np.arange(half, dtype=np.float32) * np.float32(2.0 * math.log(10000.0) / ROT)
    ).astype(np.float32)
    angles = np.arange(length, dtype=np.float32)[:, None] * frequencies[None, :]
    angles = np.concatenate([angles, angles], axis=1).astype(np.float32)
    cos = np.ones((length, HD), np.float32)
    low = np.zeros((length, HD), np.float32)
    high = np.zeros((length, HD), np.float32)
    cos[:, :ROT] = np.cos(angles)
    low[:, :half] = -np.sin(angles)[:, :half]
    high[:, half:ROT] = np.sin(angles)[:, half:]
    return np.stack([np.concatenate([t, t], axis=1) for t in (cos, low, high)])


def ring_spot(device, n):
    odd = lax.rem(device, jnp.int32(2))
    half = lax.div(device, jnp.int32(2))
    return (1 - odd) * half + odd * (n - 1 - half)


def ring_device(spot, n):
    far = lax.div(spot, jnp.int32(n // 2))
    return (1 - far) * (2 * spot) + far * (2 * (n - 1 - spot) + 1)


def ring_neighbours(n):
    spot = ring_spot(lax.axis_index("dp"), n)
    after = ring_device(lax.rem(spot + 1, jnp.int32(n)), n)
    before = ring_device(lax.rem(spot + n - 1, jnp.int32(n)), n)
    return spot, after, before


def find_members(group_ref, wanted):
    count = group_ref.shape[0]
    first = jnp.int32(count)
    last = jnp.int32(-1)
    for j in range(count):
        hit = group_ref[j] == wanted
        first = jnp.minimum(first, jnp.where(hit, jnp.int32(j), jnp.int32(count)))
        last = jnp.maximum(last, jnp.where(hit, jnp.int32(j), jnp.int32(-1)))
    return jnp.minimum(first, count - 1), jnp.maximum(last, 0)


def meet(devices):
    barrier = pltpu.get_barrier_semaphore()
    for device in devices:
        pl.semaphore_signal(barrier, inc=1, device_id=device, device_id_type=MESH)
    pl.semaphore_wait(barrier, len(devices))


def remote(src, dst, send, recv, device):
    return pltpu.make_async_remote_copy(
        src_ref=src, dst_ref=dst, send_sem=send, recv_sem=recv, device_id=device, device_id_type=MESH
    )


def span(start, size, step):
    return pl.ds(pl.multiple_of(start, step), size)


def piece_rows(rows, n):
    return rows // (2 * n), max(16, rows // (2 * n))


def ring_shape(rows, width, n):
    return (n, 2, piece_rows(rows, n)[1], width)


def put_tile(buffer, k, value, rows, n, cols=slice(None)):
    size = piece_rows(rows, n)[0]
    pieces = TILE // size
    for p in range(pieces):
        buffer[k * (pieces // 2) + p // 2, p % 2, :size, cols] = value[p * size : (p + 1) * size].astype(bf16)


class RingSum:
    def __init__(self, buffer, arrived, send, recv, n):
        self.buffer, self.arrived, self.send, self.recv, self.n = buffer, arrived, send, recv, n
        self.spot, self.after, self.before = ring_neighbours(n)

    def copies(self, k):
        n = self.n
        ahead = lax.rem(self.spot + (2 * n - 1) - k, jnp.int32(n))
        back = lax.rem(self.spot + 1 + k, jnp.int32(n))
        return [
            remote(
                self.buffer.at[chunk, way], self.arrived.at[k, way], self.send.at[way, k], self.recv.at[way, k],
                {"dp": device},
            )
            for way, (chunk, device) in enumerate(((ahead, self.after), (back, self.before)))
        ]

    def start(self, k):
        for c in self.copies(k):
            c.start()

    def finish(self, k):
        n = self.n
        for c in self.copies(k):
            c.wait()
        for way, chunk in enumerate(
            (lax.rem(self.spot + (2 * n - 2) - k, jnp.int32(n)), lax.rem(self.spot + 2 + k, jnp.int32(n)))
        ):
            self.buffer[chunk, way] = (
                self.buffer[chunk, way].astype(f32) + self.arrived[k, way].astype(f32)
            ).astype(bf16)


class RingGather:
    def __init__(self, buffer, send, recv, n):
        self.buffer, self.send, self.recv, self.n = buffer, send, recv, n
        self.spot, self.after, self.before = ring_neighbours(n)

    def copies(self, k):
        n = self.n
        ahead = lax.rem(self.spot + n - k, jnp.int32(n))
        back = lax.rem(self.spot + k, jnp.int32(n))
        return [
            remote(
                self.buffer.at[chunk, way], self.buffer.at[chunk, way], self.send.at[way, k], self.recv.at[way, k],
                {"dp": device},
            )
            for way, (chunk, device) in enumerate(((ahead, self.after), (back, self.before)))
        ]

    def start(self, k):
        for c in self.copies(k):
            c.start()

    def finish(self, k):
        for c in self.copies(k):
            c.wait()


def advance(summing, gathering, t, stop):
    n = summing.n

    @pl.when(t < n - 1)
    def _():
        summing.finish(t)

    @pl.when(t < n - 2)
    def _():
        summing.start(t + 1)

    @pl.when((t == n - 2) & (stop > n - 1))
    def _():
        gathering.start(jnp.int32(0))

    @pl.when((t >= n - 1) & (t < stop))
    def _():
        gathering.finish(t - (n - 1))

    @pl.when((t >= n - 1) & (t < stop - 1))
    def _():
        gathering.start(t - (n - 2))


def mlp_kernel(
    n_dp, n_tensor, group_ref, xp, xc, dp, dc, w1, w2, vecs,
    g_out, da_out, w1g_out, w2g_out, vec_out, picked_out,
    x_all, dy_all, w1_v, w2_v, g_all, h_all, du_all, da_all, w1g, w2g, ring,
    own_sem, load_sem, out_sem, send, recv,
):
    prompt_len, width = xp.shape
    cont_total = xc.shape[0]
    conts = cont_total // CONT_LEN
    rows = prompt_len + cont_total
    hidden = w1.shape[1]
    piece = CONT_LEN // n_tensor
    me_dp, me_t = lax.axis_index("dp"), lax.axis_index("tensor")
    spot, after, before = ring_neighbours(n_dp)

    own = [
        pltpu.make_async_copy(
            src.at[span(s * CONT_LEN + me_t * piece, piece, 16)], ring.at[spot, a, s], own_sem.at[a, s]
        )
        for a, src in enumerate((xc, dc))
        for s in range(conts)
    ]
    for c in own:
        c.start()
    loads = [
        pltpu.make_async_copy(src, dst, load_sem.at[i])
        for i, (src, dst) in enumerate(
            (
                (xp, x_all.at[pl.ds(0, prompt_len)]),
                (xc, x_all.at[pl.ds(prompt_len, cont_total)]),
                (w1, w1_v),
                (dp, dy_all.at[pl.ds(0, prompt_len)]),
                (dc, dy_all.at[pl.ds(prompt_len, cont_total)]),
                (w2, w2_v),
            )
        )
    ]
    for c in loads:
        c.start()
    meet([{"dp": after}, {"dp": before}])

    moving = RingGather(ring, send, recv, n_dp)
    for c in own:
        c.wait()
    moving.start(jnp.int32(0))

    turns = rows // TILE + hidden // TILE
    per_turn = -(-(n_dp - 1) // turns)

    def tick(turn):
        def one(j, _):
            k = turn * per_turn + j

            @pl.when(k < n_dp - 1)
            def _():
                moving.finish(k)

            @pl.when(k < n_dp - 2)
            def _():
                moving.start(k + 1)

            return 0

        lax.fori_loop(0, per_turn, one, 0)

    for c in loads:
        c.wait()
    vec_out[...] = jnp.zeros_like(vec_out)
    gain, shift, bias = vecs[2:3], vecs[3:4], vecs[5:6, :hidden]

    def row_tile(i, _):
        at = span(i * TILE, TILE, TILE)
        xhat, _ = row_stats(x_all[at].astype(f32))
        h = (xhat * gain + shift).astype(bf16)
        h_all[at] = h
        dy = dy_all[at]
        for k in range(hidden // TILE):
            cols = slice(k * TILE, (k + 1) * TILE)
            u = dot(h, w1_v[:, cols]) + bias[:, cols]
            dg = dot_nt(dy, w2_v[cols, :])
            value, slope = gelu_and_slope(u)
            g_all[at, cols] = value.astype(bf16)
            du = (dg * slope).astype(bf16)
            du_all[at, cols] = du
            vec_out[3:4, cols] += jnp.sum(du.astype(f32), axis=0, keepdims=True)
        da = dot_nt(du_all[at], w1_v[...])
        da_all[at] = da.astype(bf16)
        xhat, _ = row_stats(x_all[at].astype(f32))
        vec_out[0:1] += jnp.sum(da * xhat, axis=0, keepdims=True)
        vec_out[1:2] += jnp.sum(da, axis=0, keepdims=True)
        vec_out[2:3] += jnp.sum(dy.astype(f32), axis=0, keepdims=True)
        tick(i)
        return 0

    lax.fori_loop(0, rows // TILE, row_tile, 0)
    outs = [
        pltpu.make_async_copy(src, dst, out_sem.at[i])
        for i, (src, dst) in enumerate(
            ((g_all, g_out), (da_all, da_out), (w2g, w2g_out), (w1g, w1g_out))
        )
    ]
    outs[0].start()
    outs[1].start()

    def down_tile(k, _):
        cols = span(k * TILE, TILE, TILE)
        put_tile(w2g, k, dot_tn(g_all[:, cols], dy_all[...]), hidden, n_dp)
        tick(rows // TILE + k)
        return 0

    lax.fori_loop(0, hidden // TILE, down_tile, 0)
    outs[2].start()

    def up_tile(k, _):
        cols = span(k * TILE, TILE, TILE)
        put_tile(w1g, k, dot_tn(h_all[:, cols], du_all[...]), width, n_dp)
        return 0

    lax.fori_loop(0, width // TILE, up_tile, 0)
    outs[3].start()

    for m, member in enumerate(find_members(group_ref, me_dp)):
        where = ring_spot(lax.div(member, jnp.int32(conts)), n_dp)
        slot = lax.rem(member, jnp.int32(conts))
        for a in range(2):
            picked_out[a, m] = ring[where, a, slot]
    for c in outs:
        c.wait()


def run_mlp(n_dp, n_tensor, group_of, xp, xc, dp, dc, w1, w2, vecs):
    prompt_len, width = xp.shape
    rows = prompt_len + xc.shape[0]
    conts = xc.shape[0] // CONT_LEN
    hidden = w1.shape[1]
    piece = CONT_LEN // n_tensor
    shape = jax.ShapeDtypeStruct
    hbm = pl.BlockSpec(memory_space=pl.ANY)
    vmem = pl.BlockSpec(memory_space=pltpu.VMEM)
    smem = pl.BlockSpec(memory_space=pltpu.SMEM)
    return pl.pallas_call(
        functools.partial(mlp_kernel, n_dp, n_tensor),
        out_shape=(
            shape((rows, hidden), bf16),
            shape((rows, width), bf16),
            shape(ring_shape(width, hidden, n_dp), bf16),
            shape(ring_shape(hidden, width, n_dp), bf16),
            shape((8, width), f32),
            shape((2, MEMBERS, piece, width), bf16),
        ),
        in_specs=[smem, hbm, hbm, hbm, hbm, hbm, hbm, vmem],
        out_specs=(hbm, hbm, hbm, hbm, vmem, vmem),
        scratch_shapes=[
            pltpu.VMEM((rows, width), bf16),
            pltpu.VMEM((rows, width), bf16),
            pltpu.VMEM((width, hidden), bf16),
            pltpu.VMEM((hidden, width), bf16),
            pltpu.VMEM((rows, hidden), bf16),
            pltpu.VMEM((rows, width), bf16),
            pltpu.VMEM((rows, hidden), bf16),
            pltpu.VMEM((rows, width), bf16),
            pltpu.VMEM(ring_shape(width, hidden, n_dp), bf16),
            pltpu.VMEM(ring_shape(hidden, width, n_dp), bf16),
            pltpu.VMEM((n_dp, 2, conts, piece, width), bf16),
            pltpu.SemaphoreType.DMA((2, conts)),
            pltpu.SemaphoreType.DMA((6,)),
            pltpu.SemaphoreType.DMA((4,)),
            pltpu.SemaphoreType.DMA((2, n_dp - 1)),
            pltpu.SemaphoreType.DMA((2, n_dp - 1)),
        ],
        compiler_params=pltpu.CompilerParams(
            collective_id=0, has_side_effects=True, vmem_limit_bytes=58 * 2**20
        ),
        cost_estimate=pl.CostEstimate(flops=14 * 10**9, bytes_accessed=20 * 10**6, transcendentals=10**6),
        name="mlp",
    )(group_of, xp, xc, dp, dc, w1, w2, vecs)


def attention_kernel(
    n_dp, n_tensor, early, group_ref, offsets, picked, xp, dp, table, wqkv, wd, w1g, w2g, vecs,
    o_out, da_out, wg_out, w1s_out, w2s_out, vec_out,
    x_all, dy_all, moved, h_all, tab, wqkv_v, wd_v, qs, ks, vs, dos, oh, dqs, dks, dvs, o_all, dqkv, da_all, wg, sum1, sum2, got1, got2,
    load_sem, own_sem, y_send, y_recv, core_send, core_recv, out_sem, rs_send, rs_recv, ag_send, ag_recv,
):
    prompt_len, width = xp.shape
    conts = MEMBERS
    cont_total = conts * CONT_LEN
    rows = prompt_len + cont_total
    prompt_tiles = prompt_len // TILE
    local = wd.shape[0]
    heads = local // HD
    piece = CONT_LEN // n_tensor
    lines = n_tensor // 2
    table_len = table.shape[1]
    scale = 1.0 / math.sqrt(HD)
    me_dp, me_t = lax.axis_index("dp"), lax.axis_index("tensor")
    core = lax.rem(me_t, jnp.int32(2))
    sibling = me_t + 1 - 2 * core
    peers = [lax.rem(me_t + 2 * k, jnp.int32(n_tensor)) for k in range(1, lines)]

    mine = pltpu.make_async_copy(picked, moved.at[me_t], own_sem)
    mine.start()
    loads = [
        pltpu.make_async_copy(src, dst, load_sem.at[i])
        for i, (src, dst) in enumerate(
            (
                (xp, x_all.at[pl.ds(0, prompt_len)]),
                (wqkv, wqkv_v),
                (table, tab.at[:, pl.ds(0, table_len)]),
                (dp, dy_all.at[pl.ds(0, prompt_len)]),
                (wd, wd_v),
                (w1g, sum1),
                (w2g, sum2),
            )
        )
    ]
    for c in loads[-2:] + loads[:-2]:
        c.start()
    _, after, before = ring_neighbours(n_dp)
    meet([{"tensor": sibling}] + [{"tensor": p} for p in peers] + [{"dp": after}, {"dp": before}])
    sums = [
        (
            RingSum(buffer, got, rs_send.at[i], rs_recv.at[i], n_dp),
            RingGather(buffer, ag_send.at[i], ag_recv.at[i], n_dp),
        )
        for i, (buffer, got) in enumerate(((sum1, got1), (sum2, got2)))
    ]
    stop = n_dp - 1 + early
    points = 2 * (rows // TILE) + 3 * heads
    per_turn = -(-2 * stop // points)

    def turn(point):
        def one(j, _):
            t = point * per_turn + j
            for i, (summing, gathering) in enumerate(sums):
                @pl.when(lax.rem(t, jnp.int32(2)) == i)
                def _():
                    advance(summing, gathering, lax.div(t, jnp.int32(2)), stop)
            return 0

        lax.fori_loop(0, per_turn, one, 0)

    mine.wait()
    over_y = [
        remote(moved.at[me_t], moved.at[me_t], y_send.at[k], y_recv.at[k], {"tensor": p})
        for k, p in enumerate(peers)
    ]
    over_core = [
        remote(
            moved.at[2 * j + core], moved.at[2 * j + core], core_send.at[j], core_recv.at[j], {"tensor": sibling}
        )
        for j in range(lines)
    ]
    for c in over_y:
        c.start()
    for c, (summing, _) in zip(loads[-2:], sums):
        c.wait()
        summing.start(jnp.int32(0))
    members = find_members(group_ref, me_dp)
    offs = [offsets[m] for m in members]
    for c in loads[:-2]:
        c.wait()
    for m, off in enumerate(offs):
        for a in range(3):
            tab[a, table_len + m * CONT_LEN : table_len + (m + 1) * CONT_LEN, :] = tab[a, pl.ds(off, CONT_LEN), :]
    vec_out[...] = jnp.zeros_like(vec_out)
    gain, shift, bias = vecs[0:1], vecs[1:2], vecs[6:7, : 3 * local]
    lane = lax.broadcasted_iota(jnp.int32, (1, CHUNK), 1)

    def tables(start, c, sign):
        cos, low, high = (tab[a, pl.ds(start, TILE), :] for a in range(3))
        kinds = [(2 * c) % 3, (2 * c + 1) % 3]
        if 2 in kinds:
            turned = lane >= HD if kinds[0] == 2 else lane < HD
            cos = jnp.where(turned, cos, 1.0)
            low = jnp.where(turned, low, 0.0)
            high = jnp.where(turned, high, 0.0)
        return cos, low * sign, high * sign

    def turned(z, tabs):
        cos, low, high = tabs
        half = ROT // 2
        return z * cos + pltpu.roll(z, CHUNK - half, 1) * low + pltpu.roll(z, half, 1) * high

    def table_start(i):
        return pl.multiple_of(i * TILE + lax.div(i, jnp.int32(prompt_tiles)) * (table_len - prompt_len), CHUNK)

    def project(i, _):
        @pl.when(i == 1)
        def _():
            for c in over_y:
                c.wait()
            for c in over_core:
                c.start()

        @pl.when(i == prompt_tiles)
        def _():
            for c in over_core:
                c.wait()
            for q in range(n_tensor):
                for s in range(conts):
                    to = slice(prompt_len + s * CONT_LEN + q * piece, prompt_len + s * CONT_LEN + (q + 1) * piece)
                    x_all[to, :] = moved[q, 0, s]
                    dy_all[to, :] = moved[q, 1, s]

        at = span(i * TILE, TILE, TILE)
        xhat, _ = row_stats(x_all[at].astype(f32))
        h = (xhat * gain + shift).astype(bf16)
        h_all[at] = h
        for c in range(3 * local // CHUNK):
            cols = slice(c * CHUNK, (c + 1) * CHUNK)
            z = dot(h, wqkv_v[:, cols]) + bias[:, cols]
            z = turned(z, tables(table_start(i), c, 1.0)).astype(bf16)
            for part in range(2):
                head, kind = divmod(2 * c + part, 3)
                (qs, ks, vs)[kind][head, at] = z[:, part * HD : (part + 1) * HD]
        do = dot_nt(dy_all[at], wd_v[...]).astype(bf16)
        for head in range(heads):
            dos[head, at] = do[:, head * HD : (head + 1) * HD]
        turn(i)
        return 0

    lax.fori_loop(0, rows // TILE, project, 0)

    query_lane = lax.broadcasted_iota(jnp.int32, (1, TILE), 1)
    reach = jnp.zeros((1, TILE), jnp.int32)
    for m, off in enumerate(offs):
        reach = jnp.where(lax.div(query_lane, jnp.int32(CONT_LEN)) == m, off, reach)

    def attend(head, _):
        for block in range(rows // TILE - 1, -1, -1):
            first = block * TILE
            seen = first + TILE
            at = slice(first, seen)
            q, do = qs[head, at], dos[head, at]
            k, v = ks[head, :seen], vs[head, :seen]
            s = dot_nt(k, q) * scale
            key = lax.broadcasted_iota(jnp.int32, (TILE, TILE), 0)
            query = lax.broadcasted_iota(jnp.int32, (TILE, TILE), 1)
            if block == prompt_tiles:
                key_row = lax.broadcasted_iota(jnp.int32, (prompt_len, TILE), 0)
                far = jnp.where(key_row < reach, s[:first], masked_value)
                same = lax.div(key, jnp.int32(CONT_LEN)) == lax.div(query, jnp.int32(CONT_LEN))
                near = jnp.where((key <= query) & same, s[first:], masked_value)
                s = jnp.concatenate([far, near], axis=0)
            else:
                near = jnp.where(key <= query, s[first:], masked_value)
                s = near if first == 0 else jnp.concatenate([s[:first], near], axis=0)
            p = jnp.exp(s - jnp.max(s, axis=0, keepdims=True))
            p = p * (1.0 / jnp.sum(p, axis=0, keepdims=True))
            low = p.astype(bf16)
            oh[head, at] = dot_tn(v, low).T.astype(bf16)
            dprob = dot_nt(v, do)
            delta = jnp.sum(p * dprob, axis=0, keepdims=True)
            ds = (p * (dprob - delta)).astype(bf16)
            dqs[head, at] = dot_tn(k, ds).T * scale
            dk = dot(ds, q) * scale
            dv = dot(low, do)
            if block == rows // TILE - 1:
                dks[head, :seen] = dk
                dvs[head, :seen] = dv
            else:
                dks[head, :seen] += dk
                dvs[head, :seen] += dv
            if block in (prompt_tiles, prompt_tiles - 1, prompt_tiles - 3):
                turn(rows // TILE + head * 3 + (prompt_tiles - block + 1) // 2)
        return 0

    lax.fori_loop(0, heads, attend, 0)

    def gather_back(i, _):
        at = span(i * TILE, TILE, TILE)
        for c in range(local // CHUNK):
            o_all[at, c * CHUNK : (c + 1) * CHUNK] = jnp.concatenate([oh[2 * c, at], oh[2 * c + 1, at]], axis=1)
        for c in range(3 * local // CHUNK):
            parts = []
            for part in range(2):
                head, kind = divmod(2 * c + part, 3)
                parts.append((dqs, dks, dvs)[kind][head, at])
            z = jnp.concatenate(parts, axis=1)
            z = turned(z, tables(table_start(i), c, -1.0)).astype(bf16)
            cols = slice(c * CHUNK, (c + 1) * CHUNK)
            dqkv[at, cols] = z
            vec_out[2:3, cols] += jnp.sum(z.astype(f32), axis=0, keepdims=True)
        da = dot_nt(dqkv[at], wqkv_v[...])
        da_all[at] = da.astype(bf16)
        xhat, _ = row_stats(x_all[at].astype(f32))
        vec_out[0:1] += jnp.sum(da * xhat, axis=0, keepdims=True)
        vec_out[1:2] += jnp.sum(da, axis=0, keepdims=True)
        turn(rows // TILE + 3 * heads + i)
        return 0

    lax.fori_loop(0, rows // TILE, gather_back, 0)
    outs = [
        pltpu.make_async_copy(src, dst, out_sem.at[i])
        for i, (src, dst) in enumerate(
            ((o_all, o_out), (da_all, da_out), (sum1, w1s_out), (sum2, w2s_out), (wg, wg_out))
        )
    ]
    for c in outs[:4]:
        c.start()

    def weight_tile(k, _):
        cols = span(k * TILE, TILE, TILE)
        put_tile(wg, k, dot_tn(h_all[:, cols], dqkv[...]), width, n_dp, slice(0, 3 * local))
        put_tile(wg, k, dot_tn(dy_all[:, cols], o_all[...]), width, n_dp, slice(3 * local, 4 * local))
        return 0

    lax.fori_loop(0, width // TILE, weight_tile, 0)
    outs[4].start()
    for c in outs:
        c.wait()


def run_attention(n_dp, n_tensor, early, group_of, offsets, picked, xp, dp, wqkv, wd, w1g, w2g, vecs):
    prompt_len, width = xp.shape
    rows = prompt_len + MEMBERS * CONT_LEN
    local = wd.shape[0]
    heads = local // HD
    piece = CONT_LEN // n_tensor
    lines = n_tensor // 2
    table = jnp.asarray(rotary_table(prompt_len + CONT_LEN))
    table_rows = table.shape[1] + MEMBERS * CONT_LEN
    shape = jax.ShapeDtypeStruct
    hbm = pl.BlockSpec(memory_space=pl.ANY)
    vmem = pl.BlockSpec(memory_space=pltpu.VMEM)
    smem = pl.BlockSpec(memory_space=pltpu.SMEM)
    return pl.pallas_call(
        functools.partial(attention_kernel, n_dp, n_tensor, early),
        out_shape=(
            shape((rows, local), bf16),
            shape((rows, width), bf16),
            shape(ring_shape(width, 4 * local, n_dp), bf16),
            shape(w1g.shape, bf16),
            shape(w2g.shape, bf16),
            shape((8, width), f32),
        ),
        in_specs=[smem, smem, hbm, hbm, hbm, hbm, hbm, hbm, hbm, hbm, vmem],
        out_specs=(hbm, hbm, hbm, hbm, hbm, vmem),
        scratch_shapes=[
            pltpu.VMEM((rows, width), bf16),
            pltpu.VMEM((rows, width), bf16),
            pltpu.VMEM((n_tensor, 2, MEMBERS, piece, width), bf16),
            pltpu.VMEM((rows, width), bf16),
            pltpu.VMEM((3, table_rows, CHUNK), f32),
            pltpu.VMEM((width, 3 * local), bf16),
            pltpu.VMEM((local, width), bf16),
        ]
        + [pltpu.VMEM((heads, rows, HD), bf16)] * 5
        + [pltpu.VMEM((heads, rows, HD), f32)] * 3
        + [
            pltpu.VMEM((rows, local), bf16),
            pltpu.VMEM((rows, 3 * local), bf16),
            pltpu.VMEM((rows, width), bf16),
            pltpu.VMEM(ring_shape(width, 4 * local, n_dp), bf16),
            pltpu.VMEM(w1g.shape, bf16),
            pltpu.VMEM(w2g.shape, bf16),
            pltpu.VMEM((n_dp - 1,) + w1g.shape[1:], bf16),
            pltpu.VMEM((n_dp - 1,) + w2g.shape[1:], bf16),
            pltpu.SemaphoreType.DMA((7,)),
            pltpu.SemaphoreType.DMA,
            pltpu.SemaphoreType.DMA((lines - 1,)),
            pltpu.SemaphoreType.DMA((lines - 1,)),
            pltpu.SemaphoreType.DMA((lines,)),
            pltpu.SemaphoreType.DMA((lines,)),
            pltpu.SemaphoreType.DMA((5,)),
        ]
        + [pltpu.SemaphoreType.DMA((2, 2, n_dp - 1))] * 4,
        compiler_params=pltpu.CompilerParams(
            collective_id=1, has_side_effects=True, vmem_limit_bytes=58 * 2**20
        ),
        cost_estimate=pl.CostEstimate(flops=20 * 10**9, bytes_accessed=20 * 10**6, transcendentals=4 * 10**6),
        name="attention",
    )(group_of, offsets, picked, xp, dp, table, wqkv, wd, w1g, w2g, vecs)


def tail_kernel(
    n_dp, n_tensor, early, group_ref, xp, xc, dp, dc, picked, o, g, da1, da2, wd, w2, w1s, w2s, wg, vecs, vec1, vec2,
    out_p, out_c, grad_p, grad_c, w1_out, w2_out, wg_out, vec_out,
    part, rc, sy, ry, o_v, g_v, wd_v, w2_v, xq, dyq, xm, xh, dyh, keep_y, keep_d, ag, ring, fin,
    small, small_core, small_y, small_ring, sum1, sum2, sum3, got3,
    load_sem, part_sem, rc_send, rc_recv, ry_send, ry_recv, ag_send, ag_recv, agc_send, agc_recv,
    ring_send, ring_recv, sc_send, sc_recv, sy_send, sy_recv, fin_send, fin_recv, finc_send, finc_recv,
    out_sem, outc_sem, sum_load, sum_out, rs_send, rs_recv, wag_send, wag_recv,
):
    prompt_len, width = xp.shape
    cont_total = xc.shape[0]
    conts = MEMBERS
    piece = CONT_LEN // n_tensor
    lines = n_tensor // 2
    quarter = prompt_len // n_tensor
    few = conts * piece
    me_dp, me_t = lax.axis_index("dp"), lax.axis_index("tensor")
    core = lax.rem(me_t, jnp.int32(2))
    line = lax.div(me_t, jnp.int32(2))
    sibling = me_t + 1 - 2 * core
    peers = [lax.rem(me_t + 2 * k, jnp.int32(n_tensor)) for k in range(1, lines)]
    spot, after, before = ring_neighbours(n_dp)
    base_one, base_two, base_y = 4 * few, 4 * few + quarter, 4 * few + 2 * quarter
    group_rows = (slice(0, base_one), slice(base_one, base_y), slice(base_y, base_y + quarter))

    loads = [
        (o, o_v), (wd, wd_v), (g, g_v), (w2, w2_v),
        (xp.at[span(me_t * quarter, quarter, 16)], xq),
        (dp.at[span(me_t * quarter, quarter, 16)], dyq),
        (picked.at[0], xm),
    ]
    for s in range(conts):
        loads.append((xc.at[span(s * CONT_LEN + me_t * piece, piece, 16)], xh.at[s]))
        loads.append((dc.at[span(s * CONT_LEN + me_t * piece, piece, 16)], dyh.at[s]))
    loads = [pltpu.make_async_copy(src, dst, load_sem.at[i]) for i, (src, dst) in enumerate(loads)]
    fills = []
    for q in range(n_tensor):
        pairs = [
            (da1.at[pl.ds(q * quarter, quarter)], part.at[q, pl.ds(base_one, quarter)]),
            (da2.at[pl.ds(q * quarter, quarter)], part.at[q, pl.ds(base_two, quarter)]),
        ]
        for s in range(conts):
            from_rows = pl.ds(prompt_len + s * CONT_LEN + q * piece, piece)
            pairs.append((da1.at[from_rows], part.at[q, pl.ds(2 * few + s * piece, piece)]))
            pairs.append((da2.at[from_rows], part.at[q, pl.ds(3 * few + s * piece, piece)]))
        fills += [pltpu.make_async_copy(src, dst, part_sem.at[q, i]) for i, (src, dst) in enumerate(pairs)]
    sum_loads = [
        pltpu.make_async_copy(src, dst, sum_load.at[i])
        for i, (src, dst) in enumerate(((wg, sum3), (w1s, sum1), (w2s, sum2)))
    ]
    sum_outs = [
        pltpu.make_async_copy(src, dst, sum_out.at[i])
        for i, (src, dst) in enumerate(((sum3, wg_out), (sum1, w1_out), (sum2, w2_out)))
    ]
    for c in sum_loads + loads[:4]:
        c.start()
    for c in fills:
        c.start()
    for c in loads[4:]:
        c.start()
    for c in sum_loads:
        c.wait()
    meet([{"tensor": sibling}] + [{"tensor": p} for p in peers] + [{"dp": after}, {"dp": before}])

    summing = RingSum(sum3, got3, rs_send, rs_recv, n_dp)
    gathering = RingGather(sum3, wag_send.at[0], wag_recv.at[0], n_dp)
    rest = [RingGather(s, wag_send.at[i], wag_recv.at[i], n_dp) for i, s in ((1, sum1), (2, sum2))]
    left = n_dp - 1 - early
    summing.start(jnp.int32(0))
    if left > 0:
        rest[0].start(jnp.int32(early))

    def first_ticks(t, _):
        advance(summing, gathering, t, 2 * (n_dp - 1))
        for i, part_gather in enumerate(rest):
            @pl.when((t >= i * left) & (t < (i + 1) * left))
            def _():
                part_gather.finish(t - i * left + early)

            @pl.when((t >= i * left) & (t < (i + 1) * left - 1))
            def _():
                part_gather.start(t - i * left + early + 1)

        @pl.when(t == left - 1)
        def _():
            rest[1].start(jnp.int32(early))

        return 0

    small[0:2] = vec2[0:2]
    small[2:4] = vec1[0:2]
    small[4:6] = vec1[2:4]
    small[6:7] = vec2[2:3]
    small[7:8] = jnp.zeros((1, width), f32)
    small_to_core = remote(small, small_core, sc_send, sc_recv, {"tensor": sibling})
    small_to_core.start()

    for c in loads[:4]:
        c.wait()
    o_cont = dot(o_v[prompt_len:], wd_v[...]).astype(bf16)
    g_cont = dot(g_v[prompt_len:], w2_v[...]).astype(bf16)
    for q in range(n_tensor):
        for s in range(conts):
            from_rows = slice(s * CONT_LEN + q * piece, s * CONT_LEN + (q + 1) * piece)
            part[q, s * piece : (s + 1) * piece] = o_cont[from_rows]
            part[q, few + s * piece : few + (s + 1) * piece] = g_cont[from_rows]
    for c in fills:
        c.wait()

    def to_core(n):
        return [
            remote(
                part.at[2 * j + 1 - core, group_rows[n]], rc.at[j, group_rows[n]],
                rc_send.at[n, j], rc_recv.at[n, j], {"tensor": sibling},
            )
            for j in range(lines)
        ]

    def to_line(n):
        return [
            remote(
                sy.at[k, group_rows[n]], ry.at[k, group_rows[n]], ry_send.at[n, k], ry_recv.at[n, k], {"tensor": p}
            )
            for k, p in enumerate(peers)
        ]

    for c in to_core(0) + to_core(1):
        c.start()

    def outputs(q, _):
        at = span(q * quarter, quarter, quarter)
        total = dot(o_v[at], wd_v[...]) + dot(g_v[at], w2_v[...])
        part[q, group_rows[2]] = total.astype(bf16)
        return 0

    lax.fori_loop(0, n_tensor, outputs, 0)
    for c in to_core(2):
        c.start()

    small_to_core.wait()
    row = lax.broadcasted_iota(jnp.int32, (8, 1), 0)
    small_y[line] = small[...] + jnp.where(row < 4, small_core[...], 0.0)
    small_to_line = [
        remote(small_y.at[line], small_y.at[line], sy_send.at[k], sy_recv.at[k], {"tensor": p})
        for k, p in enumerate(peers)
    ]
    for c in small_to_line:
        c.start()
    for n in range(3):
        for c in to_core(n):
            c.wait()
        for k in range(1, lines):
            j = lax.rem(line + k, jnp.int32(lines))
            sy[k - 1, group_rows[n]] = (
                part[2 * j + core, group_rows[n]].astype(f32) + rc[j, group_rows[n]].astype(f32)
            ).astype(bf16)
        for c in to_line(n):
            c.start()

    lax.fori_loop(0, 2 * left, first_ticks, 0)
    sum_outs[1].start()
    sum_outs[2].start()
    for c in loads[4:]:
        c.wait()

    def summed(start, size):
        at = pl.ds(start, size)
        total = part[me_t, at].astype(f32) + rc[line, at].astype(f32)
        for k in range(lines - 1):
            total = total + ry[k, at].astype(f32)
        return total

    gain_one, gain_two = vecs[0:1], vecs[2:3]
    bias = vecs[4:5]
    for c in to_line(0):
        c.wait()
    for s in range(conts):
        ring[spot, 0, s] = summed(s * piece, piece).astype(bf16)
        pulled = norm_pull(xm[s].astype(f32), summed(2 * few + s * piece, piece) * gain_one)
        ring[spot, 1, s] = pulled.astype(bf16)
        home = xh[s].astype(f32)
        keep_y[s] = home + summed(few + s * piece, piece) + bias
        keep_d[s] = dyh[s].astype(f32) + norm_pull(home, summed(3 * few + s * piece, piece) * gain_two)
    for c in small_to_line:
        c.wait()
    reduced = small_y[0]
    for j in range(1, lines):
        reduced = reduced + small_y[j]
    small_ring[spot] = jnp.where(row < 4, reduced, small[...])

    def steps(k):
        ahead = lax.rem(spot - k + n_dp, jnp.int32(n_dp))
        back = lax.rem(spot + k, jnp.int32(n_dp))
        return (
            remote(ring.at[ahead, 0], ring.at[ahead, 0], ring_send.at[0, k], ring_recv.at[0, k], {"dp": after}),
            remote(ring.at[back, 1], ring.at[back, 1], ring_send.at[1, k], ring_recv.at[1, k], {"dp": before}),
            remote(
                small_ring.at[ahead], small_ring.at[ahead], ring_send.at[2, k], ring_recv.at[2, k], {"dp": after}
            ),
        )

    for c in steps(jnp.int32(0)):
        c.start()

    def ticks(t, _):
        @pl.when(t < 2 * (n_dp - 1))
        def _():
            advance(summing, gathering, t, 2 * (n_dp - 1))

        k = t - 2 * left

        @pl.when(k < n_dp - 1)
        def _():
            for c in steps(k):
                c.wait()

        @pl.when(k < n_dp - 2)
        def _():
            for c in steps(k + 1):
                c.start()

        return 0

    last_tick = max(2 * (n_dp - 1), 2 * left + n_dp - 1)
    lax.fori_loop(2 * left, 2 * left + 4, ticks, 0)

    def gather_line(a):
        return [
            remote(ag.at[me_t, a], ag.at[me_t, a], ag_send.at[a, k], ag_recv.at[a, k], {"tensor": p})
            for k, p in enumerate(peers)
        ]

    def gather_core(a):
        return [
            remote(
                ag.at[2 * j + core, a], ag.at[2 * j + core, a], agc_send.at[a, j], agc_recv.at[a, j],
                {"tensor": sibling},
            )
            for j in range(lines)
        ]

    for c in to_line(1):
        c.wait()
    e = summed(base_one, quarter) * gain_one + summed(base_two, quarter) * gain_two
    ag[me_t, 1] = (dyq[...].astype(f32) + norm_pull(xq[...].astype(f32), e)).astype(bf16)
    for c in gather_line(1):
        c.start()
    lax.fori_loop(2 * left + 4, 2 * left + 6, ticks, 0)
    for c in to_line(2):
        c.wait()
    ag[me_t, 0] = (xq[...].astype(f32) + summed(base_y, quarter) + bias).astype(bf16)
    for c in gather_line(0):
        c.start()

    lax.fori_loop(2 * left + 6, last_tick, ticks, 0)
    sum_outs[0].start()
    total = small_ring[0]
    for j in range(1, n_dp):
        total = total + small_ring[j]
    vec_out[...] = total

    for s in range(conts):
        mine = me_dp * conts + s
        group = group_ref[mine]
        first, _ = find_members(group_ref, group)
        slot = jnp.where(first == mine, jnp.int32(0), jnp.int32(1))
        where = ring_spot(group, n_dp)
        fin[me_t, 0, s] = (keep_y[s] + ring[where, 0, slot].astype(f32)).astype(bf16)
        fin[me_t, 1, s] = (keep_d[s] + ring[where, 1, slot].astype(f32)).astype(bf16)
    fin_line = [
        remote(fin.at[me_t], fin.at[me_t], fin_send.at[k], fin_recv.at[k], {"tensor": p})
        for k, p in enumerate(peers)
    ]
    fin_core = [
        remote(
            fin.at[2 * j + core], fin.at[2 * j + core], finc_send.at[j], finc_recv.at[j], {"tensor": sibling}
        )
        for j in range(lines)
    ]
    for c in fin_line:
        c.start()
    for a in (1, 0):
        for c in gather_line(a):
            c.wait()
        for c in gather_core(a):
            c.start()
    for c in fin_line:
        c.wait()
    for c in fin_core:
        c.start()
    outs = []
    for a, dst in ((1, grad_p), (0, out_p)):
        for c in gather_core(a):
            c.wait()
        for q in range(n_tensor):
            outs.append(
                pltpu.make_async_copy(ag.at[q, a], dst.at[pl.ds(q * quarter, quarter)], out_sem.at[a, q])
            )
            outs[-1].start()
    for c in fin_core:
        c.wait()
    for a, dst in ((1, grad_c), (0, out_c)):
        for q in range(n_tensor):
            for s in range(conts):
                outs.append(
                    pltpu.make_async_copy(
                        fin.at[q, a, s], dst.at[pl.ds(s * CONT_LEN + q * piece, piece)], outc_sem.at[a, q, s]
                    )
                )
                outs[-1].start()
    for c in outs + sum_outs:
        c.wait()


def run_tail(
    n_dp, n_tensor, early, group_of, xp, xc, dp, dc, picked, o, g, da1, da2, wd, w2, w1s, w2s, wg, vecs, vec1, vec2
):
    prompt_len, width = xp.shape
    cont_total = xc.shape[0]
    conts = MEMBERS
    piece = CONT_LEN // n_tensor
    lines = n_tensor // 2
    quarter = prompt_len // n_tensor
    stack = 4 * conts * piece + 3 * quarter
    shape = jax.ShapeDtypeStruct
    hbm = pl.BlockSpec(memory_space=pl.ANY)
    vmem = pl.BlockSpec(memory_space=pltpu.VMEM)
    smem = pl.BlockSpec(memory_space=pltpu.SMEM)
    sem = pltpu.SemaphoreType.DMA
    return pl.pallas_call(
        functools.partial(tail_kernel, n_dp, n_tensor, early),
        out_shape=(
            shape(xp.shape, bf16),
            shape(xc.shape, bf16),
            shape(xp.shape, bf16),
            shape(xc.shape, bf16),
            shape(w1s.shape, bf16),
            shape(w2s.shape, bf16),
            shape(wg.shape, bf16),
            shape((8, width), f32),
        ),
        in_specs=[smem] + [hbm] * 14 + [vmem] * 3,
        out_specs=(hbm,) * 7 + (vmem,),
        scratch_shapes=[
            pltpu.VMEM((n_tensor, stack, width), bf16),
            pltpu.VMEM((lines, stack, width), bf16),
            pltpu.VMEM((lines - 1, stack, width), bf16),
            pltpu.VMEM((lines - 1, stack, width), bf16),
            pltpu.VMEM(o.shape, bf16),
            pltpu.VMEM(g.shape, bf16),
            pltpu.VMEM(wd.shape, bf16),
            pltpu.VMEM(w2.shape, bf16),
            pltpu.VMEM((quarter, width), bf16),
            pltpu.VMEM((quarter, width), bf16),
            pltpu.VMEM((conts, piece, width), bf16),
            pltpu.VMEM((conts, piece, width), bf16),
            pltpu.VMEM((conts, piece, width), bf16),
            pltpu.VMEM((conts, piece, width), f32),
            pltpu.VMEM((conts, piece, width), f32),
            pltpu.VMEM((n_tensor, 2, quarter, width), bf16),
            pltpu.VMEM((n_dp, 2, conts, piece, width), bf16),
            pltpu.VMEM((n_tensor, 2, conts, piece, width), bf16),
            pltpu.VMEM((8, width), f32),
            pltpu.VMEM((8, width), f32),
            pltpu.VMEM((lines, 8, width), f32),
            pltpu.VMEM((n_dp, 8, width), f32),
            pltpu.VMEM(w1s.shape, bf16),
            pltpu.VMEM(w2s.shape, bf16),
            pltpu.VMEM(wg.shape, bf16),
            pltpu.VMEM((n_dp - 1,) + wg.shape[1:], bf16),
            sem((7 + 2 * conts,)),
            sem((n_tensor, 2 + 2 * conts)),
            sem((3, lines)),
            sem((3, lines)),
            sem((3, lines - 1)),
            sem((3, lines - 1)),
            sem((2, lines - 1)),
            sem((2, lines - 1)),
            sem((2, lines)),
            sem((2, lines)),
            sem((3, n_dp - 1)),
            sem((3, n_dp - 1)),
            sem,
            sem,
            sem((lines - 1,)),
            sem((lines - 1,)),
            sem((lines - 1,)),
            sem((lines - 1,)),
            sem((lines,)),
            sem((lines,)),
            sem((2, n_tensor)),
            sem((2, n_tensor, conts)),
            sem((3,)),
            sem((3,)),
            sem((2, n_dp - 1)),
            sem((2, n_dp - 1)),
            sem((3, 2, n_dp - 1)),
            sem((3, 2, n_dp - 1)),
        ],
        compiler_params=pltpu.CompilerParams(
            collective_id=2, has_side_effects=True, vmem_limit_bytes=58 * 2**20
        ),
        cost_estimate=pl.CostEstimate(flops=20 * 10**9, bytes_accessed=30 * 10**6, transcendentals=0),
        name="tail",
    )(group_of, xp, xc, dp, dc, picked, o, g, da1, da2, wd, w2, w1s, w2s, wg, vecs, vec1, vec2)


def per_device(
    n_dp, n_tensor,
    prompt_in, cont_in, prompt_cot, cont_cot, group_of, offsets, ln1_gain, ln1_bias, ln2_gain, ln2_bias,
    qkv_weight, qkv_bias, dense_weight, dense_bias, fc1_weight, fc1_bias, fc2_weight, fc2_bias,
):
    width = prompt_in.shape[1]
    hidden = fc1_weight.shape[1]
    local3 = qkv_weight.shape[1]

    def row(v):
        return jnp.pad(v.astype(f32), (0, width - v.shape[0]))

    vecs = jnp.stack(
        [
            row(ln1_gain), row(ln1_bias), row(ln2_gain), row(ln2_bias),
            row(dense_bias.astype(f32) + fc2_bias.astype(f32)), row(fc1_bias), row(qkv_bias),
            jnp.zeros((width,), f32),
        ]
    )
    g, da2, w1g, w2g, vec1, picked = run_mlp(
        n_dp, n_tensor, group_of, prompt_in, cont_in, prompt_cot, cont_cot, fc1_weight, fc2_weight, vecs
    )
    early = min(n_dp - 1, 4)
    o, da1, wg, w1g, w2g, vec2 = run_attention(
        n_dp, n_tensor, early, group_of, offsets, picked, prompt_in, prompt_cot, qkv_weight, dense_weight, w1g, w2g,
        vecs,
    )
    out_p, out_c, grad_p, grad_c, w1g, w2g, wg, total = run_tail(
        n_dp, n_tensor, early, group_of, prompt_in, cont_in, prompt_cot, cont_cot, picked, o, g, da1, da2,
        dense_weight, fc2_weight, w1g, w2g, wg, vecs, vec1, vec2,
    )

    def unpacked(buffer, rows):
        return buffer[:, :, : piece_rows(rows, n_dp)[0]].reshape(rows, buffer.shape[-1]).astype(f32)

    wg = unpacked(wg, width)
    return (
        out_p, out_c, grad_p, grad_c,
        total[0], total[1], total[2], total[3],
        wg[:, :local3], total[6, :local3],
        wg[:, local3:].T, total[4],
        unpacked(w1g, width), total[5, :hidden],
        unpacked(w2g, hidden), total[4],
    )


def solution(mesh):
    rows, whole, columns, segment, depth = P("dp", None), P(), P(None, "tensor"), P("tensor"), P("tensor", None)
    return jax.shard_map(
        functools.partial(per_device, mesh.shape["dp"], mesh.shape["tensor"]),
        mesh=mesh,
        in_specs=(
            rows, rows, rows, rows, whole, whole, whole, whole, whole, whole,
            columns, segment, depth, whole, columns, segment, depth, whole,
        ),
        out_specs=(
            rows, rows, rows, rows, whole, whole, whole, whole,
            columns, segment, depth, whole, columns, segment, depth, whole,
        ),
        check_vma=False,
    )
```

```python
import functools
import math

import jax
import jax.numpy as jnp
import numpy as np
from jax import lax
from jax.experimental import pallas as pl
from jax.experimental.pallas import tpu as pltpu
from jax.sharding import PartitionSpec as P

HD = 64
ROT = 16
CONT_LEN = 128
TILE = 256
CHUNK = 128
MEMBERS = 2

eps_norm = 1e-05
masked_value = -1e30
MESH = pl.DeviceIdType.MESH
bf16 = jnp.bfloat16
f32 = jnp.float32


def dot(a, b):
    return jnp.dot(a, b, preferred_element_type=f32)


def dot_nt(a, b):
    return lax.dot_general(a, b, (((1,), (1,)), ((), ())), preferred_element_type=f32)


def dot_tn(a, b):
    return lax.dot_general(a, b, (((0,), (0,)), ((), ())), preferred_element_type=f32)


def row_stats(x):
    centered = x - jnp.mean(x, axis=-1, keepdims=True)
    scale = lax.rsqrt(jnp.mean(centered * centered, axis=-1, keepdims=True) + eps_norm)
    return centered * scale, scale


def norm_pull(x, e):
    xhat, scale = row_stats(x)
    return scale * (
        e
        - jnp.mean(e, axis=-1, keepdims=True)
        - xhat * jnp.mean(e * xhat, axis=-1, keepdims=True)
    )


def gelu_and_slope(u):
    t = 1.0 / (1.0 + jnp.abs(u) * (0.3275911 / math.sqrt(2.0)))
    bell = jnp.exp(-0.5 * u * u)
    poly = t * (
        0.127414796
        + t * (-0.142248368 + t * (0.7107068705 + t * (-0.7265760135 + t * 0.5307027145)))
    )
    tail = poly * bell
    cdf = jnp.where(u >= 0, 1.0 - tail, tail)
    return u * cdf, cdf + u * bell * (1.0 / math.sqrt(2.0 * math.pi))


def rotary_table(length):
    half = ROT // 2
    frequencies = np.exp(
        -np.arange(half, dtype=np.float32) * np.float32(2.0 * math.log(10000.0) / ROT)
    ).astype(np.float32)
    angles = np.arange(length, dtype=np.float32)[:, None] * frequencies[None, :]
    angles = np.concatenate([angles, angles], axis=1).astype(np.float32)
    cos = np.ones((length, HD), np.float32)
    low = np.zeros((length, HD), np.float32)
    high = np.zeros((length, HD), np.float32)
    cos[:, :ROT] = np.cos(angles)
    low[:, :half] = -np.sin(angles)[:, :half]
    high[:, half:ROT] = np.sin(angles)[:, half:]
    return np.stack([np.concatenate([t, t], axis=1) for t in (cos, low, high)])


def ring_spot(device, n):
    odd = lax.rem(device, jnp.int32(2))
    half = lax.div(device, jnp.int32(2))
    return (1 - odd) * half + odd * (n - 1 - half)


def ring_device(spot, n):
    far = lax.div(spot, jnp.int32(n // 2))
    return (1 - far) * (2 * spot) + far * (2 * (n - 1 - spot) + 1)


def ring_neighbours(n):
    spot = ring_spot(lax.axis_index("dp"), n)
    after = ring_device(lax.rem(spot + 1, jnp.int32(n)), n)
    before = ring_device(lax.rem(spot + n - 1, jnp.int32(n)), n)
    return spot, after, before


def find_members(group_ref, wanted):
    count = group_ref.shape[0]
    first = jnp.int32(count)
    last = jnp.int32(-1)
    for j in range(count):
        hit = group_ref[j] == wanted
        first = jnp.minimum(first, jnp.where(hit, jnp.int32(j), jnp.int32(count)))
        last = jnp.maximum(last, jnp.where(hit, jnp.int32(j), jnp.int32(-1)))
    return jnp.minimum(first, count - 1), jnp.maximum(last, 0)


def meet(devices):
    barrier = pltpu.get_barrier_semaphore()
    for device in devices:
        pl.semaphore_signal(barrier, inc=1, device_id=device, device_id_type=MESH)
    pl.semaphore_wait(barrier, len(devices))


def remote(src, dst, send, recv, device):
    return pltpu.make_async_remote_copy(
        src_ref=src, dst_ref=dst, send_sem=send, recv_sem=recv, device_id=device, device_id_type=MESH
    )


def as_row(ref):
    return ref[...].astype(f32).reshape(1, ref.shape[0])


def span(start, size, step):
    return pl.ds(pl.multiple_of(start, step), size)


def piece_rows(rows, n):
    return rows // (2 * n), max(16, rows // (2 * n))


def ring_shape(rows, width, n):
    return (n, 2, piece_rows(rows, n)[1], width)


def put_tile(buffer, k, value, rows, n, cols=slice(None)):
    size = piece_rows(rows, n)[0]
    pieces = TILE // size
    for p in range(pieces):
        buffer[k * (pieces // 2) + p // 2, p % 2, :size, cols] = value[p * size : (p + 1) * size].astype(bf16)


def pair_columns(c0, c1, c2, lane):
    low = lane < HD
    crossed = jnp.where(low, c2, c0)
    return jnp.where(low, c0, c1), pltpu.roll(crossed, HD, 1), jnp.where(low, c1, c2)


def unpair_columns(q, k, v, lane):
    low = lane < HD
    crossed = pltpu.roll(k, HD, 1)
    return jnp.where(low, q, crossed), jnp.where(low, v, q), jnp.where(low, crossed, v)


class RingSum:
    def __init__(self, buffer, arrived, send, recv, n):
        self.buffer, self.arrived, self.send, self.recv, self.n = buffer, arrived, send, recv, n
        self.spot, self.after, self.before = ring_neighbours(n)

    def copies(self, k):
        n = self.n
        ahead = lax.rem(self.spot + (2 * n - 1) - k, jnp.int32(n))
        back = lax.rem(self.spot + 1 + k, jnp.int32(n))
        return [
            remote(
                self.buffer.at[chunk, way], self.arrived.at[k, way], self.send.at[way, k], self.recv.at[way, k],
                {"dp": device},
            )
            for way, (chunk, device) in enumerate(((ahead, self.after), (back, self.before)))
        ]

    def start(self, k):
        for c in self.copies(k):
            c.start()

    def finish(self, k):
        n = self.n
        for c in self.copies(k):
            c.wait()
        for way, chunk in enumerate(
            (lax.rem(self.spot + (2 * n - 2) - k, jnp.int32(n)), lax.rem(self.spot + 2 + k, jnp.int32(n)))
        ):
            self.buffer[chunk, way] = (
                self.buffer[chunk, way].astype(f32) + self.arrived[k, way].astype(f32)
            ).astype(bf16)


class RingGather:
    def __init__(self, buffer, send, recv, n, part=()):
        self.buffer, self.send, self.recv, self.n, self.part = buffer, send, recv, n, part
        self.spot, self.after, self.before = ring_neighbours(n)

    def copies(self, k):
        n = self.n
        ahead = lax.rem(self.spot + n - k, jnp.int32(n))
        back = lax.rem(self.spot + k, jnp.int32(n))
        return [
            remote(
                self.buffer.at[(chunk, way) + self.part], self.buffer.at[(chunk, way) + self.part],
                self.send.at[way, k], self.recv.at[way, k], {"dp": device},
            )
            for way, (chunk, device) in enumerate(((ahead, self.after), (back, self.before)))
        ]

    def start(self, k):
        for c in self.copies(k):
            c.start()

    def finish(self, k):
        for c in self.copies(k):
            c.wait()


def advance(summing, gathering, t, stop):
    n = summing.n

    @pl.when(t < n - 1)
    def _():
        summing.finish(t)

    @pl.when(t < n - 2)
    def _():
        summing.start(t + 1)

    @pl.when((t == n - 2) & (stop > n - 1))
    def _():
        gathering.start(jnp.int32(0))

    @pl.when((t >= n - 1) & (t < stop))
    def _():
        gathering.finish(t - (n - 1))

    @pl.when((t >= n - 1) & (t < stop - 1))
    def _():
        gathering.start(t - (n - 2))


def front_kernel(
    n_dp, n_tensor, early, group_ref, offsets, xp, xc, dp, dc, w1, w2, wqkv, wd, table,
    gain_two_ref, shift_two_ref, bias1_ref, gain_one_ref, shift_one_ref, bias_qkv_ref,
    g_out, da2_out, o_out, da1_out, w1s_out, w2s_out, wg_out, picked_out, vec_out,
    x_all, dy_all, w1_v, w2_v, wqkv_v, wd_v, tab, h_all, g_all, mixed, da_all, ring, moved,
    sum1, sum2, got1, got2, wg, qs, dos, ks, vs, k_turned, v_turned, dks, dvs, o_all,
    own_sem, load_sem, out_sem, ring_send, ring_recv, y_send, y_recv, core_send, core_recv,
    rs_send, rs_recv, ag_send, ag_recv,
):
    prompt_len, width = xp.shape
    cont_total = xc.shape[0]
    conts = MEMBERS
    rows = prompt_len + cont_total
    tiles = rows // TILE
    prompt_tiles = prompt_len // TILE
    hidden = w1.shape[1]
    local = wd.shape[0]
    heads = local // HD
    piece = CONT_LEN // n_tensor
    lines = n_tensor // 2
    table_len = table.shape[1]
    scale = 1.0 / math.sqrt(HD)
    me_dp, me_t = lax.axis_index("dp"), lax.axis_index("tensor")
    core = lax.rem(me_t, jnp.int32(2))
    sibling = me_t + 1 - 2 * core
    peers = [lax.rem(me_t + 2 * k, jnp.int32(n_tensor)) for k in range(1, lines)]
    spot, after, before = ring_neighbours(n_dp)

    own = [
        pltpu.make_async_copy(
            src.at[span(s * CONT_LEN + me_t * piece, piece, 16)], ring.at[spot, a, s], own_sem.at[a, s]
        )
        for a, src in enumerate((xc, dc))
        for s in range(conts)
    ]
    loads = [
        pltpu.make_async_copy(src, dst, load_sem.at[i])
        for i, (src, dst) in enumerate(
            (
                (xc, x_all.at[pl.ds(0, cont_total)]),
                (w1, w1_v),
                (dc, dy_all.at[pl.ds(0, cont_total)]),
                (w2, w2_v),
                (xp, x_all.at[pl.ds(cont_total, prompt_len)]),
                (dp, dy_all.at[pl.ds(cont_total, prompt_len)]),
                (wqkv, wqkv_v),
                (wd, wd_v),
                (table, tab.at[:, pl.ds(0, table_len)]),
            )
        )
    ]
    for c in own + loads:
        c.start()
    meet([{"dp": after}, {"dp": before}, {"tensor": sibling}] + [{"tensor": p} for p in peers])

    moving = [RingGather(ring, ring_send.at[s], ring_recv.at[s], n_dp, (s,)) for s in range(conts)]
    for c in own:
        c.wait()
    for m in moving:
        m.start(jnp.int32(0))
    sums = [
        (
            RingSum(buffer, got, rs_send.at[i], rs_recv.at[i], n_dp),
            RingGather(buffer, ag_send.at[i], ag_recv.at[i], n_dp),
        )
        for i, (buffer, got) in enumerate(((sum2, got2), (sum1, got1)))
    ]

    move_points = 2 * tiles + hidden // TILE
    moves = -(-conts * (n_dp - 1) // move_points)

    def move(point):
        def one(j, _):
            t = point * moves + j
            k = lax.div(t, jnp.int32(conts))
            for s, m in enumerate(moving):
                mine = lax.rem(t, jnp.int32(conts)) == s

                @pl.when(mine & (k < n_dp - 1))
                def _():
                    m.finish(k)

                @pl.when(mine & (k < n_dp - 2))
                def _():
                    m.start(k + 1)

            return 0

        lax.fori_loop(0, moves, one, 0)

    stop = n_dp - 1 + early
    sum_points = 2 * prompt_tiles + 3 * heads + width // TILE
    turns = -(-2 * stop // sum_points)

    def turn(point):
        def one(j, _):
            t = point * turns + j
            for i, (summing, gathering) in enumerate(sums):
                @pl.when(lax.rem(t, jnp.int32(2)) == i)
                def _():
                    advance(summing, gathering, lax.div(t, jnp.int32(2)), stop)
            return 0

        lax.fori_loop(0, turns, one, 0)

    vec_out[...] = jnp.zeros_like(vec_out)

    gain, shift, bias = as_row(gain_two_ref), as_row(shift_two_ref), as_row(bias1_ref)
    for c in loads[:4]:
        c.wait()

    def mlp_tile(i, _):
        @pl.when(i == 1)
        def _():
            for c in loads[4:6]:
                c.wait()

        at = span(i * TILE, TILE, TILE)
        xhat, _ = row_stats(x_all[at].astype(f32))
        h = (xhat * gain + shift).astype(bf16)
        h_all[at] = h
        dy = dy_all[at]
        for k in range(hidden // TILE):
            cols = slice(k * TILE, (k + 1) * TILE)
            u = dot(h, w1_v[:, cols]) + bias[:, cols]
            dg = dot_nt(dy, w2_v[cols, :])
            value, slope = gelu_and_slope(u)
            g_all[at, cols] = value.astype(bf16)
            du = (dg * slope).astype(bf16)
            mixed[at, cols] = du
            vec_out[5:6, cols] += jnp.sum(du.astype(f32), axis=0, keepdims=True)
        move(2 * i)
        da = dot_nt(mixed[at, :hidden], w1_v[...])
        da_all[at] = da.astype(bf16)
        xhat, _ = row_stats(x_all[at].astype(f32))
        vec_out[2:3] += jnp.sum(da * xhat, axis=0, keepdims=True)
        vec_out[3:4] += jnp.sum(da, axis=0, keepdims=True)
        vec_out[4:5] += jnp.sum(dy.astype(f32), axis=0, keepdims=True)
        move(2 * i + 1)
        return 0

    lax.fori_loop(0, tiles, mlp_tile, 0)
    outs = [
        pltpu.make_async_copy(src, dst, out_sem.at[i])
        for i, (src, dst) in enumerate(
            (
                (g_all, g_out), (da_all, da2_out), (o_all, o_out), (da_all, da1_out),
                (sum1, w1s_out), (sum2, w2s_out), (wg, wg_out),
            )
        )
    ]
    outs[0].start()
    outs[1].start()

    def down_tile(k, _):
        cols = span(k * TILE, TILE, TILE)
        put_tile(sum2, k, dot_tn(g_all[:, cols], dy_all[:rows]), hidden, n_dp)
        move(2 * tiles + k)
        return 0

    lax.fori_loop(0, hidden // TILE, down_tile, 0)
    sums[0][0].start(jnp.int32(0))

    members = find_members(group_ref, me_dp)
    offs = [offsets[m] for m in members]
    for m, member in enumerate(members):
        where = ring_spot(lax.div(member, jnp.int32(conts)), n_dp)
        slot = lax.rem(member, jnp.int32(conts))
        for a in range(2):
            found = ring[where, a, slot]
            moved[me_t, a, m] = found
            if a == 0:
                picked_out[m] = found
    over_y = [
        remote(moved.at[me_t], moved.at[me_t], y_send.at[k], y_recv.at[k], {"tensor": p})
        for k, p in enumerate(peers)
    ]
    over_core = [
        remote(
            moved.at[2 * j + core], moved.at[2 * j + core], core_send.at[j], core_recv.at[j], {"tensor": sibling}
        )
        for j in range(lines)
    ]
    for c in over_y:
        c.start()

    def up_tile(k, _):
        cols = span(k * TILE, TILE, TILE)
        put_tile(sum1, k, dot_tn(h_all[:, cols], mixed[:, :hidden]), width, n_dp)
        return 0

    lax.fori_loop(0, width // TILE, up_tile, 0)
    sums[1][0].start(jnp.int32(0))

    for c in loads[6:]:
        c.wait()
    for m, off in enumerate(offs):
        for a in range(3):
            tab[a, table_len + m * CONT_LEN : table_len + (m + 1) * CONT_LEN, :] = tab[a, pl.ds(off, CONT_LEN), :]
    gain, shift = as_row(gain_one_ref), as_row(shift_one_ref)
    lane = lax.broadcasted_iota(jnp.int32, (1, CHUNK), 1)
    bias = as_row(bias_qkv_ref)
    biases = []
    for pair in range(heads // 2):
        chunks = [slice((3 * pair + c) * CHUNK, (3 * pair + c + 1) * CHUNK) for c in range(3)]
        biases += pair_columns(*(bias[:, cols] for cols in chunks), lane)
        for cols, value in zip(chunks, pair_columns(*(wqkv_v[:, cols] for cols in chunks), lane)):
            wqkv_v[:, cols] = value

    def turned(z, start, sign):
        cos, low, high = (tab[a, pl.ds(start, TILE), :] for a in range(3))
        half = ROT // 2
        return z * cos + (pltpu.roll(z, CHUNK - half, 1) * low + pltpu.roll(z, half, 1) * high) * sign

    def table_start(i):
        return pl.multiple_of(i * TILE + lax.div(i, jnp.int32(prompt_tiles)) * (table_len - prompt_len), CHUNK)

    def project(i):
        at = span(i * TILE, TILE, TILE)
        source = span(i * TILE + cont_total, TILE, TILE)
        xhat, _ = row_stats(x_all[source].astype(f32))
        h = (xhat * gain + shift).astype(bf16)
        h_all[at] = h
        do = dot_nt(dy_all[source], wd_v[...]).astype(bf16)
        for pair in range(heads // 2):
            q, k, v = (
                dot(h, wqkv_v[:, c * CHUNK : (c + 1) * CHUNK]) + biases[c] for c in range(3 * pair, 3 * pair + 3)
            )
            q = turned(q, table_start(i), 1.0)
            qs[2 * pair, at] = jnp.where(lane < HD, q, 0.0).astype(bf16)
            qs[2 * pair + 1, at] = jnp.where(lane < HD, 0.0, q).astype(bf16)
            k = turned(k, table_start(i), 1.0)
            ks[pair, at] = k.astype(bf16)
            k_turned[pair, :, at] = k.T.astype(bf16)
            vs[pair, at] = v.astype(bf16)
            v_turned[pair, :, at] = v.T.astype(bf16)
            both = do[:, pair * CHUNK : (pair + 1) * CHUNK].astype(f32)
            dos[2 * pair, at] = jnp.where(lane < HD, both, 0.0).astype(bf16)
            dos[2 * pair + 1, at] = jnp.where(lane < HD, 0.0, both).astype(bf16)

    def project_prompt(i, _):
        project(i)
        turn(i)
        return 0

    lax.fori_loop(0, prompt_tiles, project_prompt, 0)
    for c in over_y:
        c.wait()
    for c in over_core:
        c.start()

    query_lane = lax.broadcasted_iota(jnp.int32, (1, TILE), 1)
    reach = jnp.zeros((1, TILE), jnp.int32)
    for m, off in enumerate(offs):
        reach = jnp.where(lax.div(query_lane, jnp.int32(CONT_LEN)) == m, off, reach)

    def attend(pair, _):
        for block in list(range(prompt_tiles - 1, -1, -1)) + [prompt_tiles]:
            first = block * TILE
            seen = first + TILE
            at = slice(first, seen)
            if block == prompt_tiles:
                @pl.when(pair == 0)
                def _():
                    for c in over_core:
                        c.wait()
                    for q in range(n_tensor):
                        for s in range(conts):
                            to = rows + s * CONT_LEN + q * piece
                            x_all[to : to + piece, :] = moved[q, 0, s]
                            dy_all[to : to + piece, :] = moved[q, 1, s]
                    project(jnp.int32(prompt_tiles))

            k, v = ks[pair, :seen], vs[pair, :seen]
            key = lax.broadcasted_iota(jnp.int32, (TILE, TILE), 0)
            query = lax.broadcasted_iota(jnp.int32, (TILE, TILE), 1)
            seen_near = key <= query
            if block == prompt_tiles:
                key_row = lax.broadcasted_iota(jnp.int32, (prompt_len, TILE), 0)
                same = lax.div(key, jnp.int32(CONT_LEN)) == lax.div(query, jnp.int32(CONT_LEN))
                seen_near = seen_near & same
            heads_now = (2 * pair, 2 * pair + 1)
            scores = [dot_nt(k, qs[h, at]) * scale for h in heads_now]
            slopes = [dot_nt(v, dos[h, at]) for h in heads_now]
            lows, low_slopes, o_turned, dq_turned = [], [], [], []
            for sub in range(2):
                s, dprob = scores[sub], slopes[sub]
                near = jnp.where(seen_near, s[first:], masked_value)
                if block == prompt_tiles:
                    s = jnp.concatenate([jnp.where(key_row < reach, s[:first], masked_value), near], axis=0)
                else:
                    s = near if first == 0 else jnp.concatenate([s[:first], near], axis=0)
                p = jnp.exp(s - jnp.max(s, axis=0, keepdims=True))
                p = p * (1.0 / jnp.sum(p, axis=0, keepdims=True))
                low = p.astype(bf16)
                delta = jnp.sum(p * dprob, axis=0, keepdims=True)
                ds = (p * (dprob - delta)).astype(bf16)
                part = slice(sub * HD, (sub + 1) * HD)
                o_turned.append(dot(v_turned[pair, part, :seen], low))
                dq_turned.append(dot(k_turned[pair, part, :seen], ds))
                lows.append(low)
                low_slopes.append(ds)
            o_all[at, span(pair * CHUNK, CHUNK, CHUNK)] = jnp.concatenate(o_turned, axis=0).T.astype(bf16)
            dq = jnp.concatenate(dq_turned, axis=0).T * scale
            dq = turned(dq, table_start(jnp.int32(block)), -1.0).astype(bf16)
            cols = span(3 * pair * CHUNK, CHUNK, CHUNK)
            mixed[at, cols] = dq
            vec_out[6:7, cols] += jnp.sum(dq.astype(f32), axis=0, keepdims=True)
            q_both = jnp.concatenate([qs[h, at] for h in heads_now], axis=0)
            do_both = jnp.concatenate([dos[h, at] for h in heads_now], axis=0)
            dk = dot(jnp.concatenate(low_slopes, axis=1), q_both)
            dv = dot(jnp.concatenate(lows, axis=1), do_both)
            if block == prompt_tiles - 1:
                dks[:seen] = dk
                dvs[:seen] = dv
            else:
                old = min(seen, prompt_len)
                dks[:old] += dk[:old]
                dvs[:old] += dv[:old]
                if old < seen:
                    dks[old:seen] = dk[old:]
                    dvs[old:seen] = dv[old:]
            turn(prompt_tiles + 6 * pair + (prompt_tiles - 1 - block if block < prompt_tiles else block))

        for i in range(tiles):
            at = slice(i * TILE, (i + 1) * TILE)
            dk = turned(dks[at] * scale, table_start(jnp.int32(i)), -1.0).astype(bf16)
            for c, value in ((1, dk), (2, dvs[at].astype(bf16))):
                cols = span((3 * pair + c) * CHUNK, CHUNK, CHUNK)
                mixed[at, cols] = value
                vec_out[6:7, cols] += jnp.sum(value.astype(f32), axis=0, keepdims=True)
        turn(prompt_tiles + 6 * pair + 5)
        return 0

    lax.fori_loop(0, heads // 2, attend, 0)
    outs[2].start()
    outs[1].wait()

    def back(i, _):
        at = span(i * TILE, TILE, TILE)
        da = dot_nt(mixed[at, : 3 * local], wqkv_v[...])
        da_all[at] = da.astype(bf16)
        xhat, _ = row_stats(x_all[span(i * TILE + cont_total, TILE, TILE)].astype(f32))
        vec_out[0:1] += jnp.sum(da * xhat, axis=0, keepdims=True)
        vec_out[1:2] += jnp.sum(da, axis=0, keepdims=True)

        @pl.when(i > 0)
        def _():
            turn(prompt_tiles + 3 * heads + i - 1)

        return 0

    lax.fori_loop(0, tiles, back, 0)
    outs[3].start()

    def weight_tile(k, _):
        cols = span(k * TILE, TILE, TILE)
        put_tile(wg, k, dot_tn(h_all[:, cols], mixed[:, : 3 * local]), width, n_dp, slice(0, 3 * local))
        put_tile(wg, k, dot_tn(dy_all[cont_total:, cols], o_all[...]), width, n_dp, slice(3 * local, 4 * local))
        turn(2 * prompt_tiles + 3 * heads + k)
        return 0

    lax.fori_loop(0, width // TILE, weight_tile, 0)
    for c in outs[4:]:
        c.start()
    outs[0].wait()
    for c in outs[2:]:
        c.wait()


def run_front(n_dp, n_tensor, early, group_of, offsets, xp, xc, dp, dc, w1, w2, wqkv, wd, *vectors):
    prompt_len, width = xp.shape
    cont_total = xc.shape[0]
    rows = prompt_len + cont_total
    hidden = w1.shape[1]
    local = wd.shape[0]
    heads = local // HD
    piece = CONT_LEN // n_tensor
    lines = n_tensor // 2
    table = jnp.asarray(rotary_table(prompt_len + CONT_LEN))
    table_rows = table.shape[1] + MEMBERS * CONT_LEN
    up, down = ring_shape(width, hidden, n_dp), ring_shape(hidden, width, n_dp)
    third = ring_shape(width, 4 * local, n_dp)
    shape = jax.ShapeDtypeStruct
    hbm = pl.BlockSpec(memory_space=pl.ANY)
    vmem = pl.BlockSpec(memory_space=pltpu.VMEM)
    smem = pl.BlockSpec(memory_space=pltpu.SMEM)
    sem = pltpu.SemaphoreType.DMA
    return pl.pallas_call(
        functools.partial(front_kernel, n_dp, n_tensor, early),
        out_shape=(
            shape((rows, hidden), bf16),
            shape((rows, width), bf16),
            shape((rows, local), bf16),
            shape((rows, width), bf16),
            shape(up, bf16),
            shape(down, bf16),
            shape(third, bf16),
            shape((MEMBERS, piece, width), bf16),
            shape((8, width), f32),
        ),
        in_specs=[smem] * 2 + [hbm] * 9 + [vmem] * 6,
        out_specs=(hbm,) * 7 + (vmem,) * 2,
        scratch_shapes=[
            pltpu.VMEM((rows + cont_total, width), bf16),
            pltpu.VMEM((rows + cont_total, width), bf16),
            pltpu.VMEM((width, hidden), bf16),
            pltpu.VMEM((hidden, width), bf16),
            pltpu.VMEM((width, 3 * local), bf16),
            pltpu.VMEM((local, width), bf16),
            pltpu.VMEM((3, table_rows, CHUNK), f32),
            pltpu.VMEM((rows, width), bf16),
            pltpu.VMEM((rows, hidden), bf16),
            pltpu.VMEM((rows, max(hidden, 3 * local)), bf16),
            pltpu.VMEM((rows, width), bf16),
            pltpu.VMEM((n_dp, 2, MEMBERS, piece, width), bf16),
            pltpu.VMEM((n_tensor, 2, MEMBERS, piece, width), bf16),
            pltpu.VMEM(up, bf16),
            pltpu.VMEM(down, bf16),
            pltpu.VMEM((n_dp - 1,) + up[1:], bf16),
            pltpu.VMEM((n_dp - 1,) + down[1:], bf16),
            pltpu.VMEM(third, bf16),
        ]
        + [pltpu.VMEM((heads, rows, CHUNK), bf16)] * 2
        + [pltpu.VMEM((heads // 2, rows, CHUNK), bf16)] * 2
        + [pltpu.VMEM((heads // 2, CHUNK, rows), bf16)] * 2
        + [pltpu.VMEM((rows, CHUNK), f32)] * 2
        + [
            pltpu.VMEM((rows, local), bf16),
            sem((2, MEMBERS)),
            sem((9,)),
            sem((7,)),
            sem((MEMBERS, 2, n_dp - 1)),
            sem((MEMBERS, 2, n_dp - 1)),
            sem((lines - 1,)),
            sem((lines - 1,)),
            sem((lines,)),
            sem((lines,)),
        ]
        + [sem((2, 2, n_dp - 1))] * 4,
        compiler_params=pltpu.CompilerParams(
            collective_id=0, has_side_effects=True, vmem_limit_bytes=62 * 2**20
        ),
        cost_estimate=pl.CostEstimate(flops=34 * 10**9, bytes_accessed=40 * 10**6, transcendentals=5 * 10**6),
        name="front",
    )(group_of, offsets, xp, xc, dp, dc, w1, w2, wqkv, wd, table, *vectors)


def tail_kernel(
    n_dp, n_tensor, early, group_ref, xp, xc, dp, dc, picked, o, g, da1, da2, wd, w2, w1s, w2s, wg,
    gain_one_ref, gain_two_ref, bias_one_ref, bias_two_ref, vec,
    out_p, out_c, grad_p, grad_c, w1_out, w2_out, wg_out, vec_out,
    part, rc, sy, ry, o_v, g_v, wd_v, w2_v, xq, dyq, xm, xh, dyh, keep_y, keep_d, ag, ring, fin,
    small, small_core, small_y, small_ring, sum1, sum2, sum3, got3,
    load_sem, part_sem, rc_send, rc_recv, ry_send, ry_recv, ag_send, ag_recv, agc_send, agc_recv,
    ring_send, ring_recv, sc_send, sc_recv, sy_send, sy_recv, fin_send, fin_recv, finc_send, finc_recv,
    out_sem, outc_sem, sum_load, sum_out, rs_send, rs_recv, wag_send, wag_recv,
):
    prompt_len, width = xp.shape
    cont_total = xc.shape[0]
    conts = MEMBERS
    piece = CONT_LEN // n_tensor
    lines = n_tensor // 2
    quarter = prompt_len // n_tensor
    few = conts * piece
    me_dp, me_t = lax.axis_index("dp"), lax.axis_index("tensor")
    core = lax.rem(me_t, jnp.int32(2))
    line = lax.div(me_t, jnp.int32(2))
    sibling = me_t + 1 - 2 * core
    peers = [lax.rem(me_t + 2 * k, jnp.int32(n_tensor)) for k in range(1, lines)]
    spot, after, before = ring_neighbours(n_dp)
    base_one, base_two, base_y = 4 * few, 4 * few + quarter, 4 * few + 2 * quarter
    group_rows = (slice(0, base_one), slice(base_one, base_y), slice(base_y, base_y + quarter))

    loads = [
        (o, o_v), (wd, wd_v), (g, g_v), (w2, w2_v),
        (xp.at[span(me_t * quarter, quarter, 16)], xq),
        (dp.at[span(me_t * quarter, quarter, 16)], dyq),
        (picked, xm),
    ]
    for s in range(conts):
        loads.append((xc.at[span(s * CONT_LEN + me_t * piece, piece, 16)], xh.at[s]))
        loads.append((dc.at[span(s * CONT_LEN + me_t * piece, piece, 16)], dyh.at[s]))
    loads = [pltpu.make_async_copy(src, dst, load_sem.at[i]) for i, (src, dst) in enumerate(loads)]
    fills = []
    for q in range(n_tensor):
        pairs = [
            (da1.at[pl.ds(q * quarter, quarter)], part.at[q, pl.ds(base_one, quarter)]),
            (da2.at[pl.ds(cont_total + q * quarter, quarter)], part.at[q, pl.ds(base_two, quarter)]),
        ]
        for s in range(conts):
            at = s * CONT_LEN + q * piece
            pairs.append((da1.at[pl.ds(prompt_len + at, piece)], part.at[q, pl.ds(2 * few + s * piece, piece)]))
            pairs.append((da2.at[pl.ds(at, piece)], part.at[q, pl.ds(3 * few + s * piece, piece)]))
        fills += [pltpu.make_async_copy(src, dst, part_sem.at[q, i]) for i, (src, dst) in enumerate(pairs)]
    sum_loads = [
        pltpu.make_async_copy(src, dst, sum_load.at[i])
        for i, (src, dst) in enumerate(((wg, sum3), (w1s, sum1), (w2s, sum2)))
    ]
    sum_outs = [
        pltpu.make_async_copy(src, dst, sum_out.at[i])
        for i, (src, dst) in enumerate(((sum3, wg_out), (sum1, w1_out), (sum2, w2_out)))
    ]
    for c in sum_loads:
        c.start()
    for c in sum_loads:
        c.wait()
    for c in loads[:4] + fills + loads[4:]:
        c.start()
    meet([{"tensor": sibling}] + [{"tensor": p} for p in peers] + [{"dp": after}, {"dp": before}])

    summing = RingSum(sum3, got3, rs_send, rs_recv, n_dp)
    gathering = RingGather(sum3, wag_send.at[0], wag_recv.at[0], n_dp)
    rest = [RingGather(s, wag_send.at[i], wag_recv.at[i], n_dp) for i, s in ((1, sum1), (2, sum2))]
    left = n_dp - 1 - early
    summing.start(jnp.int32(0))
    if left > 0:
        rest[0].start(jnp.int32(early))

    def rest_tick(t):
        for i, part_gather in enumerate(rest):
            @pl.when((t >= i * left) & (t < (i + 1) * left))
            def _():
                part_gather.finish(t - i * left + early)

            @pl.when((t >= i * left) & (t < (i + 1) * left - 1))
            def _():
                part_gather.start(t - i * left + early + 1)

        @pl.when(t == left - 1)
        def _():
            rest[1].start(jnp.int32(early))

    cont_from = min(2 * left, 4)
    all_ticks = max(2 * (n_dp - 1), 2 * left, cont_from + n_dp - 1)

    def run_ticks(begin, end):
        def one(t, _):
            advance(summing, gathering, t, 2 * (n_dp - 1))
            rest_tick(t)
            k = t - cont_from

            @pl.when((k >= 0) & (k < n_dp - 1))
            def _():
                for c in steps(k):
                    c.wait()

            @pl.when((k >= 0) & (k < n_dp - 2))
            def _():
                for c in steps(k + 1):
                    c.start()

            return 0

        lax.fori_loop(begin, end, one, 0)

    def steps(k):
        ahead = lax.rem(spot - k + n_dp, jnp.int32(n_dp))
        back = lax.rem(spot + k, jnp.int32(n_dp))
        return (
            remote(ring.at[ahead, 0], ring.at[ahead, 0], ring_send.at[0, k], ring_recv.at[0, k], {"dp": after}),
            remote(ring.at[back, 1], ring.at[back, 1], ring_send.at[1, k], ring_recv.at[1, k], {"dp": before}),
            remote(
                small_ring.at[ahead], small_ring.at[ahead], ring_send.at[2, k], ring_recv.at[2, k], {"dp": after}
            ),
        )

    small[...] = vec[...]
    small_to_core = remote(small, small_core, sc_send, sc_recv, {"tensor": sibling})
    small_to_core.start()

    for c in loads[:4]:
        c.wait()
    o_cont = dot(o_v[prompt_len:], wd_v[...]).astype(bf16)
    g_cont = dot(g_v[:cont_total], w2_v[...]).astype(bf16)
    for q in range(n_tensor):
        for s in range(conts):
            from_rows = slice(s * CONT_LEN + q * piece, s * CONT_LEN + (q + 1) * piece)
            part[q, s * piece : (s + 1) * piece] = o_cont[from_rows]
            part[q, few + s * piece : few + (s + 1) * piece] = g_cont[from_rows]
    for c in fills:
        c.wait()

    def to_core(n):
        return [
            remote(
                part.at[2 * j + 1 - core, group_rows[n]], rc.at[j, group_rows[n]],
                rc_send.at[n, j], rc_recv.at[n, j], {"tensor": sibling},
            )
            for j in range(lines)
        ]

    def to_line(n):
        return [
            remote(
                sy.at[k, group_rows[n]], ry.at[k, group_rows[n]], ry_send.at[n, k], ry_recv.at[n, k], {"tensor": p}
            )
            for k, p in enumerate(peers)
        ]

    for c in to_core(0) + to_core(1):
        c.start()
    run_ticks(0, 1)

    def outputs(q, _):
        at = span(q * quarter, quarter, quarter)
        total = dot(o_v[at], wd_v[...]) + dot(g_v[span(cont_total + q * quarter, quarter, quarter)], w2_v[...])
        part[q, group_rows[2]] = total.astype(bf16)
        return 0

    lax.fori_loop(0, n_tensor, outputs, 0)
    for c in to_core(2):
        c.start()

    small_to_core.wait()
    row = lax.broadcasted_iota(jnp.int32, (8, 1), 0)
    small_y[line] = small[...] + jnp.where(row < 4, small_core[...], 0.0)
    small_to_line = [
        remote(small_y.at[line], small_y.at[line], sy_send.at[k], sy_recv.at[k], {"tensor": p})
        for k, p in enumerate(peers)
    ]
    for c in small_to_line:
        c.start()
    for n in range(3):
        if n == 2:
            run_ticks(1, 2)
        for c in to_core(n):
            c.wait()
        for k in range(1, lines):
            j = lax.rem(line + k, jnp.int32(lines))
            sy[k - 1, group_rows[n]] = (
                part[2 * j + core, group_rows[n]].astype(f32) + rc[j, group_rows[n]].astype(f32)
            ).astype(bf16)
        for c in to_line(n):
            c.start()
    run_ticks(2, cont_from)
    for c in loads[4:]:
        c.wait()

    def summed(start, size):
        at = pl.ds(start, size)
        total = part[me_t, at].astype(f32) + rc[line, at].astype(f32)
        for k in range(lines - 1):
            total = total + ry[k, at].astype(f32)
        return total

    gain_one, gain_two = as_row(gain_one_ref), as_row(gain_two_ref)
    bias = as_row(bias_one_ref) + as_row(bias_two_ref)
    for c in to_line(0):
        c.wait()
    for s in range(conts):
        ring[spot, 0, s] = summed(s * piece, piece).astype(bf16)
        pulled = norm_pull(xm[s].astype(f32), summed(2 * few + s * piece, piece) * gain_one)
        ring[spot, 1, s] = pulled.astype(bf16)
        home = xh[s].astype(f32)
        keep_y[s] = home + summed(few + s * piece, piece) + bias
        keep_d[s] = dyh[s].astype(f32) + norm_pull(home, summed(3 * few + s * piece, piece) * gain_two)
    for c in small_to_line:
        c.wait()
    reduced = small_y[0]
    for j in range(1, lines):
        reduced = reduced + small_y[j]
    small_ring[spot] = jnp.where(row < 4, reduced, small[...])

    for c in steps(jnp.int32(0)):
        c.start()
    run_ticks(cont_from, cont_from + 4)

    def gather_line(a):
        return [
            remote(ag.at[me_t, a], ag.at[me_t, a], ag_send.at[a, k], ag_recv.at[a, k], {"tensor": p})
            for k, p in enumerate(peers)
        ]

    def gather_core(a):
        return [
            remote(
                ag.at[2 * j + core, a], ag.at[2 * j + core, a], agc_send.at[a, j], agc_recv.at[a, j],
                {"tensor": sibling},
            )
            for j in range(lines)
        ]

    for c in to_line(1):
        c.wait()
    e = summed(base_one, quarter) * gain_one + summed(base_two, quarter) * gain_two
    ag[me_t, 1] = (dyq[...].astype(f32) + norm_pull(xq[...].astype(f32), e)).astype(bf16)
    for c in gather_line(1):
        c.start()
    run_ticks(cont_from + 4, cont_from + 5)
    for c in to_line(2):
        c.wait()
    ag[me_t, 0] = (xq[...].astype(f32) + summed(base_y, quarter) + bias).astype(bf16)
    for c in gather_line(0):
        c.start()

    moved_home = cont_from + n_dp - 1
    run_ticks(cont_from + 5, moved_home)
    total = small_ring[0]
    for j in range(1, n_dp):
        total = total + small_ring[j]
    vec_out[...] = total

    for s in range(conts):
        mine = me_dp * conts + s
        group = group_ref[mine]
        first, _ = find_members(group_ref, group)
        slot = jnp.where(first == mine, jnp.int32(0), jnp.int32(1))
        where = ring_spot(group, n_dp)
        fin[me_t, 0, s] = (keep_y[s] + ring[where, 0, slot].astype(f32)).astype(bf16)
        fin[me_t, 1, s] = (keep_d[s] + ring[where, 1, slot].astype(f32)).astype(bf16)
    fin_line = [
        remote(fin.at[me_t], fin.at[me_t], fin_send.at[k], fin_recv.at[k], {"tensor": p})
        for k, p in enumerate(peers)
    ]
    fin_core = [
        remote(
            fin.at[2 * j + core], fin.at[2 * j + core], finc_send.at[j], finc_recv.at[j], {"tensor": sibling}
        )
        for j in range(lines)
    ]
    for c in fin_line:
        c.start()
    run_ticks(moved_home, moved_home + 1)
    for c in gather_line(1):
        c.wait()
    for c in gather_core(1):
        c.start()
    run_ticks(moved_home + 1, moved_home + 2)
    for c in gather_line(0):
        c.wait()
    for c in gather_core(0):
        c.start()
    for c in fin_line:
        c.wait()
    for c in fin_core:
        c.start()
    run_ticks(moved_home + 2, max(moved_home + 2, all_ticks))
    for c in sum_outs:
        c.start()
    outs = []
    for a, dst in ((1, grad_p), (0, out_p)):
        for c in gather_core(a):
            c.wait()
        for q in range(n_tensor):
            outs.append(
                pltpu.make_async_copy(ag.at[q, a], dst.at[pl.ds(q * quarter, quarter)], out_sem.at[a, q])
            )
            outs[-1].start()
    for c in fin_core:
        c.wait()
    for a, dst in ((1, grad_c), (0, out_c)):
        for q in range(n_tensor):
            for s in range(conts):
                outs.append(
                    pltpu.make_async_copy(
                        fin.at[q, a, s], dst.at[pl.ds(s * CONT_LEN + q * piece, piece)], outc_sem.at[a, q, s]
                    )
                )
                outs[-1].start()
    for c in outs + sum_outs:
        c.wait()


def run_tail(
    n_dp, n_tensor, early, group_of, xp, xc, dp, dc, picked, o, g, da1, da2, wd, w2, w1s, w2s, wg, *vecs
):
    prompt_len, width = xp.shape
    cont_total = xc.shape[0]
    conts = MEMBERS
    piece = CONT_LEN // n_tensor
    lines = n_tensor // 2
    quarter = prompt_len // n_tensor
    stack = 4 * conts * piece + 3 * quarter
    shape = jax.ShapeDtypeStruct
    hbm = pl.BlockSpec(memory_space=pl.ANY)
    vmem = pl.BlockSpec(memory_space=pltpu.VMEM)
    smem = pl.BlockSpec(memory_space=pltpu.SMEM)
    sem = pltpu.SemaphoreType.DMA
    return pl.pallas_call(
        functools.partial(tail_kernel, n_dp, n_tensor, early),
        out_shape=(
            shape(xp.shape, bf16),
            shape(xc.shape, bf16),
            shape(xp.shape, bf16),
            shape(xc.shape, bf16),
            shape(w1s.shape, bf16),
            shape(w2s.shape, bf16),
            shape(wg.shape, bf16),
            shape((8, width), f32),
        ),
        in_specs=[smem] + [hbm] * 14 + [vmem] * 5,
        out_specs=(hbm,) * 7 + (vmem,),
        scratch_shapes=[
            pltpu.VMEM((n_tensor, stack, width), bf16),
            pltpu.VMEM((lines, stack, width), bf16),
            pltpu.VMEM((lines - 1, stack, width), bf16),
            pltpu.VMEM((lines - 1, stack, width), bf16),
            pltpu.VMEM(o.shape, bf16),
            pltpu.VMEM(g.shape, bf16),
            pltpu.VMEM(wd.shape, bf16),
            pltpu.VMEM(w2.shape, bf16),
            pltpu.VMEM((quarter, width), bf16),
            pltpu.VMEM((quarter, width), bf16),
            pltpu.VMEM((conts, piece, width), bf16),
            pltpu.VMEM((conts, piece, width), bf16),
            pltpu.VMEM((conts, piece, width), bf16),
            pltpu.VMEM((conts, piece, width), f32),
            pltpu.VMEM((conts, piece, width), f32),
            pltpu.VMEM((n_tensor, 2, quarter, width), bf16),
            pltpu.VMEM((n_dp, 2, conts, piece, width), bf16),
            pltpu.VMEM((n_tensor, 2, conts, piece, width), bf16),
            pltpu.VMEM((8, width), f32),
            pltpu.VMEM((8, width), f32),
            pltpu.VMEM((lines, 8, width), f32),
            pltpu.VMEM((n_dp, 8, width), f32),
            pltpu.VMEM(w1s.shape, bf16),
            pltpu.VMEM(w2s.shape, bf16),
            pltpu.VMEM(wg.shape, bf16),
            pltpu.VMEM((n_dp - 1,) + wg.shape[1:], bf16),
            sem((7 + 2 * conts,)),
            sem((n_tensor, 2 + 2 * conts)),
            sem((3, lines)),
            sem((3, lines)),
            sem((3, lines - 1)),
            sem((3, lines - 1)),
            sem((2, lines - 1)),
            sem((2, lines - 1)),
            sem((2, lines)),
            sem((2, lines)),
            sem((3, n_dp - 1)),
            sem((3, n_dp - 1)),
            sem,
            sem,
            sem((lines - 1,)),
            sem((lines - 1,)),
            sem((lines - 1,)),
            sem((lines - 1,)),
            sem((lines,)),
            sem((lines,)),
            sem((2, n_tensor)),
            sem((2, n_tensor, conts)),
            sem((3,)),
            sem((3,)),
            sem((2, n_dp - 1)),
            sem((2, n_dp - 1)),
            sem((3, 2, n_dp - 1)),
            sem((3, 2, n_dp - 1)),
        ],
        compiler_params=pltpu.CompilerParams(
            collective_id=1, has_side_effects=True, vmem_limit_bytes=58 * 2**20
        ),
        cost_estimate=pl.CostEstimate(flops=20 * 10**9, bytes_accessed=30 * 10**6, transcendentals=0),
        name="tail",
    )(group_of, xp, xc, dp, dc, picked, o, g, da1, da2, wd, w2, w1s, w2s, wg, *vecs)


def finish_kernel(
    hidden, local3, out_p, out_c, grad_p, grad_c, w1s, w2s, wg, total,
    out_p_out, out_c_out, grad_p_out, grad_c_out, gain_one, shift_one, gain_two, shift_two,
    qkv_out, qkv_bias, dense_out, dense_bias, w1_out, w1_bias, w2_out, w2_bias,
):
    for src, dst in (
        (out_p, out_p_out), (out_c, out_c_out), (grad_p, grad_p_out), (grad_c, grad_c_out),
    ):
        dst[...] = src[...]

    def unpack(src, dst, cols=slice(None)):
        chunks = src.shape[0]
        size = dst.shape[0] // (2 * chunks)
        for p in range(2 * chunks):
            dst[p * size : (p + 1) * size, :] = src[p // 2, p % 2, :size, cols].astype(f32)

    unpack(w1s, w1_out)
    unpack(w2s, w2_out)
    lane = lax.broadcasted_iota(jnp.int32, (1, CHUNK), 1)
    for pair in range(local3 // (3 * CHUNK)):
        columns = [slice((3 * pair + c) * CHUNK, (3 * pair + c + 1) * CHUNK) for c in range(3)]
        for p in range(2 * wg.shape[0]):
            size = wg.shape[2]
            parts = unpair_columns(*(wg[p // 2, p % 2, :, cols].astype(f32) for cols in columns), lane)
            for cols, value in zip(columns, parts):
                qkv_out[p * size : (p + 1) * size, cols] = value
    chunks, size = wg.shape[0], wg.shape[2]
    dense = [wg[p // 2, p % 2, :, local3:].astype(f32) for p in range(2 * chunks)]
    dense_out[...] = jnp.concatenate(dense, axis=0).T

    @pl.when(pl.program_id(0) == 0)
    def _():
        for n, dst in enumerate(
            (gain_one, shift_one, gain_two, shift_two, dense_bias, w1_bias, qkv_bias)
        ):
            if n < 6:
                dst[...] = total[n, : dst.shape[0]]
        w2_bias[...] = total[4, :]
        for pair in range(local3 // (3 * CHUNK)):
            columns = [slice((3 * pair + c) * CHUNK, (3 * pair + c + 1) * CHUNK) for c in range(3)]
            parts = unpair_columns(*(total[6:7, cols] for cols in columns), lane)
            for cols, value in zip(columns, parts):
                qkv_bias[cols] = value[0]


def run_finish(n_dp, local3, hidden, out_p, out_c, grad_p, grad_c, w1s, w2s, wg, total):
    width = out_p.shape[1]
    local = local3 // 3
    steps = 8
    shape = jax.ShapeDtypeStruct

    def rows_of(a):
        return pl.BlockSpec((a.shape[0] // steps, a.shape[1]), lambda i: (i, 0))

    def pieces_of(a):
        return pl.BlockSpec((a.shape[0] // steps,) + a.shape[1:], lambda i: (i, 0, 0, 0))

    def vector(size):
        return pl.BlockSpec((size,), lambda i: (0,))

    def weight(rows, cols):
        return pl.BlockSpec((rows // steps, cols), lambda i: (i, 0))

    moved = [rows_of(a) for a in (out_p, out_c, grad_p, grad_c)]
    return pl.pallas_call(
        functools.partial(finish_kernel, hidden, local3),
        grid=(steps,),
        out_shape=tuple(shape(a.shape, bf16) for a in (out_p, out_c, grad_p, grad_c))
        + (shape((width,), f32),) * 4
        + (
            shape((width, local3), f32), shape((local3,), f32),
            shape((local, width), f32), shape((width,), f32),
            shape((width, hidden), f32), shape((hidden,), f32),
            shape((hidden, width), f32), shape((width,), f32),
        ),
        in_specs=moved + [pieces_of(a) for a in (w1s, w2s, wg)] + [pl.BlockSpec((8, width), lambda i: (0, 0))],
        out_specs=tuple(moved)
        + (vector(width),) * 4
        + (
            weight(width, local3), vector(local3),
            pl.BlockSpec((local, width // steps), lambda i: (0, i)), vector(width),
            weight(width, hidden), vector(hidden),
            weight(hidden, width), vector(width),
        ),
        compiler_params=pltpu.CompilerParams(vmem_limit_bytes=60 * 2**20),
        name="finish",
    )(out_p, out_c, grad_p, grad_c, w1s, w2s, wg, total)


def per_device(
    n_dp, n_tensor,
    prompt_in, cont_in, prompt_cot, cont_cot, group_of, offsets, ln1_gain, ln1_bias, ln2_gain, ln2_bias,
    qkv_weight, qkv_bias, dense_weight, dense_bias, fc1_weight, fc1_bias, fc2_weight, fc2_bias,
):
    width = prompt_in.shape[1]
    hidden = fc1_weight.shape[1]
    local3 = qkv_weight.shape[1]

    early = min(n_dp - 1, 5)
    g, da2, o, da1, w1g, w2g, wg, picked, vec = run_front(
        n_dp, n_tensor, early, group_of, offsets, prompt_in, cont_in, prompt_cot, cont_cot,
        fc1_weight, fc2_weight, qkv_weight, dense_weight,
        ln2_gain, ln2_bias, fc1_bias, ln1_gain, ln1_bias, qkv_bias,
    )
    out_p, out_c, grad_p, grad_c, w1g, w2g, wg, total = run_tail(
        n_dp, n_tensor, early, group_of, prompt_in, cont_in, prompt_cot, cont_cot, picked, o, g, da1, da2,
        dense_weight, fc2_weight, w1g, w2g, wg, ln1_gain, ln2_gain, dense_bias, fc2_bias, vec,
    )
    return run_finish(n_dp, local3, hidden, out_p, out_c, grad_p, grad_c, w1g, w2g, wg, total)


def solution(mesh):
    rows, whole, columns, segment, depth = P("dp", None), P(), P(None, "tensor"), P("tensor"), P("tensor", None)
    return jax.shard_map(
        functools.partial(per_device, mesh.shape["dp"], mesh.shape["tensor"]),
        mesh=mesh,
        in_specs=(
            rows, rows, rows, rows, whole, whole, whole, whole, whole, whole,
            columns, segment, depth, whole, columns, segment, depth, whole,
        ),
        out_specs=(
            rows, rows, rows, rows, whole, whole, whole, whole,
            columns, segment, depth, whole, columns, segment, depth, whole,
        ),
        check_vma=False,
    )
```

```python
import functools
import math

import jax
import jax.numpy as jnp
import numpy as np
from jax import lax
from jax.experimental import pallas as pl
from jax.experimental.pallas import tpu as pltpu
from jax.sharding import PartitionSpec as P

HD = 64
ROT = 16
CONT_LEN = 128
TILE = 256
CHUNK = 128
MEMBERS = 2

eps_norm = 1e-05
masked_value = -1e30
MESH = pl.DeviceIdType.MESH
bf16 = jnp.bfloat16
f32 = jnp.float32


def dot(a, b):
    return jnp.dot(a, b, preferred_element_type=f32)


def dot_nt(a, b):
    return lax.dot_general(a, b, (((1,), (1,)), ((), ())), preferred_element_type=f32)


def dot_tn(a, b):
    return lax.dot_general(a, b, (((0,), (0,)), ((), ())), preferred_element_type=f32)


def row_stats(x):
    centered = x - jnp.mean(x, axis=-1, keepdims=True)
    scale = lax.rsqrt(jnp.mean(centered * centered, axis=-1, keepdims=True) + eps_norm)
    return centered * scale, scale


def norm_pull(x, e):
    xhat, scale = row_stats(x)
    return scale * (
        e
        - jnp.mean(e, axis=-1, keepdims=True)
        - xhat * jnp.mean(e * xhat, axis=-1, keepdims=True)
    )


def gelu_and_slope(u):
    t = 1.0 / (1.0 + jnp.abs(u) * (0.3275911 / math.sqrt(2.0)))
    bell = jnp.exp(-0.5 * u * u)
    poly = t * (
        0.127414796
        + t * (-0.142248368 + t * (0.7107068705 + t * (-0.7265760135 + t * 0.5307027145)))
    )
    tail = poly * bell
    cdf = jnp.where(u >= 0, 1.0 - tail, tail)
    return u * cdf, cdf + u * bell * (1.0 / math.sqrt(2.0 * math.pi))


def rotary_table(length):
    half = ROT // 2
    frequencies = np.exp(
        -np.arange(half, dtype=np.float32) * np.float32(2.0 * math.log(10000.0) / ROT)
    ).astype(np.float32)
    angles = np.arange(length, dtype=np.float32)[:, None] * frequencies[None, :]
    angles = np.concatenate([angles, angles], axis=1).astype(np.float32)
    cos = np.ones((length, HD), np.float32)
    low = np.zeros((length, HD), np.float32)
    high = np.zeros((length, HD), np.float32)
    cos[:, :ROT] = np.cos(angles)
    low[:, :half] = -np.sin(angles)[:, :half]
    high[:, half:ROT] = np.sin(angles)[:, half:]
    return np.stack([np.concatenate([t, t], axis=1) for t in (cos, low, high)])


def ring_spot(device, n):
    odd = lax.rem(device, jnp.int32(2))
    half = lax.div(device, jnp.int32(2))
    return (1 - odd) * half + odd * (n - 1 - half)


def ring_device(spot, n):
    far = lax.div(spot, jnp.int32(n // 2))
    return (1 - far) * (2 * spot) + far * (2 * (n - 1 - spot) + 1)


def ring_neighbours(n):
    spot = ring_spot(lax.axis_index("dp"), n)
    after = ring_device(lax.rem(spot + 1, jnp.int32(n)), n)
    before = ring_device(lax.rem(spot + n - 1, jnp.int32(n)), n)
    return spot, after, before


def find_members(group_ref, wanted):
    count = group_ref.shape[0]
    first = jnp.int32(count)
    last = jnp.int32(-1)
    for j in range(count):
        hit = group_ref[j] == wanted
        first = jnp.minimum(first, jnp.where(hit, jnp.int32(j), jnp.int32(count)))
        last = jnp.maximum(last, jnp.where(hit, jnp.int32(j), jnp.int32(-1)))
    return jnp.minimum(first, count - 1), jnp.maximum(last, 0)


def meet(devices):
    barrier = pltpu.get_barrier_semaphore()
    for device in devices:
        pl.semaphore_signal(barrier, inc=1, device_id=device, device_id_type=MESH)
    pl.semaphore_wait(barrier, len(devices))


def remote(src, dst, send, recv, device):
    return pltpu.make_async_remote_copy(
        src_ref=src, dst_ref=dst, send_sem=send, recv_sem=recv, device_id=device, device_id_type=MESH
    )


def as_row(ref):
    return ref[...].astype(f32).reshape(1, ref.shape[0])


def span(start, size, step):
    return pl.ds(pl.multiple_of(start, step), size)


def piece_rows(rows, n):
    return rows // (2 * n), max(16, rows // (2 * n))


def ring_shape(rows, width, n):
    return (n, 2, piece_rows(rows, n)[1], width)


def put_tile(buffer, k, value, rows, n, cols=slice(None)):
    size = piece_rows(rows, n)[0]
    pieces = TILE // size
    for p in range(pieces):
        buffer[k * (pieces // 2) + p // 2, p % 2, :size, cols] = value[p * size : (p + 1) * size].astype(bf16)


def pair_columns(c0, c1, c2, lane):
    low = lane < HD
    crossed = jnp.where(low, c2, c0)
    return jnp.where(low, c0, c1), pltpu.roll(crossed, HD, 1), jnp.where(low, c1, c2)


def unpair_columns(q, k, v, lane):
    low = lane < HD
    crossed = pltpu.roll(k, HD, 1)
    return jnp.where(low, q, crossed), jnp.where(low, v, q), jnp.where(low, crossed, v)


class RingSum:
    def __init__(self, buffer, arrived, send, recv, n):
        self.buffer, self.arrived, self.send, self.recv, self.n = buffer, arrived, send, recv, n
        self.spot, self.after, self.before = ring_neighbours(n)

    def copies(self, k):
        n = self.n
        ahead = lax.rem(self.spot + (2 * n - 1) - k, jnp.int32(n))
        back = lax.rem(self.spot + 1 + k, jnp.int32(n))
        return [
            remote(
                self.buffer.at[chunk, way], self.arrived.at[k, way], self.send.at[way, k], self.recv.at[way, k],
                {"dp": device},
            )
            for way, (chunk, device) in enumerate(((ahead, self.after), (back, self.before)))
        ]

    def start(self, k):
        for c in self.copies(k):
            c.start()

    def finish(self, k):
        n = self.n
        for c in self.copies(k):
            c.wait()
        for way, chunk in enumerate(
            (lax.rem(self.spot + (2 * n - 2) - k, jnp.int32(n)), lax.rem(self.spot + 2 + k, jnp.int32(n)))
        ):
            self.buffer[chunk, way] = (
                self.buffer[chunk, way].astype(f32) + self.arrived[k, way].astype(f32)
            ).astype(bf16)


class RingGather:
    def __init__(self, buffer, send, recv, n, part=()):
        self.buffer, self.send, self.recv, self.n, self.part = buffer, send, recv, n, part
        self.spot, self.after, self.before = ring_neighbours(n)

    def copies(self, k):
        n = self.n
        ahead = lax.rem(self.spot + n - k, jnp.int32(n))
        back = lax.rem(self.spot + k, jnp.int32(n))
        return [
            remote(
                self.buffer.at[(chunk, way) + self.part], self.buffer.at[(chunk, way) + self.part],
                self.send.at[way, k], self.recv.at[way, k], {"dp": device},
            )
            for way, (chunk, device) in enumerate(((ahead, self.after), (back, self.before)))
        ]

    def start(self, k):
        for c in self.copies(k):
            c.start()

    def finish(self, k):
        for c in self.copies(k):
            c.wait()


def advance(summing, gathering, t, stop):
    n = summing.n

    @pl.when(t < n - 1)
    def _():
        summing.finish(t)

    @pl.when(t < n - 2)
    def _():
        summing.start(t + 1)

    @pl.when((t == n - 2) & (stop > n - 1))
    def _():
        gathering.start(jnp.int32(0))

    @pl.when((t >= n - 1) & (t < stop))
    def _():
        gathering.finish(t - (n - 1))

    @pl.when((t >= n - 1) & (t < stop - 1))
    def _():
        gathering.start(t - (n - 2))


def layer_kernel(
    n_dp, n_tensor, early, group_ref, offsets, xp, xc, dp, dc, w1, w2, wqkv, wd, table,
    gain_two_ref, shift_two_ref, bias1_ref, gain_one_ref, shift_one_ref, bias_qkv_ref, bias_one_ref, bias_two_ref,
    out_p, out_c, grad_p, grad_c, w1s_out, w2s_out, wg_out, stack, vec_out,
    x_all, dy_all, w1_v, w2_v, wqkv_v, wd_v, tab, h_all, g_all, mixed, da_all, ring, moved,
    sum1, sum2, got1, got2, wg, qs, dos, ks, vs, k_turned, v_turned, dks, dvs, o_all, y_home,
    rc, ry, own_rows, keep_y, keep_d, fin, small, small_core, small_y, small_ring,
    own_sem, load_sem, out_sem, part_sem, home_sem, ring_send, ring_recv, y_send, y_recv, core_send, core_recv,
    rs_send, rs_recv, ag_send, ag_recv,
    fill_sem, rc_send, rc_recv, ry_send, ry_recv, gl_send, gl_recv, gc_send, gc_recv,
    home_send, home_recv, sc_send, sc_recv, sy_send, sy_recv, fin_send, fin_recv, finc_send, finc_recv,
    rows_sem, outc_sem, x_send, x_recv, xg_send, xg_recv,
):
    prompt_len, width = xp.shape
    cont_total = xc.shape[0]
    conts = MEMBERS
    rows = prompt_len + cont_total
    tiles = rows // TILE
    prompt_tiles = prompt_len // TILE
    hidden = w1.shape[1]
    local = wd.shape[0]
    heads = local // HD
    piece = CONT_LEN // n_tensor
    lines = n_tensor // 2
    table_len = table.shape[1]
    scale = 1.0 / math.sqrt(HD)
    me_dp, me_t = lax.axis_index("dp"), lax.axis_index("tensor")
    core = lax.rem(me_t, jnp.int32(2))
    sibling = me_t + 1 - 2 * core
    peers = [lax.rem(me_t + 2 * k, jnp.int32(n_tensor)) for k in range(1, lines)]
    spot, after, before = ring_neighbours(n_dp)

    own = [
        pltpu.make_async_copy(
            src.at[span(s * CONT_LEN + me_t * piece, piece, 16)], ring.at[spot, a, s], own_sem.at[a, s]
        )
        for a, src in enumerate((xc, dc))
        for s in range(conts)
    ]
    loads = [
        pltpu.make_async_copy(src, dst, load_sem.at[i])
        for i, (src, dst) in enumerate(
            (
                (xc, x_all.at[pl.ds(0, cont_total)]),
                (w1, w1_v),
                (dc, dy_all.at[pl.ds(0, cont_total)]),
                (w2, w2_v),
                (xp, x_all.at[pl.ds(cont_total, prompt_len)]),
                (dp, dy_all.at[pl.ds(cont_total, prompt_len)]),
                (wqkv, wqkv_v),
                (wd, wd_v),
                (table, tab.at[:, pl.ds(0, table_len)]),
            )
        )
    ]
    for c in own + [loads[i] for i in (1, 0, 4, 2, 5, 3, 6, 7, 8)]:
        c.start()
    meet([{"dp": after}, {"dp": before}, {"tensor": sibling}] + [{"tensor": p} for p in peers])

    halves = min(2, piece // 16)
    moving = [
        RingGather(
            ring, ring_send.at[s, b], ring_recv.at[s, b], n_dp, (s, pl.ds(b * (piece // halves), piece // halves))
        )
        for s in range(conts)
        for b in range(halves)
    ]
    for c in own:
        c.wait()
    for m in moving:
        m.start(jnp.int32(0))
    sums = [
        (
            RingSum(buffer, got, rs_send.at[i], rs_recv.at[i], n_dp),
            RingGather(buffer, ag_send.at[i], ag_recv.at[i], n_dp),
        )
        for i, (buffer, got) in enumerate(((sum2, got2), (sum1, got1)))
    ]

    def spread(point, points, total, step):
        begin = lax.div(point * total, jnp.int32(points))
        end = lax.div((point + 1) * total, jnp.int32(points))

        def one(t, _):
            step(t)
            return 0

        lax.fori_loop(begin, end, one, 0)

    def move_step(t):
        k = lax.div(t, jnp.int32(len(moving)))
        for s, m in enumerate(moving):
            mine = lax.rem(t, jnp.int32(len(moving))) == s

            @pl.when(mine)
            def _():
                m.finish(k)

            @pl.when(mine & (k < n_dp - 2))
            def _():
                m.start(k + 1)

    move_points = 2 * tiles + hidden // TILE

    def move(point):
        spread(point, move_points, len(moving) * (n_dp - 1), move_step)

    stop = n_dp - 1 + early
    lead = min(2, stop)
    sum_points = prompt_tiles + 3 * heads + width // TILE + tiles

    def sum_step(t):
        k = lax.div(t, jnp.int32(2))

        @pl.when(lax.rem(t, jnp.int32(2)) == 0)
        def _():
            advance(*sums[1], k, stop)

        @pl.when((lax.rem(t, jnp.int32(2)) == 1) & (k + lead < stop))
        def _():
            advance(*sums[0], k + lead, stop)

    def turn(point):
        spread(point, sum_points, 2 * stop - 1, sum_step)

    few = conts * piece
    quarter = prompt_len // n_tensor

    def deal(src, prompt_row, cont_row, prompt_base, cont_base, which):
        copies = []
        for q in range(n_tensor):
            copies.append(
                pltpu.make_async_copy(
                    src.at[pl.ds(prompt_row + q * quarter, quarter)], stack.at[q, pl.ds(prompt_base, quarter)],
                    part_sem.at[which, q, conts],
                )
            )
            for s in range(conts):
                copies.append(
                    pltpu.make_async_copy(
                        src.at[pl.ds(cont_row + s * CONT_LEN + q * piece, piece)],
                        stack.at[q, pl.ds(cont_base + s * piece, piece)], part_sem.at[which, q, s],
                    )
                )
        return copies

    deal_da2 = deal(da_all, cont_total, 0, 4 * few + quarter, 3 * few, 0)
    deal_da1 = deal(da_all, 0, prompt_len, 4 * few, 2 * few, 1)
    deal_y = deal(da_all, 0, prompt_len, 4 * few + 2 * quarter, 0, 2)
    deal_home = [
        pltpu.make_async_copy(
            y_home.at[pl.ds(s * CONT_LEN + q * piece, piece)], stack.at[q, pl.ds(few + s * piece, piece)],
            home_sem.at[q, s],
        )
        for q in range(n_tensor)
        for s in range(conts)
    ]
    outs = [
        pltpu.make_async_copy(src, dst, out_sem.at[i])
        for i, (src, dst) in enumerate(((sum1, w1s_out), (sum2, w2s_out), (wg, wg_out)))
    ]
    small[...] = jnp.zeros_like(small)

    gain, shift, bias = as_row(gain_two_ref), as_row(shift_two_ref), as_row(bias1_ref)
    loads[0].wait()
    loads[1].wait()

    def mlp_forward(i, _):
        @pl.when(i == 1)
        def _():
            loads[4].wait()

        at = span(i * TILE, TILE, TILE)
        xhat, _ = row_stats(x_all[at].astype(f32))
        h = (xhat * gain + shift).astype(bf16)
        h_all[at] = h
        for k in range(hidden // TILE):
            cols = slice(k * TILE, (k + 1) * TILE)
            value, slope = gelu_and_slope(dot(h, w1_v[:, cols]) + bias[:, cols])
            g_all[at, cols] = value.astype(bf16)
            mixed[at, cols] = slope.astype(bf16)
        move(i)
        return 0

    lax.fori_loop(0, tiles, mlp_forward, 0)
    loads[2].wait()
    loads[5].wait()

    def down_tile(k, _):
        cols = span(k * TILE, TILE, TILE)
        put_tile(sum2, k, dot_tn(g_all[:, cols], dy_all[:rows]), hidden, n_dp)
        move(tiles + k)
        return 0

    lax.fori_loop(0, hidden // TILE, down_tile, 0)
    sums[0][0].start(jnp.int32(0))
    loads[3].wait()

    def mlp_backward(i, _):
        at = span(i * TILE, TILE, TILE)
        dy = dy_all[at]
        for k in range(hidden // TILE):
            cols = slice(k * TILE, (k + 1) * TILE)
            du = (dot_nt(dy, w2_v[cols, :]) * mixed[at, cols].astype(f32)).astype(bf16)
            mixed[at, cols] = du
            small[5:6, cols] += jnp.sum(du.astype(f32), axis=0, keepdims=True)
        da = dot_nt(mixed[at, :hidden], w1_v[...])
        da_all[at] = da.astype(bf16)
        xhat, _ = row_stats(x_all[at].astype(f32))
        small[2:3] += jnp.sum(da * xhat, axis=0, keepdims=True)
        small[3:4] += jnp.sum(da, axis=0, keepdims=True)
        small[4:5] += jnp.sum(dy.astype(f32), axis=0, keepdims=True)
        move(tiles + hidden // TILE + i)

        @pl.when((lax.rem(i, jnp.int32(2)) == 0) & (i > 0) & (lax.div(i, jnp.int32(2)) <= lead))
        def _():
            advance(*sums[0], lax.div(i, jnp.int32(2)) - 1, stop)

        return 0

    lax.fori_loop(0, tiles, mlp_backward, 0)
    for c in deal_da2:
        c.start()

    members = find_members(group_ref, me_dp)
    offs = [offsets[m] for m in members]
    for m, member in enumerate(members):
        where = ring_spot(lax.div(member, jnp.int32(conts)), n_dp)
        slot = lax.rem(member, jnp.int32(conts))
        for a in range(2):
            moved[me_t, a, m] = ring[where, a, slot]
    over_y = [
        remote(moved.at[me_t], moved.at[me_t], y_send.at[k], y_recv.at[k], {"tensor": p})
        for k, p in enumerate(peers)
    ]
    over_core = [
        remote(
            moved.at[2 * j + core], moved.at[2 * j + core], core_send.at[j], core_recv.at[j], {"tensor": sibling}
        )
        for j in range(lines)
    ]
    for c in over_y:
        c.start()

    def up_tile(k, _):
        cols = span(k * TILE, TILE, TILE)
        put_tile(sum1, k, dot_tn(h_all[:, cols], mixed[:, :hidden]), width, n_dp)
        return 0

    lax.fori_loop(0, width // TILE, up_tile, 0)
    sums[1][0].start(jnp.int32(0))

    for c in loads[6:]:
        c.wait()
    for m, off in enumerate(offs):
        for a in range(3):
            tab[a, table_len + m * CONT_LEN : table_len + (m + 1) * CONT_LEN, :] = tab[a, pl.ds(off, CONT_LEN), :]
    gain, shift = as_row(gain_one_ref), as_row(shift_one_ref)
    lane = lax.broadcasted_iota(jnp.int32, (1, CHUNK), 1)
    bias = as_row(bias_qkv_ref)
    biases = []
    for pair in range(heads // 2):
        chunks = [slice((3 * pair + c) * CHUNK, (3 * pair + c + 1) * CHUNK) for c in range(3)]
        biases += pair_columns(*(bias[:, cols] for cols in chunks), lane)
        for cols, value in zip(chunks, pair_columns(*(wqkv_v[:, cols] for cols in chunks), lane)):
            wqkv_v[:, cols] = value

    def turned(z, start, sign):
        cos, low, high = (tab[a, pl.ds(start, TILE), :] for a in range(3))
        half = ROT // 2
        return z * cos + (pltpu.roll(z, CHUNK - half, 1) * low + pltpu.roll(z, half, 1) * high) * sign

    def table_start(i):
        return pl.multiple_of(i * TILE + lax.div(i, jnp.int32(prompt_tiles)) * (table_len - prompt_len), CHUNK)

    def project(i):
        at = span(i * TILE, TILE, TILE)
        source = span(i * TILE + cont_total, TILE, TILE)
        xhat, _ = row_stats(x_all[source].astype(f32))
        h = (xhat * gain + shift).astype(bf16)
        h_all[at] = h
        do = dot_nt(dy_all[source], wd_v[...]).astype(bf16)
        for pair in range(heads // 2):
            q, k, v = (
                dot(h, wqkv_v[:, c * CHUNK : (c + 1) * CHUNK]) + biases[c] for c in range(3 * pair, 3 * pair + 3)
            )
            q = turned(q, table_start(i), 1.0)
            qs[2 * pair, at] = jnp.where(lane < HD, q, 0.0).astype(bf16)
            qs[2 * pair + 1, at] = jnp.where(lane < HD, 0.0, q).astype(bf16)
            k = turned(k, table_start(i), 1.0)
            ks[pair, at] = k.astype(bf16)
            k_turned[pair, :, at] = k.T.astype(bf16)
            vs[pair, at] = v.astype(bf16)
            v_turned[pair, :, at] = v.T.astype(bf16)
            both = do[:, pair * CHUNK : (pair + 1) * CHUNK].astype(f32)
            dos[2 * pair, at] = jnp.where(lane < HD, both, 0.0).astype(bf16)
            dos[2 * pair + 1, at] = jnp.where(lane < HD, 0.0, both).astype(bf16)

    def project_prompt(i, _):
        project(i)
        turn(i)
        return 0

    lax.fori_loop(0, prompt_tiles, project_prompt, 0)
    for c in over_y:
        c.wait()
    for c in over_core:
        c.start()

    query_lane = lax.broadcasted_iota(jnp.int32, (1, TILE), 1)
    reach = jnp.zeros((1, TILE), jnp.int32)
    for m, off in enumerate(offs):
        reach = jnp.where(lax.div(query_lane, jnp.int32(CONT_LEN)) == m, off, reach)

    def attend(pair, _):
        for block in list(range(prompt_tiles - 1, -1, -1)) + [prompt_tiles]:
            first = block * TILE
            seen = first + TILE
            at = slice(first, seen)
            if block == prompt_tiles:
                @pl.when(pair == 0)
                def _():
                    for c in over_core:
                        c.wait()
                    for q in range(n_tensor):
                        for s in range(conts):
                            to = rows + s * CONT_LEN + q * piece
                            x_all[to : to + piece, :] = moved[q, 0, s]
                            dy_all[to : to + piece, :] = moved[q, 1, s]
                    project(jnp.int32(prompt_tiles))

            k, v = ks[pair, :seen], vs[pair, :seen]
            key = lax.broadcasted_iota(jnp.int32, (TILE, TILE), 0)
            query = lax.broadcasted_iota(jnp.int32, (TILE, TILE), 1)
            seen_near = key <= query
            if block == prompt_tiles:
                key_row = lax.broadcasted_iota(jnp.int32, (prompt_len, TILE), 0)
                same = lax.div(key, jnp.int32(CONT_LEN)) == lax.div(query, jnp.int32(CONT_LEN))
                seen_near = seen_near & same
            heads_now = (2 * pair, 2 * pair + 1)
            scores = [dot_nt(k, qs[h, at]) * scale for h in heads_now]
            dprobs = [dot_nt(v, dos[h, at]) for h in heads_now]
            lows, low_slopes, o_turned, dq_turned = [], [], [], []
            for sub in range(2):
                s, dprob = scores[sub], dprobs[sub]
                near = jnp.where(seen_near, s[first:], masked_value)
                if block == prompt_tiles:
                    s = jnp.concatenate([jnp.where(key_row < reach, s[:first], masked_value), near], axis=0)
                else:
                    s = near if first == 0 else jnp.concatenate([s[:first], near], axis=0)
                p = jnp.exp(s - jnp.max(s, axis=0, keepdims=True))
                p = p * (1.0 / jnp.sum(p, axis=0, keepdims=True))
                low = p.astype(bf16)
                delta = jnp.sum(p * dprob, axis=0, keepdims=True)
                ds = (p * (dprob - delta)).astype(bf16)
                part = slice(sub * HD, (sub + 1) * HD)
                o_turned.append(dot(v_turned[pair, part, :seen], low))
                dq_turned.append(dot(k_turned[pair, part, :seen], ds))
                lows.append(low)
                low_slopes.append(ds)
            o_all[at, span(pair * CHUNK, CHUNK, CHUNK)] = jnp.concatenate(o_turned, axis=0).T.astype(bf16)
            dq = jnp.concatenate(dq_turned, axis=0).T * scale
            dq = turned(dq, table_start(jnp.int32(block)), -1.0).astype(bf16)
            cols = span(3 * pair * CHUNK, CHUNK, CHUNK)
            mixed[at, cols] = dq
            small[6:7, cols] += jnp.sum(dq.astype(f32), axis=0, keepdims=True)
            q_both = jnp.concatenate([qs[h, at] for h in heads_now], axis=0)
            do_both = jnp.concatenate([dos[h, at] for h in heads_now], axis=0)
            dk = dot(jnp.concatenate(low_slopes, axis=1), q_both)
            dv = dot(jnp.concatenate(lows, axis=1), do_both)
            if block == prompt_tiles - 1:
                dks[:seen] = dk
                dvs[:seen] = dv
            else:
                old = min(seen, prompt_len)
                dks[:old] += dk[:old]
                dvs[:old] += dv[:old]
                if old < seen:
                    dks[old:seen] = dk[old:]
                    dvs[old:seen] = dv[old:]
            turn(prompt_tiles + 6 * pair + (prompt_tiles - 1 - block if block < prompt_tiles else block))

        for i in range(tiles):
            at = slice(i * TILE, (i + 1) * TILE)
            dk = turned(dks[at] * scale, table_start(jnp.int32(i)), -1.0).astype(bf16)
            for c, value in ((1, dk), (2, dvs[at].astype(bf16))):
                cols = span((3 * pair + c) * CHUNK, CHUNK, CHUNK)
                mixed[at, cols] = value
                small[6:7, cols] += jnp.sum(value.astype(f32), axis=0, keepdims=True)
        turn(prompt_tiles + 6 * pair + 5)
        return 0

    lax.fori_loop(0, heads // 2, attend, 0)
    for c in deal_da2:
        c.wait()

    def back(i, _):
        at = span(i * TILE, TILE, TILE)
        da = dot_nt(mixed[at, : 3 * local], wqkv_v[...])
        da_all[at] = da.astype(bf16)
        xhat, _ = row_stats(x_all[span(i * TILE + cont_total, TILE, TILE)].astype(f32))
        small[0:1] += jnp.sum(da * xhat, axis=0, keepdims=True)
        small[1:2] += jnp.sum(da, axis=0, keepdims=True)

        turn(prompt_tiles + 3 * heads + i)
        return 0

    lax.fori_loop(0, tiles, back, 0)
    for c in deal_da1:
        c.start()

    def weight_tile(k, _):
        cols = span(k * TILE, TILE, TILE)
        put_tile(wg, k, dot_tn(h_all[:, cols], mixed[:, : 3 * local]), width, n_dp, slice(0, 3 * local))
        put_tile(wg, k, dot_tn(dy_all[cont_total:, cols], o_all[...]), width, n_dp, slice(3 * local, 4 * local))
        turn(prompt_tiles + 3 * heads + tiles + k)
        return 0

    lax.fori_loop(0, width // TILE, weight_tile, 0)
    summing = RingSum(wg, got1, x_send, x_recv, n_dp)
    gathering = RingGather(wg, xg_send, xg_recv, n_dp)
    rest = [gather for _, gather in sums]
    left = n_dp - 1 - early
    cont_from = 6
    all_ticks = max(2 * (n_dp - 1), 2 * left, cont_from + n_dp - 1)
    summing.start(jnp.int32(0))
    if left > 0:
        rest[0].start(jnp.int32(early))

    def rest_tick(t):
        for i, gather in enumerate(rest):
            @pl.when((t >= i * left) & (t < (i + 1) * left))
            def _():
                gather.finish(t - i * left + early)

            @pl.when((t >= i * left) & (t < (i + 1) * left - 1))
            def _():
                gather.start(t - i * left + early + 1)

        @pl.when(t == left - 1)
        def _():
            rest[1].start(jnp.int32(early))

    def home_steps(k):
        ahead = lax.rem(spot - k + n_dp, jnp.int32(n_dp))
        back = lax.rem(spot + k, jnp.int32(n_dp))
        return (
            remote(ring.at[ahead, 0], ring.at[ahead, 0], home_send.at[0, k], home_recv.at[0, k], {"dp": after}),
            remote(ring.at[back, 1], ring.at[back, 1], home_send.at[1, k], home_recv.at[1, k], {"dp": before}),
            remote(
                small_ring.at[ahead], small_ring.at[ahead], home_send.at[2, k], home_recv.at[2, k], {"dp": after}
            ),
        )

    def run_ticks(begin, end):
        def one(t, _):
            advance(summing, gathering, t, 2 * (n_dp - 1))
            rest_tick(t)
            k = t - cont_from

            @pl.when((k >= 0) & (k < n_dp - 1))
            def _():
                for c in home_steps(k):
                    c.wait()

            @pl.when((k >= 0) & (k < n_dp - 2))
            def _():
                for c in home_steps(k + 1):
                    c.start()

            return 0

        lax.fori_loop(begin, end, one, 0)

    line = lax.div(me_t, jnp.int32(2))
    base_one, base_two, base_y = 4 * few, 4 * few + quarter, 4 * few + 2 * quarter
    depth = base_y + quarter
    group_rows = ((0, base_one), (base_one, 2 * quarter), (base_y, quarter))
    room = rows // depth

    def own_part(m, start, size):
        return (h_all, da_all)[m // room].at[pl.ds((m % room) * depth + start, size)]

    def fill(n, m):
        j = lax.rem(line + (m + 1), jnp.int32(lines))
        return pltpu.make_async_copy(
            stack.at[2 * j + core, pl.ds(*group_rows[n])], own_part(m, *group_rows[n]), fill_sem.at[n, m]
        )

    def to_core(n):
        at = pl.ds(*group_rows[n])
        return [
            remote(
                stack.at[2 * j + 1 - core, at], rc.at[j, at], rc_send.at[n, j], rc_recv.at[n, j], {"tensor": sibling}
            )
            for j in range(lines)
        ]

    def to_line(n):
        return [
            remote(
                own_part(k, *group_rows[n]), ry.at[k, pl.ds(*group_rows[n])], ry_send.at[n, k], ry_recv.at[n, k],
                {"tensor": p},
            )
            for k, p in enumerate(peers)
        ]

    def pass_on(n):
        for c in to_core(n):
            c.wait()
        for k in range(lines - 1):
            j = lax.rem(line + (k + 1), jnp.int32(lines))
            mine = own_part(k, *group_rows[n])
            mine[...] = (mine[...].astype(f32) + rc[j, pl.ds(*group_rows[n])].astype(f32)).astype(bf16)
        for c in to_line(n):
            c.start()

    small_to_core = remote(small, small_core, sc_send, sc_recv, {"tensor": sibling})
    small_to_core.start()
    for c in deal_da1:
        c.wait()
    for c in to_core(1):
        c.start()

    def y_tile(i, _):
        at = span(i * TILE, TILE, TILE)
        total = dot(o_all[at], wd_v[...]) + dot(g_all[span(i * TILE + cont_total, TILE, TILE)], w2_v[...])
        da_all[at] = total.astype(bf16)
        return 0

    lax.fori_loop(0, prompt_tiles, y_tile, 0)
    da_all[prompt_len:] = dot(o_all[prompt_len:], wd_v[...]).astype(bf16)
    y_home[...] = dot(g_all[:cont_total], w2_v[...]).astype(bf16)
    for c in deal_y + deal_home:
        c.start()
    run_ticks(0, 1)
    for c in deal_y + deal_home:
        c.wait()
    for n in (0, 2):
        for c in to_core(n):
            c.start()
    fills = [fill(n, m) for n in (1, 0, 2) for m in range(lines)]
    for c in fills:
        c.start()
    small_to_core.wait()
    row = lax.broadcasted_iota(jnp.int32, (8, 1), 0)
    small_y[line] = small[...] + jnp.where(row < 4, small_core[...], 0.0)
    small_to_line = [
        remote(small_y.at[line], small_y.at[line], sy_send.at[k], sy_recv.at[k], {"tensor": p})
        for k, p in enumerate(peers)
    ]
    for c in small_to_line:
        c.start()
    for c in fills:
        c.wait()
    pass_on(1)
    run_ticks(1, 2)
    pass_on(0)
    pass_on(2)
    for c in small_to_line:
        c.wait()
    reduced = small_y[0]
    for j in range(1, lines):
        reduced = reduced + small_y[j]
    small_ring[spot] = jnp.where(row < 4, reduced, small[...])
    run_ticks(2, cont_from - 1)

    def summed(start, size):
        total = own_part(lines - 1, start, size)[...].astype(f32) + rc[line, pl.ds(start, size)].astype(f32)
        for k in range(lines - 1):
            total = total + ry[k, pl.ds(start, size)].astype(f32)
        return total

    def quarter_rows(q):
        return pl.ds(pl.multiple_of(q * quarter, 16), quarter)

    gain_two = as_row(gain_two_ref)
    both = as_row(bias_one_ref) + as_row(bias_two_ref)
    results = (out_p, grad_p)

    def gather_line(a):
        at = quarter_rows(me_t)
        return [pltpu.make_async_copy(own_rows.at[a], results[a].at[at], rows_sem.at[a])] + [
            remote(own_rows.at[a], results[a].at[at], gl_send.at[a, k], gl_recv.at[a, k], {"tensor": p})
            for k, p in enumerate(peers)
        ]

    def gather_core(a):
        at = quarter_rows(me_t)
        copies = [remote(own_rows.at[a], results[a].at[at], gc_send.at[a, 0], gc_recv.at[a, 0], {"tensor": sibling})]
        for k in range(1, lines):
            at = quarter_rows(2 * lax.rem(line + k, jnp.int32(lines)) + core)
            copies.append(
                remote(results[a].at[at], results[a].at[at], gc_send.at[a, k], gc_recv.at[a, k], {"tensor": sibling})
            )
        return copies

    quarter_at = span(cont_total + me_t * quarter, quarter, 16)
    for c in to_line(1):
        c.wait()
    e = summed(base_one, quarter) * gain + summed(base_two, quarter) * gain_two
    own_rows[1] = (dy_all[quarter_at].astype(f32) + norm_pull(x_all[quarter_at].astype(f32), e)).astype(bf16)
    for c in gather_line(1) + gather_core(1)[:1]:
        c.start()
    run_ticks(cont_from - 1, cont_from)
    for c in to_line(0):
        c.wait()
    for s in range(conts):
        ring[spot, 0, s] = summed(s * piece, piece).astype(bf16)
        theirs = x_all[span(rows + s * CONT_LEN + me_t * piece, piece, 16)].astype(f32)
        ring[spot, 1, s] = norm_pull(theirs, summed(2 * few + s * piece, piece) * gain).astype(bf16)
        home = span(s * CONT_LEN + me_t * piece, piece, 16)
        x_home = x_all[home].astype(f32)
        keep_y[s] = x_home + summed(few + s * piece, piece) + both
        pulled = norm_pull(x_home, summed(3 * few + s * piece, piece) * gain_two)
        keep_d[s] = dy_all[home].astype(f32) + pulled
    for c in home_steps(jnp.int32(0)):
        c.start()
    run_ticks(cont_from, cont_from + 2)
    for c in to_line(2):
        c.wait()
    own_rows[0] = (x_all[quarter_at].astype(f32) + summed(base_y, quarter) + both).astype(bf16)
    for c in gather_line(0) + gather_core(0)[:1]:
        c.start()
    run_ticks(cont_from + 2, cont_from + 5)
    for c in gather_line(1):
        c.wait()
    for c in gather_core(1)[1:]:
        c.start()
    moved_home = cont_from + n_dp - 1
    run_ticks(cont_from + 5, moved_home)
    total = small_ring[0]
    for j in range(1, n_dp):
        total = total + small_ring[j]
    vec_out[...] = total
    for s in range(conts):
        mine = me_dp * conts + s
        group = group_ref[mine]
        first, _ = find_members(group_ref, group)
        slot = jnp.where(first == mine, jnp.int32(0), jnp.int32(1))
        where = ring_spot(group, n_dp)
        fin[me_t, 0, s] = (keep_y[s] + ring[where, 0, slot].astype(f32)).astype(bf16)
        fin[me_t, 1, s] = (keep_d[s] + ring[where, 1, slot].astype(f32)).astype(bf16)
    fin_line = [
        remote(fin.at[me_t], fin.at[me_t], fin_send.at[k], fin_recv.at[k], {"tensor": p})
        for k, p in enumerate(peers)
    ]
    fin_core = [
        remote(
            fin.at[2 * j + core], fin.at[2 * j + core], finc_send.at[j], finc_recv.at[j], {"tensor": sibling}
        )
        for j in range(lines)
    ]
    for c in fin_line:
        c.start()
    for c in gather_line(0):
        c.wait()
    for c in gather_core(0)[1:]:
        c.start()
    run_ticks(moved_home, max(moved_home, all_ticks))
    for c in outs:
        c.start()
    for c in fin_line:
        c.wait()
    for c in fin_core:
        c.start()
    for c in gather_core(0) + gather_core(1) + fin_core:
        c.wait()
    last = [
        pltpu.make_async_copy(
            fin.at[q, a, s], dst.at[pl.ds(s * CONT_LEN + q * piece, piece)], outc_sem.at[a, q, s]
        )
        for a, dst in ((0, out_c), (1, grad_c))
        for q in range(n_tensor)
        for s in range(conts)
    ]
    for c in last:
        c.start()
    for c in last + outs:
        c.wait()


def run_layer(n_dp, n_tensor, early, group_of, offsets, xp, xc, dp, dc, w1, w2, wqkv, wd, *vectors):
    prompt_len, width = xp.shape
    cont_total = xc.shape[0]
    rows = prompt_len + cont_total
    hidden = w1.shape[1]
    local = wd.shape[0]
    heads = local // HD
    piece = CONT_LEN // n_tensor
    lines = n_tensor // 2
    table = jnp.asarray(rotary_table(prompt_len + CONT_LEN))
    table_rows = table.shape[1] + MEMBERS * CONT_LEN
    up, down = ring_shape(width, hidden, n_dp), ring_shape(hidden, width, n_dp)
    third = ring_shape(width, 4 * local, n_dp)
    quarter = prompt_len // n_tensor
    depth = 4 * MEMBERS * piece + 3 * quarter
    shape = jax.ShapeDtypeStruct
    hbm = pl.BlockSpec(memory_space=pl.ANY)
    vmem = pl.BlockSpec(memory_space=pltpu.VMEM)
    smem = pl.BlockSpec(memory_space=pltpu.SMEM)
    sem = pltpu.SemaphoreType.DMA
    return pl.pallas_call(
        functools.partial(layer_kernel, n_dp, n_tensor, early),
        out_shape=(
            shape(xp.shape, bf16),
            shape(xc.shape, bf16),
            shape(xp.shape, bf16),
            shape(xc.shape, bf16),
            shape(up, bf16),
            shape(down, bf16),
            shape(third, bf16),
            shape((n_tensor, depth, width), bf16),
            shape((8, width), f32),
        ),
        in_specs=[smem] * 2 + [hbm] * 9 + [vmem] * 8,
        out_specs=(hbm,) * 8 + (vmem,),
        scratch_shapes=[
            pltpu.VMEM((rows + cont_total, width), bf16),
            pltpu.VMEM((rows + cont_total, width), bf16),
            pltpu.VMEM((width, hidden), bf16),
            pltpu.VMEM((hidden, width), bf16),
            pltpu.VMEM((width, 3 * local), bf16),
            pltpu.VMEM((local, width), bf16),
            pltpu.VMEM((3, table_rows, CHUNK), f32),
            pltpu.VMEM((rows, width), bf16),
            pltpu.VMEM((rows, hidden), bf16),
            pltpu.VMEM((rows, max(hidden, 3 * local)), bf16),
            pltpu.VMEM((rows, width), bf16),
            pltpu.VMEM((n_dp, 2, MEMBERS, piece, width), bf16),
            pltpu.VMEM((n_tensor, 2, MEMBERS, piece, width), bf16),
            pltpu.VMEM(up, bf16),
            pltpu.VMEM(down, bf16),
            pltpu.VMEM((n_dp - 1,) + up[1:], bf16),
            pltpu.VMEM((n_dp - 1,) + down[1:], bf16),
            pltpu.VMEM(third, bf16),
        ]
        + [pltpu.VMEM((heads, rows, CHUNK), bf16)] * 2
        + [pltpu.VMEM((heads // 2, rows, CHUNK), bf16)] * 2
        + [pltpu.VMEM((heads // 2, CHUNK, rows), bf16)] * 2
        + [pltpu.VMEM((rows, CHUNK), f32)] * 2
        + [
            pltpu.VMEM((rows, local), bf16),
            pltpu.VMEM((cont_total, width), bf16),
            pltpu.VMEM((lines, depth, width), bf16),
            pltpu.VMEM((lines - 1, depth, width), bf16),
            pltpu.VMEM((2, quarter, width), bf16),
            pltpu.VMEM((MEMBERS, piece, width), f32),
            pltpu.VMEM((MEMBERS, piece, width), f32),
            pltpu.VMEM((n_tensor, 2, MEMBERS, piece, width), bf16),
            pltpu.VMEM((8, width), f32),
            pltpu.VMEM((8, width), f32),
            pltpu.VMEM((lines, 8, width), f32),
            pltpu.VMEM((n_dp, 8, width), f32),
            sem((2, MEMBERS)),
            sem((9,)),
            sem((3,)),
            sem((3, n_tensor, MEMBERS + 1)),
            sem((n_tensor, MEMBERS)),
            sem((MEMBERS, 2, 2, n_dp - 1)),
            sem((MEMBERS, 2, 2, n_dp - 1)),
            sem((lines - 1,)),
            sem((lines - 1,)),
            sem((lines,)),
            sem((lines,)),
        ]
        + [sem((2, 2, n_dp - 1))] * 4
        + [sem((3, lines))] * 3
        + [sem((3, lines - 1))] * 2
        + [sem((2, lines - 1))] * 2
        + [sem((2, lines))] * 2
        + [sem((3, n_dp - 1))] * 2
        + [sem] * 2
        + [sem((lines - 1,))] * 4
        + [sem((lines,))] * 2
        + [sem((2,)), sem((2, n_tensor, MEMBERS))]
        + [sem((2, n_dp - 1))] * 4,
        compiler_params=pltpu.CompilerParams(
            collective_id=0, has_side_effects=True, vmem_limit_bytes=63 * 2**20
        ),
        cost_estimate=pl.CostEstimate(flops=34 * 10**9, bytes_accessed=40 * 10**6, transcendentals=5 * 10**6),
        name="layer",
    )(group_of, offsets, xp, xc, dp, dc, w1, w2, wqkv, wd, table, *vectors)


def finish_kernel(
    groups, out_p, out_c, grad_p, grad_c, w1s, w2s, wg, total,
    out_p_out, out_c_out, grad_p_out, grad_c_out, gain_one, shift_one, gain_two, shift_two,
    qkv_out, qkv_bias, dense_out, dense_bias, w1_out, w1_bias, w2_out, w2_bias,
    out_p_v, out_c_v, grad_p_v, grad_c_v, w1s_v, w2s_v, wg_v, qkv_v, dense_v, w1_v, w2_v,
    copy_in, copy_out, piece_in, piece_out, dense_sem,
):
    local3 = qkv_out.shape[1]
    plain = (
        (out_p, out_p_v, out_p_out), (grad_p, grad_p_v, grad_p_out),
        (out_c, out_c_v, out_c_out), (grad_c, grad_c_v, grad_c_out),
    )
    plain_in = [pltpu.make_async_copy(a, b, copy_in.at[i]) for i, (a, b, _) in enumerate(plain)]
    plain_out = [pltpu.make_async_copy(b, c, copy_out.at[i]) for i, (_, b, c) in enumerate(plain)]
    weights = ((w1s, w1s_v, w1_v, w1_out), (w2s, w2s_v, w2_v, w2_out), (wg, wg_v, qkv_v, qkv_out))

    def chunks_of(a, g):
        return pl.ds(g * (a.shape[0] // groups), a.shape[0] // groups)

    def rows_of(a, g):
        return pl.ds(g * (a.shape[0] // groups), a.shape[0] // groups)

    loads = [
        [pltpu.make_async_copy(a.at[chunks_of(a, g)], b.at[chunks_of(a, g)], piece_in.at[i, g]) for g in range(groups)]
        for i, (a, b, _, _) in enumerate(weights)
    ]
    stores = [
        [pltpu.make_async_copy(c.at[rows_of(c, g)], d.at[rows_of(c, g)], piece_out.at[i, g]) for g in range(groups)]
        for i, (_, _, c, d) in enumerate(weights)
    ]
    for c in plain_in[:1] + loads[0] + plain_in[1:2] + loads[1] + plain_in[2:] + loads[2]:
        c.start()
    lane = lax.broadcasted_iota(jnp.int32, (1, CHUNK), 1)
    pairs = [
        [slice((3 * pair + c) * CHUNK, (3 * pair + c + 1) * CHUNK) for c in range(3)]
        for pair in range(local3 // (3 * CHUNK))
    ]
    for n, dst in enumerate((gain_one, shift_one, gain_two, shift_two, dense_bias, w1_bias)):
        dst[...] = total[n, : dst.shape[0]]
    w2_bias[...] = total[4, :]
    for columns in pairs:
        for cols, value in zip(columns, unpair_columns(*(total[6:7, cols] for cols in columns), lane)):
            qkv_bias[cols] = value[0]

    def pieces(src, dst, g):
        per_group = src.shape[0] // groups
        size = dst.shape[0] // (2 * src.shape[0])
        for p in range(2 * per_group):
            first = g * (dst.shape[0] // groups) + p * size
            yield g * per_group + p // 2, p % 2, size, slice(first, first + size)

    for i in range(2):
        plain_in[i].wait()
        plain_out[i].start()
        _, src, dst, _ = weights[i]
        for g in range(groups):
            loads[i][g].wait()
            for chunk, way, size, to in pieces(src, dst, g):
                dst[to, :] = src[chunk, way, :size].astype(f32)
            stores[i][g].start()
    for i in (2, 3):
        plain_in[i].wait()
        plain_out[i].start()
    for g in range(groups):
        loads[2][g].wait()
        dense = []
        for chunk, way, size, to in pieces(wg_v, qkv_v, g):
            for columns in pairs:
                parts = unpair_columns(*(wg_v[chunk, way, :size, cols].astype(f32) for cols in columns), lane)
                for cols, value in zip(columns, parts):
                    qkv_v[to, cols] = value
            dense.append(wg_v[chunk, way, :size, local3:].astype(f32))
        stores[2][g].start()
        size = dense_v.shape[1] // groups
        dense_v[:, g * size : (g + 1) * size] = jnp.concatenate(dense, axis=0).T
    last = pltpu.make_async_copy(dense_v, dense_out, dense_sem)
    last.start()
    for c in plain_out + stores[0] + stores[1] + stores[2] + [last]:
        c.wait()


def run_finish(local3, hidden, out_p, out_c, grad_p, grad_c, w1s, w2s, wg, total):
    width = out_p.shape[1]
    local = local3 // 3
    groups = 4
    shape = jax.ShapeDtypeStruct
    hbm = pl.BlockSpec(memory_space=pl.ANY)
    vmem = pl.BlockSpec(memory_space=pltpu.VMEM)
    sem = pltpu.SemaphoreType.DMA
    moved = (out_p, out_c, grad_p, grad_c)
    return pl.pallas_call(
        functools.partial(finish_kernel, groups),
        out_shape=tuple(shape(a.shape, bf16) for a in moved)
        + (shape((width,), f32),) * 4
        + (
            shape((width, local3), f32), shape((local3,), f32),
            shape((local, width), f32), shape((width,), f32),
            shape((width, hidden), f32), shape((hidden,), f32),
            shape((hidden, width), f32), shape((width,), f32),
        ),
        in_specs=[hbm] * 7 + [vmem],
        out_specs=(hbm,) * 4 + (vmem,) * 4 + (hbm, vmem) * 4,
        scratch_shapes=[pltpu.VMEM(a.shape, bf16) for a in moved + (w1s, w2s, wg)]
        + [
            pltpu.VMEM((width, local3), f32),
            pltpu.VMEM((local, width), f32),
            pltpu.VMEM((width, hidden), f32),
            pltpu.VMEM((hidden, width), f32),
            sem((4,)),
            sem((4,)),
            sem((3, groups)),
            sem((3, groups)),
            sem,
        ],
        compiler_params=pltpu.CompilerParams(vmem_limit_bytes=60 * 2**20),
        name="finish",
    )(out_p, out_c, grad_p, grad_c, w1s, w2s, wg, total)


def per_device(
    n_dp, n_tensor,
    prompt_in, cont_in, prompt_cot, cont_cot, group_of, offsets, ln1_gain, ln1_bias, ln2_gain, ln2_bias,
    qkv_weight, qkv_bias, dense_weight, dense_bias, fc1_weight, fc1_bias, fc2_weight, fc2_bias,
):
    width = prompt_in.shape[1]
    hidden = fc1_weight.shape[1]
    local3 = qkv_weight.shape[1]

    out_p, out_c, grad_p, grad_c, w1g, w2g, wg, _, total = run_layer(
        n_dp, n_tensor, 0, group_of, offsets, prompt_in, cont_in, prompt_cot, cont_cot,
        fc1_weight, fc2_weight, qkv_weight, dense_weight,
        ln2_gain, ln2_bias, fc1_bias, ln1_gain, ln1_bias, qkv_bias, dense_bias, fc2_bias,
    )
    return run_finish(local3, hidden, out_p, out_c, grad_p, grad_c, w1g, w2g, wg, total)


def solution(mesh):
    rows, whole, columns, segment, depth = P("dp", None), P(), P(None, "tensor"), P("tensor"), P("tensor", None)
    return jax.shard_map(
        functools.partial(per_device, mesh.shape["dp"], mesh.shape["tensor"]),
        mesh=mesh,
        in_specs=(
            rows, rows, rows, rows, whole, whole, whole, whole, whole, whole,
            columns, segment, depth, whole, columns, segment, depth, whole,
        ),
        out_specs=(
            rows, rows, rows, rows, whole, whole, whole, whole,
            columns, segment, depth, whole, columns, segment, depth, whole,
        ),
        check_vma=False,
    )
```

```python
import functools
import math

import jax
import jax.numpy as jnp
import numpy as np
from jax import lax
from jax.experimental import pallas as pl
from jax.experimental.pallas import tpu as pltpu
from jax.sharding import PartitionSpec as P

HD = 64
ROT = 16
CONT_LEN = 128
TILE = 256
CHUNK = 128
MEMBERS = 2

eps_norm = 1e-05
masked_value = -1e30
MESH = pl.DeviceIdType.MESH
bf16 = jnp.bfloat16
f32 = jnp.float32


def dot(a, b):
    return jnp.dot(a, b, preferred_element_type=f32)


def dot_nt(a, b):
    return lax.dot_general(a, b, (((1,), (1,)), ((), ())), preferred_element_type=f32)


def dot_tn(a, b):
    return lax.dot_general(a, b, (((0,), (0,)), ((), ())), preferred_element_type=f32)


def row_stats(x):
    centered = x - jnp.mean(x, axis=-1, keepdims=True)
    scale = lax.rsqrt(jnp.mean(centered * centered, axis=-1, keepdims=True) + eps_norm)
    return centered * scale, scale


def norm_pull(x, e):
    xhat, scale = row_stats(x)
    return scale * (
        e
        - jnp.mean(e, axis=-1, keepdims=True)
        - xhat * jnp.mean(e * xhat, axis=-1, keepdims=True)
    )


def gelu_and_slope(u):
    t = 1.0 / (1.0 + jnp.abs(u) * (0.3275911 / math.sqrt(2.0)))
    bell = jnp.exp(-0.5 * u * u)
    poly = t * (
        0.127414796
        + t * (-0.142248368 + t * (0.7107068705 + t * (-0.7265760135 + t * 0.5307027145)))
    )
    tail = poly * bell
    cdf = jnp.where(u >= 0, 1.0 - tail, tail)
    return u * cdf, cdf + u * bell * (1.0 / math.sqrt(2.0 * math.pi))


def rotary_table(length):
    half = ROT // 2
    frequencies = np.exp(
        -np.arange(half, dtype=np.float32) * np.float32(2.0 * math.log(10000.0) / ROT)
    ).astype(np.float32)
    angles = np.arange(length, dtype=np.float32)[:, None] * frequencies[None, :]
    angles = np.concatenate([angles, angles], axis=1).astype(np.float32)
    cos = np.ones((length, HD), np.float32)
    low = np.zeros((length, HD), np.float32)
    high = np.zeros((length, HD), np.float32)
    cos[:, :ROT] = np.cos(angles)
    low[:, :half] = -np.sin(angles)[:, :half]
    high[:, half:ROT] = np.sin(angles)[:, half:]
    return np.stack([np.concatenate([t, t], axis=1) for t in (cos, low, high)])


def ring_spot(device, n):
    odd = lax.rem(device, jnp.int32(2))
    half = lax.div(device, jnp.int32(2))
    return (1 - odd) * half + odd * (n - 1 - half)


def ring_device(spot, n):
    far = lax.div(spot, jnp.int32(n // 2))
    return (1 - far) * (2 * spot) + far * (2 * (n - 1 - spot) + 1)


def ring_neighbours(n):
    spot = ring_spot(lax.axis_index("dp"), n)
    after = ring_device(lax.rem(spot + 1, jnp.int32(n)), n)
    before = ring_device(lax.rem(spot + n - 1, jnp.int32(n)), n)
    return spot, after, before


def find_members(group_ref, wanted):
    count = group_ref.shape[0]
    first = jnp.int32(count)
    last = jnp.int32(-1)
    for j in range(count):
        hit = group_ref[j] == wanted
        first = jnp.minimum(first, jnp.where(hit, jnp.int32(j), jnp.int32(count)))
        last = jnp.maximum(last, jnp.where(hit, jnp.int32(j), jnp.int32(-1)))
    return jnp.minimum(first, count - 1), jnp.maximum(last, 0)


def meet(devices):
    barrier = pltpu.get_barrier_semaphore()
    for device in devices:
        pl.semaphore_signal(barrier, inc=1, device_id=device, device_id_type=MESH)
    pl.semaphore_wait(barrier, len(devices))


def remote(src, dst, send, recv, device):
    return pltpu.make_async_remote_copy(
        src_ref=src, dst_ref=dst, send_sem=send, recv_sem=recv, device_id=device, device_id_type=MESH
    )


def as_row(ref):
    return ref[...].astype(f32).reshape(1, ref.shape[0])


def span(start, size, step):
    return pl.ds(pl.multiple_of(start, step), size)


def piece_rows(rows, n):
    return rows // (2 * n), max(16, rows // (2 * n))


def ring_shape(rows, width, n):
    return (n, 2, piece_rows(rows, n)[1], width)


def put_tile(buffer, k, value, rows, n, cols=slice(None)):
    size = piece_rows(rows, n)[0]
    pieces = TILE // size
    for p in range(pieces):
        buffer[k * (pieces // 2) + p // 2, p % 2, :size, cols] = value[p * size : (p + 1) * size].astype(bf16)


def pair_columns(c0, c1, c2, lane):
    low = lane < HD
    crossed = jnp.where(low, c2, c0)
    return jnp.where(low, c0, c1), pltpu.roll(crossed, HD, 1), jnp.where(low, c1, c2)


def unpair_columns(q, k, v, lane):
    low = lane < HD
    crossed = pltpu.roll(k, HD, 1)
    return jnp.where(low, q, crossed), jnp.where(low, v, q), jnp.where(low, crossed, v)


class RingSum:
    def __init__(self, buffer, arrived, send, recv, n):
        self.buffer, self.arrived, self.send, self.recv, self.n = buffer, arrived, send, recv, n
        self.spot, self.after, self.before = ring_neighbours(n)

    def copies(self, k):
        n = self.n
        ahead = lax.rem(self.spot + (2 * n - 1) - k, jnp.int32(n))
        back = lax.rem(self.spot + 1 + k, jnp.int32(n))
        return [
            remote(
                self.buffer.at[chunk, way], self.arrived.at[k, way], self.send.at[way, k], self.recv.at[way, k],
                {"dp": device},
            )
            for way, (chunk, device) in enumerate(((ahead, self.after), (back, self.before)))
        ]

    def start(self, k):
        for c in self.copies(k):
            c.start()

    def finish(self, k):
        n = self.n
        for c in self.copies(k):
            c.wait()
        for way, chunk in enumerate(
            (lax.rem(self.spot + (2 * n - 2) - k, jnp.int32(n)), lax.rem(self.spot + 2 + k, jnp.int32(n)))
        ):
            self.buffer[chunk, way] += self.arrived[k, way]


class RingGather:
    def __init__(self, buffer, send, recv, n, part=()):
        self.buffer, self.send, self.recv, self.n, self.part = buffer, send, recv, n, part
        self.spot, self.after, self.before = ring_neighbours(n)

    def copies(self, k):
        n = self.n
        ahead = lax.rem(self.spot + n - k, jnp.int32(n))
        back = lax.rem(self.spot + k, jnp.int32(n))
        return [
            remote(
                self.buffer.at[(chunk, way) + self.part], self.buffer.at[(chunk, way) + self.part],
                self.send.at[way, k], self.recv.at[way, k], {"dp": device},
            )
            for way, (chunk, device) in enumerate(((ahead, self.after), (back, self.before)))
        ]

    def start(self, k):
        for c in self.copies(k):
            c.start()

    def finish(self, k):
        for c in self.copies(k):
            c.wait()


def advance(summing, gathering, t, stop):
    n = summing.n

    @pl.when(t < n - 1)
    def _():
        summing.finish(t)

    @pl.when(t < n - 2)
    def _():
        summing.start(t + 1)

    @pl.when((t == n - 2) & (stop > n - 1))
    def _():
        gathering.start(jnp.int32(0))

    @pl.when((t >= n - 1) & (t < stop))
    def _():
        gathering.finish(t - (n - 1))

    @pl.when((t >= n - 1) & (t < stop - 1))
    def _():
        gathering.start(t - (n - 2))


def layer_kernel(
    n_dp, n_tensor, early, group_ref, offsets, xp, xc, dp, dc, w1, w2, wqkv, wd, table,
    gain_two_ref, shift_two_ref, bias1_ref, gain_one_ref, shift_one_ref, bias_qkv_ref, bias_one_ref, bias_two_ref,
    out_p, out_c, grad_p, grad_c, w1s_out, w2s_out, wg_out, stack, vec_out,
    x_all, dy_all, w1_v, w2_v, wqkv_v, wd_v, tab, h_all, g_all, mixed, da_all, ring, moved,
    sum1, sum2, got1, got2, wg, qs, dos, ks, vs, k_turned, v_turned, dks, dvs, o_all, y_home,
    rc, ry, own_rows, keep_y, keep_d, fin, small, small_core, small_y, small_ring,
    own_sem, load_sem, out_sem, part_sem, home_sem, ring_send, ring_recv, y_send, y_recv, core_send, core_recv,
    rs_send, rs_recv, ag_send, ag_recv,
    fill_sem, rc_send, rc_recv, ry_send, ry_recv, gl_send, gl_recv, gc_send, gc_recv,
    home_send, home_recv, sc_send, sc_recv, sy_send, sy_recv, fin_send, fin_recv, finc_send, finc_recv,
    rows_sem, outc_sem, x_send, x_recv, xg_send, xg_recv,
):
    prompt_len, width = xp.shape
    cont_total = xc.shape[0]
    conts = MEMBERS
    rows = prompt_len + cont_total
    tiles = rows // TILE
    prompt_tiles = prompt_len // TILE
    hidden = w1.shape[1]
    local = wd.shape[0]
    heads = local // HD
    piece = CONT_LEN // n_tensor
    lines = n_tensor // 2
    table_len = table.shape[1]
    scale = 1.0 / math.sqrt(HD)
    me_dp, me_t = lax.axis_index("dp"), lax.axis_index("tensor")
    core = lax.rem(me_t, jnp.int32(2))
    sibling = me_t + 1 - 2 * core
    peers = [lax.rem(me_t + 2 * k, jnp.int32(n_tensor)) for k in range(1, lines)]
    spot, after, before = ring_neighbours(n_dp)

    own = [
        pltpu.make_async_copy(
            src.at[span(s * CONT_LEN + me_t * piece, piece, 16)], ring.at[spot, a, s], own_sem.at[a, s]
        )
        for a, src in enumerate((xc, dc))
        for s in range(conts)
    ]
    loads = [
        pltpu.make_async_copy(src, dst, load_sem.at[i])
        for i, (src, dst) in enumerate(
            (
                (xc, x_all.at[pl.ds(0, cont_total)]),
                (w1, w1_v),
                (dc, dy_all.at[pl.ds(0, cont_total)]),
                (w2, w2_v),
                (xp, x_all.at[pl.ds(cont_total, prompt_len)]),
                (dp, dy_all.at[pl.ds(cont_total, prompt_len)]),
                (wqkv, wqkv_v),
                (wd, wd_v),
                (table, tab.at[:, pl.ds(0, table_len)]),
            )
        )
    ]
    for c in own + [loads[i] for i in (1, 0, 4, 2, 5, 3, 6, 7, 8)]:
        c.start()
    meet([{"dp": after}, {"dp": before}, {"tensor": sibling}] + [{"tensor": p} for p in peers])

    halves = min(2, piece // 16)
    moving = [
        RingGather(
            ring, ring_send.at[s, b], ring_recv.at[s, b], n_dp, (s, pl.ds(b * (piece // halves), piece // halves))
        )
        for s in range(conts)
        for b in range(halves)
    ]
    for c in own:
        c.wait()
    for m in moving:
        m.start(jnp.int32(0))
    sums = [
        (
            RingSum(buffer, got, rs_send.at[i], rs_recv.at[i], n_dp),
            RingGather(buffer, ag_send.at[i], ag_recv.at[i], n_dp),
        )
        for i, (buffer, got) in enumerate(((sum2, got2), (sum1, got1)))
    ]

    def spread(point, points, total, step):
        begin = lax.div(point * total, jnp.int32(points))
        end = lax.div((point + 1) * total, jnp.int32(points))

        def one(t, _):
            step(t)
            return 0

        lax.fori_loop(begin, end, one, 0)

    def move_step(t):
        k = lax.div(t, jnp.int32(len(moving)))
        for s, m in enumerate(moving):
            mine = lax.rem(t, jnp.int32(len(moving))) == s

            @pl.when(mine)
            def _():
                m.finish(k)

            @pl.when(mine & (k < n_dp - 2))
            def _():
                m.start(k + 1)

    move_points = 2 * tiles + hidden // TILE

    def move(point):
        spread(point, move_points, len(moving) * (n_dp - 1), move_step)

    stop = 2 * (n_dp - 1)
    lead = 2
    all_turns = 2 * (n_dp - 1 + early) - 1
    pair_turns = all_turns * 2 // (3 * heads // 2)
    project_turns = all_turns // 9
    back_turns = (all_turns - project_turns - pair_turns * (heads // 2)) // 2
    back_from = project_turns + pair_turns * (heads // 2)
    block_ends = (8, 14, 19, 22, 32, 35)

    def sum_step(t):
        k = lax.div(t, jnp.int32(2))

        @pl.when(lax.rem(t, jnp.int32(2)) == 0)
        def _():
            advance(*sums[1], k, stop)

        @pl.when((lax.rem(t, jnp.int32(2)) == 1) & (k + lead < stop))
        def _():
            advance(*sums[0], k + lead, stop)

    def turn(begin, end):
        def one(t, _):
            sum_step(t)
            return 0

        lax.fori_loop(begin, end, one, 0)

    def turn_evenly(base, point, points, total):
        spread(point, points, total, lambda t: sum_step(base + t))

    def turn_block(pair, place):
        base = project_turns + pair * pair_turns
        ends = [pair_turns * b // block_ends[-1] for b in (0,) + block_ends]
        if ends[place] < ends[place + 1]:
            turn(base + ends[place], base + ends[place + 1])

    few = conts * piece
    quarter = prompt_len // n_tensor

    def deal(src, prompt_row, cont_row, prompt_base, cont_base, which):
        copies = []
        for q in range(n_tensor):
            copies.append(
                pltpu.make_async_copy(
                    src.at[pl.ds(prompt_row + q * quarter, quarter)], stack.at[q, pl.ds(prompt_base, quarter)],
                    part_sem.at[which, q, conts],
                )
            )
            for s in range(conts):
                copies.append(
                    pltpu.make_async_copy(
                        src.at[pl.ds(cont_row + s * CONT_LEN + q * piece, piece)],
                        stack.at[q, pl.ds(cont_base + s * piece, piece)], part_sem.at[which, q, s],
                    )
                )
        return copies

    deal_da2 = deal(da_all, cont_total, 0, 4 * few + quarter, 3 * few, 0)
    deal_da1 = deal(da_all, 0, prompt_len, 4 * few, 2 * few, 1)
    deal_y = deal(da_all, 0, prompt_len, 4 * few + 2 * quarter, 0, 2)
    deal_home = [
        pltpu.make_async_copy(
            y_home.at[pl.ds(s * CONT_LEN + q * piece, piece)], stack.at[q, pl.ds(few + s * piece, piece)],
            home_sem.at[q, s],
        )
        for q in range(n_tensor)
        for s in range(conts)
    ]
    outs = [
        pltpu.make_async_copy(src, dst, out_sem.at[i])
        for i, (src, dst) in enumerate(((sum1, w1s_out), (sum2, w2s_out), (wg, wg_out)))
    ]
    small[...] = jnp.zeros_like(small)

    gain, shift, bias = as_row(gain_two_ref), as_row(shift_two_ref), as_row(bias1_ref)
    loads[0].wait()
    loads[1].wait()

    def mlp_forward(i, _):
        @pl.when(i == 1)
        def _():
            loads[4].wait()

        at = span(i * TILE, TILE, TILE)
        xhat, _ = row_stats(x_all[at].astype(f32))
        h = (xhat * gain + shift).astype(bf16)
        h_all[at] = h
        for k in range(hidden // TILE):
            cols = slice(k * TILE, (k + 1) * TILE)
            value, slope = gelu_and_slope(dot(h, w1_v[:, cols]) + bias[:, cols])
            g_all[at, cols] = value.astype(bf16)
            mixed[at, cols] = slope.astype(bf16)
        move(i)
        return 0

    lax.fori_loop(0, tiles, mlp_forward, 0)
    loads[2].wait()
    loads[5].wait()

    def down_tile(k, _):
        cols = span(k * TILE, TILE, TILE)
        put_tile(sum2, k, dot_tn(g_all[:, cols], dy_all[:rows]), hidden, n_dp)
        move(tiles + k)
        return 0

    lax.fori_loop(0, hidden // TILE, down_tile, 0)
    sums[0][0].start(jnp.int32(0))
    loads[3].wait()

    def mlp_backward(i, _):
        at = span(i * TILE, TILE, TILE)
        dy = dy_all[at]
        for k in range(hidden // TILE):
            cols = slice(k * TILE, (k + 1) * TILE)
            du = (dot_nt(dy, w2_v[cols, :]) * mixed[at, cols].astype(f32)).astype(bf16)
            mixed[at, cols] = du
            small[5:6, cols] += jnp.sum(du.astype(f32), axis=0, keepdims=True)
        da = dot_nt(mixed[at, :hidden], w1_v[...])
        da_all[at] = da.astype(bf16)
        xhat, _ = row_stats(x_all[at].astype(f32))
        small[2:3] += jnp.sum(da * xhat, axis=0, keepdims=True)
        small[3:4] += jnp.sum(da, axis=0, keepdims=True)
        small[4:5] += jnp.sum(dy.astype(f32), axis=0, keepdims=True)
        move(tiles + hidden // TILE + i)

        @pl.when((lax.rem(i, jnp.int32(2)) == 0) & (i > 0) & (lax.div(i, jnp.int32(2)) <= lead))
        def _():
            advance(*sums[0], lax.div(i, jnp.int32(2)) - 1, stop)

        return 0

    lax.fori_loop(0, tiles, mlp_backward, 0)
    for c in deal_da2:
        c.start()

    members = find_members(group_ref, me_dp)
    offs = [offsets[m] for m in members]
    for m, member in enumerate(members):
        where = ring_spot(lax.div(member, jnp.int32(conts)), n_dp)
        slot = lax.rem(member, jnp.int32(conts))
        for a in range(2):
            moved[me_t, a, m] = ring[where, a, slot]
    over_y = [
        remote(moved.at[me_t], moved.at[me_t], y_send.at[k], y_recv.at[k], {"tensor": p})
        for k, p in enumerate(peers)
    ]
    over_core = [
        remote(
            moved.at[2 * j + core], moved.at[2 * j + core], core_send.at[j], core_recv.at[j], {"tensor": sibling}
        )
        for j in range(lines)
    ]
    for c in over_y:
        c.start()

    def up_tile(k, _):
        cols = span(k * TILE, TILE, TILE)
        put_tile(sum1, k, dot_tn(h_all[:, cols], mixed[:, :hidden]), width, n_dp)
        return 0

    lax.fori_loop(0, width // TILE, up_tile, 0)
    sums[1][0].start(jnp.int32(0))

    for c in loads[6:]:
        c.wait()
    for m, off in enumerate(offs):
        for a in range(3):
            tab[a, table_len + m * CONT_LEN : table_len + (m + 1) * CONT_LEN, :] = tab[a, pl.ds(off, CONT_LEN), :]
    gain, shift = as_row(gain_one_ref), as_row(shift_one_ref)
    lane = lax.broadcasted_iota(jnp.int32, (1, CHUNK), 1)
    bias = as_row(bias_qkv_ref)
    biases = []
    for pair in range(heads // 2):
        chunks = [slice((3 * pair + c) * CHUNK, (3 * pair + c + 1) * CHUNK) for c in range(3)]
        biases += pair_columns(*(bias[:, cols] for cols in chunks), lane)
        for cols, value in zip(chunks, pair_columns(*(wqkv_v[:, cols] for cols in chunks), lane)):
            wqkv_v[:, cols] = value

    def turned(z, start, sign):
        cos, low, high = (tab[a, pl.ds(start, TILE), :] for a in range(3))
        half = ROT // 2
        return z * cos + (pltpu.roll(z, CHUNK - half, 1) * low + pltpu.roll(z, half, 1) * high) * sign

    def table_start(i):
        return pl.multiple_of(i * TILE + lax.div(i, jnp.int32(prompt_tiles)) * (table_len - prompt_len), CHUNK)

    def project(i):
        at = span(i * TILE, TILE, TILE)
        source = span(i * TILE + cont_total, TILE, TILE)
        xhat, _ = row_stats(x_all[source].astype(f32))
        h = (xhat * gain + shift).astype(bf16)
        h_all[at] = h
        do = dot_nt(dy_all[source], wd_v[...]).astype(bf16)
        for pair in range(heads // 2):
            q, k, v = (
                dot(h, wqkv_v[:, c * CHUNK : (c + 1) * CHUNK]) + biases[c] for c in range(3 * pair, 3 * pair + 3)
            )
            q = turned(q, table_start(i), 1.0)
            qs[2 * pair, at] = jnp.where(lane < HD, q, 0.0).astype(bf16)
            qs[2 * pair + 1, at] = jnp.where(lane < HD, 0.0, q).astype(bf16)
            k = turned(k, table_start(i), 1.0)
            ks[pair, at] = k.astype(bf16)
            k_turned[pair, :, at] = k.T.astype(bf16)
            vs[pair, at] = v.astype(bf16)
            v_turned[pair, :, at] = v.T.astype(bf16)
            both = do[:, pair * CHUNK : (pair + 1) * CHUNK].astype(f32)
            dos[2 * pair, at] = jnp.where(lane < HD, both, 0.0).astype(bf16)
            dos[2 * pair + 1, at] = jnp.where(lane < HD, 0.0, both).astype(bf16)

    def project_prompt(i, _):
        project(i)
        turn_evenly(0, i, prompt_tiles, project_turns)
        return 0

    lax.fori_loop(0, prompt_tiles, project_prompt, 0)
    for c in over_y:
        c.wait()
    for c in over_core:
        c.start()

    query_lane = lax.broadcasted_iota(jnp.int32, (1, TILE), 1)
    reach = jnp.zeros((1, TILE), jnp.int32)
    for m, off in enumerate(offs):
        reach = jnp.where(lax.div(query_lane, jnp.int32(CONT_LEN)) == m, off, reach)

    def attend(pair, _):
        for block in list(range(prompt_tiles - 1, -1, -1)) + [prompt_tiles]:
            first = block * TILE
            seen = first + TILE
            at = slice(first, seen)
            if block == prompt_tiles:
                @pl.when(pair == 0)
                def _():
                    for c in over_core:
                        c.wait()
                    for q in range(n_tensor):
                        for s in range(conts):
                            to = rows + s * CONT_LEN + q * piece
                            x_all[to : to + piece, :] = moved[q, 0, s]
                            dy_all[to : to + piece, :] = moved[q, 1, s]
                    project(jnp.int32(prompt_tiles))

            k, v = ks[pair, :seen], vs[pair, :seen]
            key = lax.broadcasted_iota(jnp.int32, (TILE, TILE), 0)
            query = lax.broadcasted_iota(jnp.int32, (TILE, TILE), 1)
            seen_near = key <= query
            if block == prompt_tiles:
                key_row = lax.broadcasted_iota(jnp.int32, (prompt_len, TILE), 0)
                same = lax.div(key, jnp.int32(CONT_LEN)) == lax.div(query, jnp.int32(CONT_LEN))
                seen_near = seen_near & same
            heads_now = (2 * pair, 2 * pair + 1)
            scores = [dot_nt(k, qs[h, at]) * scale for h in heads_now]
            dprobs = [dot_nt(v, dos[h, at]) for h in heads_now]
            lows, low_slopes, o_turned, dq_turned = [], [], [], []
            for sub in range(2):
                s, dprob = scores[sub], dprobs[sub]
                near = jnp.where(seen_near, s[first:], masked_value)
                if block == prompt_tiles:
                    s = jnp.concatenate([jnp.where(key_row < reach, s[:first], masked_value), near], axis=0)
                else:
                    s = near if first == 0 else jnp.concatenate([s[:first], near], axis=0)
                p = jnp.exp(s - jnp.max(s, axis=0, keepdims=True))
                p = p * (1.0 / jnp.sum(p, axis=0, keepdims=True))
                low = p.astype(bf16)
                delta = jnp.sum(p * dprob, axis=0, keepdims=True)
                ds = (p * (dprob - delta)).astype(bf16)
                part = slice(sub * HD, (sub + 1) * HD)
                o_turned.append(dot(v_turned[pair, part, :seen], low))
                dq_turned.append(dot(k_turned[pair, part, :seen], ds))
                lows.append(low)
                low_slopes.append(ds)
            o_all[at, span(pair * CHUNK, CHUNK, CHUNK)] = jnp.concatenate(o_turned, axis=0).T.astype(bf16)
            dq = jnp.concatenate(dq_turned, axis=0).T * scale
            dq = turned(dq, table_start(jnp.int32(block)), -1.0).astype(bf16)
            cols = span(3 * pair * CHUNK, CHUNK, CHUNK)
            mixed[at, cols] = dq
            small[6:7, cols] += jnp.sum(dq.astype(f32), axis=0, keepdims=True)
            q_both = jnp.concatenate([qs[h, at] for h in heads_now], axis=0)
            do_both = jnp.concatenate([dos[h, at] for h in heads_now], axis=0)
            dk = dot(jnp.concatenate(low_slopes, axis=1), q_both)
            dv = dot(jnp.concatenate(lows, axis=1), do_both)
            if block == prompt_tiles - 1:
                dks[:seen] = dk
                dvs[:seen] = dv
            else:
                old = min(seen, prompt_len)
                dks[:old] += dk[:old]
                dvs[:old] += dv[:old]
                if old < seen:
                    dks[old:seen] = dk[old:]
                    dvs[old:seen] = dv[old:]
            turn_block(pair, prompt_tiles - 1 - block if block < prompt_tiles else block)

        for i in range(tiles):
            at = slice(i * TILE, (i + 1) * TILE)
            dk = turned(dks[at] * scale, table_start(jnp.int32(i)), -1.0).astype(bf16)
            for c, value in ((1, dk), (2, dvs[at].astype(bf16))):
                cols = span((3 * pair + c) * CHUNK, CHUNK, CHUNK)
                mixed[at, cols] = value
                small[6:7, cols] += jnp.sum(value.astype(f32), axis=0, keepdims=True)
        turn_block(pair, 5)
        return 0

    lax.fori_loop(0, heads // 2, attend, 0)
    for c in deal_da2:
        c.wait()

    def back(i, _):
        at = span(i * TILE, TILE, TILE)
        da = dot_nt(mixed[at, : 3 * local], wqkv_v[...])
        da_all[at] = da.astype(bf16)
        xhat, _ = row_stats(x_all[span(i * TILE + cont_total, TILE, TILE)].astype(f32))
        small[0:1] += jnp.sum(da * xhat, axis=0, keepdims=True)
        small[1:2] += jnp.sum(da, axis=0, keepdims=True)

        turn_evenly(back_from, i, tiles, back_turns)
        return 0

    lax.fori_loop(0, tiles, back, 0)
    for c in deal_da1:
        c.start()

    def weight_tile(k, _):
        cols = span(k * TILE, TILE, TILE)
        put_tile(wg, k, dot_tn(h_all[:, cols], mixed[:, : 3 * local]), width, n_dp, slice(0, 3 * local))
        put_tile(wg, k, dot_tn(dy_all[cont_total:, cols], o_all[...]), width, n_dp, slice(3 * local, 4 * local))
        turn_evenly(back_from + back_turns, k, width // TILE, all_turns - back_from - back_turns)
        return 0

    lax.fori_loop(0, width // TILE, weight_tile, 0)
    summing = RingSum(wg, got1, x_send, x_recv, n_dp)
    gathering = RingGather(wg, xg_send, xg_recv, n_dp)
    cont_from = 5
    rest_ticks = 2 * stop - all_turns
    all_ticks = max(stop, rest_ticks, cont_from + n_dp - 1)
    summing.start(jnp.int32(0))

    def home_steps(k):
        ahead = lax.rem(spot - k + n_dp, jnp.int32(n_dp))
        back = lax.rem(spot + k, jnp.int32(n_dp))
        return (
            remote(ring.at[ahead, 0], ring.at[ahead, 0], home_send.at[0, k], home_recv.at[0, k], {"dp": after}),
            remote(ring.at[back, 1], ring.at[back, 1], home_send.at[1, k], home_recv.at[1, k], {"dp": before}),
            remote(
                small_ring.at[ahead, 0], small_ring.at[ahead, 0], home_send.at[2, k], home_recv.at[2, k], {"dp": after}
            ),
            remote(
                small_ring.at[back, 1], small_ring.at[back, 1], home_send.at[3, k], home_recv.at[3, k], {"dp": before}
            ),
        )

    def run_ticks(begin, end):
        def one(t, _):
            advance(summing, gathering, t, 2 * (n_dp - 1))

            @pl.when(t < rest_ticks)
            def _():
                sum_step(all_turns + t)

            k = t - cont_from

            @pl.when((k >= 0) & (k < n_dp - 1))
            def _():
                for c in home_steps(k):
                    c.wait()

            @pl.when((k >= 0) & (k < n_dp - 2))
            def _():
                for c in home_steps(k + 1):
                    c.start()

            return 0

        lax.fori_loop(begin, end, one, 0)

    line = lax.div(me_t, jnp.int32(2))
    base_one, base_two, base_y = 4 * few, 4 * few + quarter, 4 * few + 2 * quarter
    depth = base_y + quarter
    group_rows = ((0, base_one), (base_one, 2 * quarter), (base_y, quarter))
    room = rows // depth

    def own_part(m, start, size):
        return (h_all, da_all)[m // room].at[pl.ds((m % room) * depth + start, size)]

    def fill(n, m):
        j = lax.rem(line + (m + 1), jnp.int32(lines))
        return pltpu.make_async_copy(
            stack.at[2 * j + core, pl.ds(*group_rows[n])], own_part(m, *group_rows[n]), fill_sem.at[n, m]
        )

    def to_core(n):
        at = pl.ds(*group_rows[n])
        return [
            remote(
                stack.at[2 * j + 1 - core, at], rc.at[j, at], rc_send.at[n, j], rc_recv.at[n, j], {"tensor": sibling}
            )
            for j in range(lines)
        ]

    def to_line(n):
        return [
            remote(
                own_part(k, *group_rows[n]), ry.at[k, pl.ds(*group_rows[n])], ry_send.at[n, k], ry_recv.at[n, k],
                {"tensor": p},
            )
            for k, p in enumerate(peers)
        ]

    def pass_on(n):
        for c in to_core(n):
            c.wait()
        for k in range(lines - 1):
            j = lax.rem(line + (k + 1), jnp.int32(lines))
            mine = own_part(k, *group_rows[n])
            mine[...] = (mine[...].astype(f32) + rc[j, pl.ds(*group_rows[n])].astype(f32)).astype(bf16)
        for c in to_line(n):
            c.start()

    small_to_core = remote(small, small_core, sc_send, sc_recv, {"tensor": sibling})
    small_to_core.start()
    for c in deal_da1:
        c.wait()
    for c in to_core(1):
        c.start()

    def y_tile(i, _):
        at = span(i * TILE, TILE, TILE)
        total = dot(o_all[at], wd_v[...]) + dot(g_all[span(i * TILE + cont_total, TILE, TILE)], w2_v[...])
        da_all[at] = total.astype(bf16)
        return 0

    lax.fori_loop(0, prompt_tiles, y_tile, 0)
    da_all[prompt_len:] = dot(o_all[prompt_len:], wd_v[...]).astype(bf16)
    y_home[...] = dot(g_all[:cont_total], w2_v[...]).astype(bf16)
    for c in deal_y + deal_home:
        c.start()
    run_ticks(0, 1)
    for c in deal_y + deal_home:
        c.wait()
    for n in (0, 2):
        for c in to_core(n):
            c.start()
    fills = [fill(n, m) for n in (0, 1, 2) for m in range(lines)]
    for c in fills:
        c.start()
    small_to_core.wait()
    row = lax.broadcasted_iota(jnp.int32, (8, 1), 0)
    small_y[line] = small[...] + jnp.where(row < 4, small_core[...], 0.0)
    small_to_line = [
        remote(small_y.at[line], small_y.at[line], sy_send.at[k], sy_recv.at[k], {"tensor": p})
        for k, p in enumerate(peers)
    ]
    for c in small_to_line:
        c.start()
    for c in fills:
        c.wait()
    pass_on(0)
    run_ticks(1, 2)
    pass_on(1)
    pass_on(2)
    for c in small_to_line:
        c.wait()
    reduced = small_y[0]
    for j in range(1, lines):
        reduced = reduced + small_y[j]
    reduced = jnp.where(row < 4, reduced, small[...]).astype(bf16)
    fold = width // 4
    for part in range(4):
        small_ring[spot, part // 2, part % 2 * 8 : part % 2 * 8 + 8] = reduced[:, part * fold : (part + 1) * fold]
    run_ticks(2, cont_from)

    def summed(start, size):
        total = own_part(lines - 1, start, size)[...].astype(f32) + rc[line, pl.ds(start, size)].astype(f32)
        for k in range(lines - 1):
            total = total + ry[k, pl.ds(start, size)].astype(f32)
        return total

    def quarter_rows(q):
        return pl.ds(pl.multiple_of(q * quarter, 16), quarter)

    gain_two = as_row(gain_two_ref)
    both = as_row(bias_one_ref) + as_row(bias_two_ref)
    results = (out_p, grad_p)

    def gather_line(a):
        at = quarter_rows(me_t)
        return [pltpu.make_async_copy(own_rows.at[a], results[a].at[at], rows_sem.at[a])] + [
            remote(own_rows.at[a], results[a].at[at], gl_send.at[a, k], gl_recv.at[a, k], {"tensor": p})
            for k, p in enumerate(peers)
        ]

    def to_sibling(a):
        at = quarter_rows(me_t)
        return [remote(own_rows.at[a], results[a].at[at], gc_send.at[a, 0], gc_recv.at[a, 0], {"tensor": sibling})]

    def gather_core(a):
        copies = []
        for k in range(1, lines):
            at = quarter_rows(2 * lax.rem(line + k, jnp.int32(lines)) + core)
            copies.append(
                remote(results[a].at[at], results[a].at[at], gc_send.at[a, k], gc_recv.at[a, k], {"tensor": sibling})
            )
        return copies

    for c in to_line(0):
        c.wait()
    for s in range(conts):
        ring[spot, 0, s] = summed(s * piece, piece).astype(bf16)
        theirs = x_all[span(rows + s * CONT_LEN + me_t * piece, piece, 16)].astype(f32)
        ring[spot, 1, s] = norm_pull(theirs, summed(2 * few + s * piece, piece) * gain).astype(bf16)
        home = span(s * CONT_LEN + me_t * piece, piece, 16)
        x_home = x_all[home].astype(f32)
        keep_y[s] = x_home + summed(few + s * piece, piece) + both
        pulled = norm_pull(x_home, summed(3 * few + s * piece, piece) * gain_two)
        keep_d[s] = dy_all[home].astype(f32) + pulled
    for c in home_steps(jnp.int32(0)):
        c.start()
    run_ticks(cont_from, cont_from + 3)
    quarter_at = span(cont_total + me_t * quarter, quarter, 16)
    for c in to_line(1):
        c.wait()
    e = summed(base_one, quarter) * gain + summed(base_two, quarter) * gain_two
    own_rows[1] = (dy_all[quarter_at].astype(f32) + norm_pull(x_all[quarter_at].astype(f32), e)).astype(bf16)
    for c in gather_line(1) + to_sibling(1):
        c.start()
    run_ticks(cont_from + 3, cont_from + 5)
    for c in to_line(2):
        c.wait()
    own_rows[0] = (x_all[quarter_at].astype(f32) + summed(base_y, quarter) + both).astype(bf16)
    for c in gather_line(0) + to_sibling(0):
        c.start()
    moved_home = cont_from + n_dp - 1
    run_ticks(cont_from + 5, moved_home)
    for part in range(4):
        at = slice(part % 2 * 8, part % 2 * 8 + 8)
        total = small_ring[0, part // 2, at].astype(f32)
        for j in range(1, n_dp):
            total = total + small_ring[j, part // 2, at].astype(f32)
        vec_out[:, part * fold : (part + 1) * fold] = total
    for s in range(conts):
        mine = me_dp * conts + s
        group = group_ref[mine]
        first, _ = find_members(group_ref, group)
        slot = jnp.where(first == mine, jnp.int32(0), jnp.int32(1))
        where = ring_spot(group, n_dp)
        fin[me_t, 0, s] = (keep_y[s] + ring[where, 0, slot].astype(f32)).astype(bf16)
        fin[me_t, 1, s] = (keep_d[s] + ring[where, 1, slot].astype(f32)).astype(bf16)
    fin_line = [
        remote(fin.at[me_t], fin.at[me_t], fin_send.at[k], fin_recv.at[k], {"tensor": p})
        for k, p in enumerate(peers)
    ]
    fin_core = [
        remote(
            fin.at[2 * j + core], fin.at[2 * j + core], finc_send.at[j], finc_recv.at[j], {"tensor": sibling}
        )
        for j in range(lines)
    ]
    for c in fin_line:
        c.start()
    for c in gather_line(1):
        c.wait()
    for c in gather_core(1):
        c.start()
    run_ticks(moved_home, moved_home + 2)
    for c in gather_line(0):
        c.wait()
    for c in gather_core(0):
        c.start()
    if rest_ticks <= moved_home + 2:
        for c in outs[:2]:
            c.start()
    run_ticks(moved_home + 2, max(moved_home + 2, all_ticks))
    for c in outs if rest_ticks > moved_home + 2 else outs[2:]:
        c.start()
    for c in fin_line:
        c.wait()
    for c in fin_core:
        c.start()
    for c in gather_core(0) + to_sibling(0) + gather_core(1) + to_sibling(1) + fin_core:
        c.wait()
    last = [
        pltpu.make_async_copy(
            fin.at[q, a, s], dst.at[pl.ds(s * CONT_LEN + q * piece, piece)], outc_sem.at[a, q, s]
        )
        for a, dst in ((0, out_c), (1, grad_c))
        for q in range(n_tensor)
        for s in range(conts)
    ]
    for c in last:
        c.start()
    for c in last + outs:
        c.wait()


def run_layer(n_dp, n_tensor, early, group_of, offsets, xp, xc, dp, dc, w1, w2, wqkv, wd, *vectors):
    prompt_len, width = xp.shape
    cont_total = xc.shape[0]
    rows = prompt_len + cont_total
    hidden = w1.shape[1]
    local = wd.shape[0]
    heads = local // HD
    piece = CONT_LEN // n_tensor
    lines = n_tensor // 2
    table = jnp.asarray(rotary_table(prompt_len + CONT_LEN))
    table_rows = table.shape[1] + MEMBERS * CONT_LEN
    up, down = ring_shape(width, hidden, n_dp), ring_shape(hidden, width, n_dp)
    third = ring_shape(width, 4 * local, n_dp)
    quarter = prompt_len // n_tensor
    depth = 4 * MEMBERS * piece + 3 * quarter
    shape = jax.ShapeDtypeStruct
    hbm = pl.BlockSpec(memory_space=pl.ANY)
    vmem = pl.BlockSpec(memory_space=pltpu.VMEM)
    smem = pl.BlockSpec(memory_space=pltpu.SMEM)
    sem = pltpu.SemaphoreType.DMA
    return pl.pallas_call(
        functools.partial(layer_kernel, n_dp, n_tensor, early),
        out_shape=(
            shape(xp.shape, bf16),
            shape(xc.shape, bf16),
            shape(xp.shape, bf16),
            shape(xc.shape, bf16),
            shape(up, bf16),
            shape(down, bf16),
            shape(third, bf16),
            shape((n_tensor, depth, width), bf16),
            shape((8, width), f32),
        ),
        in_specs=[smem] * 2 + [hbm] * 9 + [vmem] * 8,
        out_specs=(hbm,) * 8 + (vmem,),
        scratch_shapes=[
            pltpu.VMEM((rows + cont_total, width), bf16),
            pltpu.VMEM((rows + cont_total, width), bf16),
            pltpu.VMEM((width, hidden), bf16),
            pltpu.VMEM((hidden, width), bf16),
            pltpu.VMEM((width, 3 * local), bf16),
            pltpu.VMEM((local, width), bf16),
            pltpu.VMEM((3, table_rows, CHUNK), f32),
            pltpu.VMEM((rows, width), bf16),
            pltpu.VMEM((rows, hidden), bf16),
            pltpu.VMEM((rows, max(hidden, 3 * local)), bf16),
            pltpu.VMEM((rows, width), bf16),
            pltpu.VMEM((n_dp, 2, MEMBERS, piece, width), bf16),
            pltpu.VMEM((n_tensor, 2, MEMBERS, piece, width), bf16),
            pltpu.VMEM(up, bf16),
            pltpu.VMEM(down, bf16),
            pltpu.VMEM((n_dp - 1,) + up[1:], bf16),
            pltpu.VMEM((n_dp - 1,) + down[1:], bf16),
            pltpu.VMEM(third, bf16),
        ]
        + [pltpu.VMEM((heads, rows, CHUNK), bf16)] * 2
        + [pltpu.VMEM((heads // 2, rows, CHUNK), bf16)] * 2
        + [pltpu.VMEM((heads // 2, CHUNK, rows), bf16)] * 2
        + [pltpu.VMEM((rows, CHUNK), f32)] * 2
        + [
            pltpu.VMEM((rows, local), bf16),
            pltpu.VMEM((cont_total, width), bf16),
            pltpu.VMEM((lines, depth, width), bf16),
            pltpu.VMEM((lines - 1, depth, width), bf16),
            pltpu.VMEM((2, quarter, width), bf16),
            pltpu.VMEM((MEMBERS, piece, width), f32),
            pltpu.VMEM((MEMBERS, piece, width), f32),
            pltpu.VMEM((n_tensor, 2, MEMBERS, piece, width), bf16),
            pltpu.VMEM((8, width), f32),
            pltpu.VMEM((8, width), f32),
            pltpu.VMEM((lines, 8, width), f32),
            pltpu.VMEM((n_dp, 2, 16, width // 4), bf16),
            sem((2, MEMBERS)),
            sem((9,)),
            sem((3,)),
            sem((3, n_tensor, MEMBERS + 1)),
            sem((n_tensor, MEMBERS)),
            sem((MEMBERS, 2, 2, n_dp - 1)),
            sem((MEMBERS, 2, 2, n_dp - 1)),
            sem((lines - 1,)),
            sem((lines - 1,)),
            sem((lines,)),
            sem((lines,)),
        ]
        + [sem((2, 2, n_dp - 1))] * 4
        + [sem((3, lines))] * 3
        + [sem((3, lines - 1))] * 2
        + [sem((2, lines - 1))] * 2
        + [sem((2, lines))] * 2
        + [sem((4, n_dp - 1))] * 2
        + [sem] * 2
        + [sem((lines - 1,))] * 4
        + [sem((lines,))] * 2
        + [sem((2,)), sem((2, n_tensor, MEMBERS))]
        + [sem((2, n_dp - 1))] * 4,
        compiler_params=pltpu.CompilerParams(
            collective_id=0, has_side_effects=True, vmem_limit_bytes=63 * 2**20
        ),
        cost_estimate=pl.CostEstimate(flops=34 * 10**9, bytes_accessed=40 * 10**6, transcendentals=5 * 10**6),
        name="layer",
    )(group_of, offsets, xp, xc, dp, dc, w1, w2, wqkv, wd, table, *vectors)


def finish_kernel(
    groups, out_p, out_c, grad_p, grad_c, w1s, w2s, wg, total,
    out_p_out, out_c_out, grad_p_out, grad_c_out, gain_one, shift_one, gain_two, shift_two,
    qkv_out, qkv_bias, dense_out, dense_bias, w1_out, w1_bias, w2_out, w2_bias,
    out_p_v, out_c_v, grad_p_v, grad_c_v, w1s_v, w2s_v, wg_v, qkv_v, dense_v, w1_v, w2_v,
    copy_in, copy_out, piece_in, piece_out, dense_sem,
):
    local3 = qkv_out.shape[1]
    plain = (
        (out_p, out_p_v, out_p_out), (grad_p, grad_p_v, grad_p_out),
        (out_c, out_c_v, out_c_out), (grad_c, grad_c_v, grad_c_out),
    )
    plain_in = [pltpu.make_async_copy(a, b, copy_in.at[i]) for i, (a, b, _) in enumerate(plain)]
    plain_out = [pltpu.make_async_copy(b, c, copy_out.at[i]) for i, (_, b, c) in enumerate(plain)]
    weights = ((w1s, w1s_v, w1_v, w1_out), (w2s, w2s_v, w2_v, w2_out), (wg, wg_v, qkv_v, qkv_out))

    def chunks_of(a, g):
        return pl.ds(g * (a.shape[0] // groups), a.shape[0] // groups)

    def rows_of(a, g):
        return pl.ds(g * (a.shape[0] // groups), a.shape[0] // groups)

    loads = [
        [pltpu.make_async_copy(a.at[chunks_of(a, g)], b.at[chunks_of(a, g)], piece_in.at[i, g]) for g in range(groups)]
        for i, (a, b, _, _) in enumerate(weights)
    ]
    stores = [
        [pltpu.make_async_copy(c.at[rows_of(c, g)], d.at[rows_of(c, g)], piece_out.at[i, g]) for g in range(groups)]
        for i, (_, _, c, d) in enumerate(weights)
    ]
    for c in plain_in[:1] + loads[0] + plain_in[1:2] + loads[1] + plain_in[2:] + loads[2]:
        c.start()
    lane = lax.broadcasted_iota(jnp.int32, (1, CHUNK), 1)
    pairs = [
        [slice((3 * pair + c) * CHUNK, (3 * pair + c + 1) * CHUNK) for c in range(3)]
        for pair in range(local3 // (3 * CHUNK))
    ]
    for n, dst in enumerate((gain_one, shift_one, gain_two, shift_two, dense_bias, w1_bias)):
        dst[...] = total[n, : dst.shape[0]]
    w2_bias[...] = total[4, :]
    for columns in pairs:
        for cols, value in zip(columns, unpair_columns(*(total[6:7, cols] for cols in columns), lane)):
            qkv_bias[cols] = value[0]

    def pieces(src, dst, g):
        per_group = src.shape[0] // groups
        size = dst.shape[0] // (2 * src.shape[0])
        for p in range(2 * per_group):
            first = g * (dst.shape[0] // groups) + p * size
            yield g * per_group + p // 2, p % 2, size, slice(first, first + size)

    for i in range(2):
        plain_in[i].wait()
        plain_out[i].start()
        _, src, dst, _ = weights[i]
        for g in range(groups):
            loads[i][g].wait()
            for chunk, way, size, to in pieces(src, dst, g):
                dst[to, :] = src[chunk, way, :size].astype(f32)
            stores[i][g].start()
    for i in (2, 3):
        plain_in[i].wait()
        plain_out[i].start()
    for g in range(groups):
        loads[2][g].wait()
        dense = []
        for chunk, way, size, to in pieces(wg_v, qkv_v, g):
            for columns in pairs:
                parts = unpair_columns(*(wg_v[chunk, way, :size, cols].astype(f32) for cols in columns), lane)
                for cols, value in zip(columns, parts):
                    qkv_v[to, cols] = value
            dense.append(wg_v[chunk, way, :size, local3:].astype(f32))
        stores[2][g].start()
        size = dense_v.shape[1] // groups
        dense_v[:, g * size : (g + 1) * size] = jnp.concatenate(dense, axis=0).T
    last = pltpu.make_async_copy(dense_v, dense_out, dense_sem)
    last.start()
    for c in plain_out + stores[0] + stores[1] + stores[2] + [last]:
        c.wait()


def run_finish(local3, hidden, out_p, out_c, grad_p, grad_c, w1s, w2s, wg, total):
    width = out_p.shape[1]
    local = local3 // 3
    groups = 4
    shape = jax.ShapeDtypeStruct
    hbm = pl.BlockSpec(memory_space=pl.ANY)
    vmem = pl.BlockSpec(memory_space=pltpu.VMEM)
    sem = pltpu.SemaphoreType.DMA
    moved = (out_p, out_c, grad_p, grad_c)
    return pl.pallas_call(
        functools.partial(finish_kernel, groups),
        out_shape=tuple(shape(a.shape, bf16) for a in moved)
        + (shape((width,), f32),) * 4
        + (
            shape((width, local3), f32), shape((local3,), f32),
            shape((local, width), f32), shape((width,), f32),
            shape((width, hidden), f32), shape((hidden,), f32),
            shape((hidden, width), f32), shape((width,), f32),
        ),
        in_specs=[hbm] * 7 + [vmem],
        out_specs=(hbm,) * 4 + (vmem,) * 4 + (hbm, vmem) * 4,
        scratch_shapes=[pltpu.VMEM(a.shape, bf16) for a in moved + (w1s, w2s, wg)]
        + [
            pltpu.VMEM((width, local3), f32),
            pltpu.VMEM((local, width), f32),
            pltpu.VMEM((width, hidden), f32),
            pltpu.VMEM((hidden, width), f32),
            sem((4,)),
            sem((4,)),
            sem((3, groups)),
            sem((3, groups)),
            sem,
        ],
        compiler_params=pltpu.CompilerParams(vmem_limit_bytes=60 * 2**20),
        name="finish",
    )(out_p, out_c, grad_p, grad_c, w1s, w2s, wg, total)


def per_device(
    n_dp, n_tensor,
    prompt_in, cont_in, prompt_cot, cont_cot, group_of, offsets, ln1_gain, ln1_bias, ln2_gain, ln2_bias,
    qkv_weight, qkv_bias, dense_weight, dense_bias, fc1_weight, fc1_bias, fc2_weight, fc2_bias,
):
    width = prompt_in.shape[1]
    hidden = fc1_weight.shape[1]
    local3 = qkv_weight.shape[1]

    out_p, out_c, grad_p, grad_c, w1g, w2g, wg, _, total = run_layer(
        n_dp, n_tensor, min(n_dp - 1, 2), group_of, offsets, prompt_in, cont_in, prompt_cot, cont_cot,
        fc1_weight, fc2_weight, qkv_weight, dense_weight,
        ln2_gain, ln2_bias, fc1_bias, ln1_gain, ln1_bias, qkv_bias, dense_bias, fc2_bias,
    )
    return run_finish(local3, hidden, out_p, out_c, grad_p, grad_c, w1g, w2g, wg, total)


def solution(mesh):
    rows, whole, columns, segment, depth = P("dp", None), P(), P(None, "tensor"), P("tensor"), P("tensor", None)
    return jax.shard_map(
        functools.partial(per_device, mesh.shape["dp"], mesh.shape["tensor"]),
        mesh=mesh,
        in_specs=(
            rows, rows, rows, rows, whole, whole, whole, whole, whole, whole,
            columns, segment, depth, whole, columns, segment, depth, whole,
        ),
        out_specs=(
            rows, rows, rows, rows, whole, whole, whole, whole,
            columns, segment, depth, whole, columns, segment, depth, whole,
        ),
        check_vma=False,
    )
```

```python
import functools
import math

import jax
import jax.numpy as jnp
import numpy as np
from jax import lax
from jax.experimental import pallas as pl
from jax.experimental.pallas import tpu as pltpu
from jax.sharding import PartitionSpec as P

HD = 64
ROT = 16
CONT_LEN = 128
TILE = 256
CHUNK = 128
MEMBERS = 2

eps_norm = 1e-05
masked_value = -1e30
MESH = pl.DeviceIdType.MESH
bf16 = jnp.bfloat16
f32 = jnp.float32


def dot(a, b):
    return jnp.dot(a, b, preferred_element_type=f32)


def dot_nt(a, b):
    return lax.dot_general(a, b, (((1,), (1,)), ((), ())), preferred_element_type=f32)


def dot_tn(a, b):
    return lax.dot_general(a, b, (((0,), (0,)), ((), ())), preferred_element_type=f32)


def row_stats(x):
    centered = x - jnp.mean(x, axis=-1, keepdims=True)
    scale = lax.rsqrt(jnp.mean(centered * centered, axis=-1, keepdims=True) + eps_norm)
    return centered * scale, scale


def norm_pull(x, e):
    xhat, scale = row_stats(x)
    return scale * (
        e
        - jnp.mean(e, axis=-1, keepdims=True)
        - xhat * jnp.mean(e * xhat, axis=-1, keepdims=True)
    )


def gelu_and_slope(u):
    t = 1.0 / (1.0 + jnp.abs(u) * (0.3275911 / math.sqrt(2.0)))
    bell = jnp.exp(-0.5 * u * u)
    poly = t * (
        0.127414796
        + t * (-0.142248368 + t * (0.7107068705 + t * (-0.7265760135 + t * 0.5307027145)))
    )
    tail = poly * bell
    cdf = jnp.where(u >= 0, 1.0 - tail, tail)
    return u * cdf, cdf + u * bell * (1.0 / math.sqrt(2.0 * math.pi))


def rotary_table(length):
    half = ROT // 2
    frequencies = np.exp(
        -np.arange(half, dtype=np.float32) * np.float32(2.0 * math.log(10000.0) / ROT)
    ).astype(np.float32)
    angles = np.arange(length, dtype=np.float32)[:, None] * frequencies[None, :]
    angles = np.concatenate([angles, angles], axis=1).astype(np.float32)
    cos = np.ones((length, HD), np.float32)
    low = np.zeros((length, HD), np.float32)
    high = np.zeros((length, HD), np.float32)
    cos[:, :ROT] = np.cos(angles)
    low[:, :half] = -np.sin(angles)[:, :half]
    high[:, half:ROT] = np.sin(angles)[:, half:]
    return np.stack([np.concatenate([t, t], axis=1) for t in (cos, low, high)])


def ring_spot(device, n):
    odd = lax.rem(device, jnp.int32(2))
    half = lax.div(device, jnp.int32(2))
    return (1 - odd) * half + odd * (n - 1 - half)


def ring_device(spot, n):
    far = lax.div(spot, jnp.int32(n // 2))
    return (1 - far) * (2 * spot) + far * (2 * (n - 1 - spot) + 1)


def ring_neighbours(n):
    spot = ring_spot(lax.axis_index("dp"), n)
    after = ring_device(lax.rem(spot + 1, jnp.int32(n)), n)
    before = ring_device(lax.rem(spot + n - 1, jnp.int32(n)), n)
    return spot, after, before


def find_members(group_ref, wanted):
    count = group_ref.shape[0]
    first = jnp.int32(count)
    last = jnp.int32(-1)
    for j in range(count):
        hit = group_ref[j] == wanted
        first = jnp.minimum(first, jnp.where(hit, jnp.int32(j), jnp.int32(count)))
        last = jnp.maximum(last, jnp.where(hit, jnp.int32(j), jnp.int32(-1)))
    return jnp.minimum(first, count - 1), jnp.maximum(last, 0)


def remote(src, dst, send, recv, device):
    return pltpu.make_async_remote_copy(
        src_ref=src, dst_ref=dst, send_sem=send, recv_sem=recv, device_id=device, device_id_type=MESH
    )


def as_row(ref):
    return ref[...].astype(f32).reshape(1, ref.shape[0])


def span(start, size, step):
    return pl.ds(pl.multiple_of(start, step), size)


def piece_rows(rows, n):
    return rows // (2 * n), max(16, rows // (2 * n))


def ring_shape(rows, width, n):
    return (n, 2, piece_rows(rows, n)[1], width)


def put_tile(buffer, k, value, rows, n, cols=slice(None)):
    size = piece_rows(rows, n)[0]
    pieces = TILE // size
    for p in range(pieces):
        buffer[k * (pieces // 2) + p // 2, p % 2, :size, cols] = value[p * size : (p + 1) * size].astype(bf16)


def pair_columns(c0, c1, c2, lane):
    low = lane < HD
    crossed = jnp.where(low, c2, c0)
    return jnp.where(low, c0, c1), pltpu.roll(crossed, HD, 1), jnp.where(low, c1, c2)


def unpair_columns(q, k, v, lane):
    low = lane < HD
    crossed = pltpu.roll(k, HD, 1)
    return jnp.where(low, q, crossed), jnp.where(low, v, q), jnp.where(low, crossed, v)


class RingSum:
    def __init__(self, buffer, arrived, send, recv, n):
        self.buffer, self.arrived, self.send, self.recv, self.n = buffer, arrived, send, recv, n
        self.spot, self.after, self.before = ring_neighbours(n)

    def copies(self, k):
        n = self.n
        ahead = lax.rem(self.spot + (2 * n - 1) - k, jnp.int32(n))
        back = lax.rem(self.spot + 1 + k, jnp.int32(n))
        return [
            remote(
                self.buffer.at[chunk, way], self.arrived.at[k, way], self.send.at[way, k], self.recv.at[way, k],
                {"dp": device},
            )
            for way, (chunk, device) in enumerate(((ahead, self.after), (back, self.before)))
        ]

    def start(self, k):
        for c in self.copies(k):
            c.start()

    def finish(self, k):
        n = self.n
        for c in self.copies(k):
            c.wait()
        for way, chunk in enumerate(
            (lax.rem(self.spot + (2 * n - 2) - k, jnp.int32(n)), lax.rem(self.spot + 2 + k, jnp.int32(n)))
        ):
            self.buffer[chunk, way] += self.arrived[k, way]


class RingGather:
    def __init__(self, buffer, send, recv, n, part=()):
        self.buffer, self.send, self.recv, self.n, self.part = buffer, send, recv, n, part
        self.spot, self.after, self.before = ring_neighbours(n)

    def copies(self, k):
        n = self.n
        ahead = lax.rem(self.spot + n - k, jnp.int32(n))
        back = lax.rem(self.spot + k, jnp.int32(n))
        return [
            remote(
                self.buffer.at[(chunk, way) + self.part], self.buffer.at[(chunk, way) + self.part],
                self.send.at[way, k], self.recv.at[way, k], {"dp": device},
            )
            for way, (chunk, device) in enumerate(((ahead, self.after), (back, self.before)))
        ]

    def start(self, k):
        for c in self.copies(k):
            c.start()

    def finish(self, k):
        for c in self.copies(k):
            c.wait()


def advance(summing, gathering, t, stop):
    n = summing.n

    @pl.when(t < n - 1)
    def _():
        summing.finish(t)

    @pl.when(t < n - 2)
    def _():
        summing.start(t + 1)

    @pl.when((t == n - 2) & (stop > n - 1))
    def _():
        gathering.start(jnp.int32(0))

    @pl.when((t >= n - 1) & (t < stop))
    def _():
        gathering.finish(t - (n - 1))

    @pl.when((t >= n - 1) & (t < stop - 1))
    def _():
        gathering.start(t - (n - 2))


def layer_kernel(
    n_dp, n_tensor, early, group_ref, offsets, xp, xc, dp, dc, w1, w2, wqkv, wd, table,
    gain_two_ref, shift_two_ref, bias1_ref, gain_one_ref, shift_one_ref, bias_qkv_ref, bias_one_ref, bias_two_ref,
    out_p, out_c, grad_p, grad_c, w1s_out, w2s_out, wg_out, stack, vec_out,
    x_all, dy_all, w1_v, w2_v, wqkv_v, wd_v, tab, h_all, g_all, mixed, da_all, ring, moved,
    sum1, sum2, got1, got2, wg, qs, dos, ks, vs, k_turned, v_turned, dks, dvs, o_all, y_home,
    rc, ry, own_rows, keep_y, keep_d, fin, small, small_core, small_y, small_ring,
    own_sem, load_sem, out_sem, part_sem, home_sem, ring_send, ring_recv, y_send, y_recv, core_send, core_recv,
    rs_send, rs_recv, ag_send, ag_recv,
    fill_sem, rc_send, rc_recv, ry_send, ry_recv, gl_send, gl_recv, gc_send, gc_recv,
    home_send, home_recv, sc_send, sc_recv, sy_send, sy_recv, fin_send, fin_recv, finc_send, finc_recv,
    rows_sem, outc_sem, x_send, x_recv, xg_send, xg_recv,
):
    prompt_len, width = xp.shape
    cont_total = xc.shape[0]
    conts = MEMBERS
    rows = prompt_len + cont_total
    tiles = rows // TILE
    prompt_tiles = prompt_len // TILE
    hidden = w1.shape[1]
    local = wd.shape[0]
    heads = local // HD
    piece = CONT_LEN // n_tensor
    lines = n_tensor // 2
    table_len = table.shape[1]
    scale = 1.0 / math.sqrt(HD)
    me_dp, me_t = lax.axis_index("dp"), lax.axis_index("tensor")
    core = lax.rem(me_t, jnp.int32(2))
    sibling = me_t + 1 - 2 * core
    peers = [lax.rem(me_t + 2 * k, jnp.int32(n_tensor)) for k in range(1, lines)]
    spot, after, before = ring_neighbours(n_dp)

    own = [
        pltpu.make_async_copy(
            src.at[span(s * CONT_LEN + me_t * piece, piece, 16)], ring.at[spot, a, s], own_sem.at[a, s]
        )
        for a, src in enumerate((xc, dc))
        for s in range(conts)
    ]
    loads = [
        pltpu.make_async_copy(src, dst, load_sem.at[i])
        for i, (src, dst) in enumerate(
            (
                (xc, x_all.at[pl.ds(0, cont_total)]),
                (w1, w1_v),
                (dc, dy_all.at[pl.ds(0, cont_total)]),
                (w2, w2_v),
                (xp, x_all.at[pl.ds(cont_total, prompt_len)]),
                (dp, dy_all.at[pl.ds(cont_total, prompt_len)]),
                (wqkv, wqkv_v),
                (wd, wd_v),
                (table, tab.at[:, pl.ds(0, table_len)]),
            )
        )
    ]
    partners = [{"dp": after}, {"dp": before}, {"tensor": sibling}] + [{"tensor": p} for p in peers]
    barrier = pltpu.get_barrier_semaphore()
    for partner in partners:
        pl.semaphore_signal(barrier, inc=1, device_id=partner, device_id_type=MESH)
    for c in own + [loads[i] for i in (1, 0, 4, 2, 5, 3, 6, 7, 8)]:
        c.start()
    pl.semaphore_wait(barrier, len(partners))

    halves = min(2, piece // 16)
    moving = [
        RingGather(
            ring, ring_send.at[s, b], ring_recv.at[s, b], n_dp, (s, pl.ds(b * (piece // halves), piece // halves))
        )
        for s in range(conts)
        for b in range(halves)
    ]
    for s in range(conts):
        for b in range(halves):
            for way, (src, device) in enumerate(((xc, after), (dc, before))):
                at = span(s * CONT_LEN + me_t * piece + b * (piece // halves), piece // halves, 16)
                part = pl.ds(b * (piece // halves), piece // halves)
                remote(
                    src.at[at], ring.at[spot, way, s, part], ring_send.at[s, b, way, 0], ring_recv.at[s, b, way, 0],
                    {"dp": device},
                ).start()
    sums = [
        (
            RingSum(buffer, got, rs_send.at[i], rs_recv.at[i], n_dp),
            RingGather(buffer, ag_send.at[i], ag_recv.at[i], n_dp),
        )
        for i, (buffer, got) in enumerate(((sum2, got2), (sum1, got1)))
    ]

    def spread(point, points, total, step):
        begin = lax.div(point * total, jnp.int32(points))
        end = lax.div((point + 1) * total, jnp.int32(points))

        def one(t, _):
            step(t)
            return 0

        lax.fori_loop(begin, end, one, 0)

    def move_step(t):
        k = lax.div(t, jnp.int32(len(moving)))
        for s, m in enumerate(moving):
            mine = lax.rem(t, jnp.int32(len(moving))) == s

            @pl.when(mine)
            def _():
                m.finish(k)

            @pl.when(mine & (k < n_dp - 2))
            def _():
                m.start(k + 1)

    move_points = 2 * tiles + hidden // TILE

    def move(point):
        spread(point, move_points, len(moving) * (n_dp - 1), move_step)

    stop = 2 * (n_dp - 1)
    lead = 3
    all_turns = 2 * (n_dp - 1 + early) - 1
    pair_turns = all_turns * 2 // (3 * heads // 2)
    project_turns = all_turns // 9
    back_turns = (all_turns - project_turns - pair_turns * (heads // 2)) // 2
    back_from = project_turns + pair_turns * (heads // 2)
    block_ends = (8, 14, 19, 22, 32, 35)

    def sum_step(t):
        k = lax.div(t, jnp.int32(2))

        @pl.when(lax.rem(t, jnp.int32(2)) == 0)
        def _():
            advance(*sums[1], k, stop)

        @pl.when((lax.rem(t, jnp.int32(2)) == 1) & (k + lead < stop))
        def _():
            advance(*sums[0], k + lead, stop)

    def turn(begin, end):
        def one(t, _):
            sum_step(t)
            return 0

        lax.fori_loop(begin, end, one, 0)

    def turn_evenly(base, point, points, total):
        spread(point, points, total, lambda t: sum_step(base + t))

    def turn_block(pair, place):
        base = project_turns + pair * pair_turns
        ends = [pair_turns * b // block_ends[-1] for b in (0,) + block_ends]
        if ends[place] < ends[place + 1]:
            turn(base + ends[place], base + ends[place + 1])

    few = conts * piece
    quarter = prompt_len // n_tensor

    def deal(src, prompt_row, cont_row, prompt_base, cont_base, which):
        copies = []
        for q in range(n_tensor):
            copies.append(
                pltpu.make_async_copy(
                    src.at[pl.ds(prompt_row + q * quarter, quarter)], stack.at[q, pl.ds(prompt_base, quarter)],
                    part_sem.at[which, q, conts],
                )
            )
            for s in range(conts):
                copies.append(
                    pltpu.make_async_copy(
                        src.at[pl.ds(cont_row + s * CONT_LEN + q * piece, piece)],
                        stack.at[q, pl.ds(cont_base + s * piece, piece)], part_sem.at[which, q, s],
                    )
                )
        return copies

    deal_da2 = deal(da_all, cont_total, 0, 4 * few + quarter, 3 * few, 0)
    deal_da1 = deal(da_all, 0, prompt_len, 4 * few, 2 * few, 1)
    deal_y = deal(da_all, 0, prompt_len, 4 * few + 2 * quarter, 0, 2)
    deal_home = [
        pltpu.make_async_copy(
            y_home.at[pl.ds(s * CONT_LEN + q * piece, piece)], stack.at[q, pl.ds(few + s * piece, piece)],
            home_sem.at[q, s],
        )
        for q in range(n_tensor)
        for s in range(conts)
    ]
    outs = [
        pltpu.make_async_copy(src, dst, out_sem.at[i])
        for i, (src, dst) in enumerate(((sum1, w1s_out), (sum2, w2s_out), (wg, wg_out)))
    ]
    small[...] = jnp.zeros_like(small)

    gain, shift, bias = as_row(gain_two_ref), as_row(shift_two_ref), as_row(bias1_ref)
    loads[0].wait()
    loads[1].wait()

    def mlp_forward(i, _):
        @pl.when(i == 1)
        def _():
            loads[4].wait()

        at = span(i * TILE, TILE, TILE)
        xhat, _ = row_stats(x_all[at].astype(f32))
        h = (xhat * gain + shift).astype(bf16)
        h_all[at] = h
        for k in range(hidden // TILE):
            cols = slice(k * TILE, (k + 1) * TILE)
            value, slope = gelu_and_slope(dot(h, w1_v[:, cols]) + bias[:, cols])
            g_all[at, cols] = value.astype(bf16)
            mixed[at, cols] = slope.astype(bf16)
        move(i)
        return 0

    lax.fori_loop(0, tiles, mlp_forward, 0)
    loads[2].wait()
    loads[5].wait()

    def down_tile(k, _):
        cols = span(k * TILE, TILE, TILE)
        put_tile(sum2, k, dot_tn(g_all[:, cols], dy_all[:rows]), hidden, n_dp)
        move(tiles + k)
        return 0

    lax.fori_loop(0, hidden // TILE, down_tile, 0)
    sums[0][0].start(jnp.int32(0))
    members = find_members(group_ref, me_dp)
    offs = [offsets[m] for m in members]
    for c in loads[6:]:
        c.wait()
    for m, off in enumerate(offs):
        for a in range(3):
            tab[a, table_len + m * CONT_LEN : table_len + (m + 1) * CONT_LEN, :] = tab[a, pl.ds(off, CONT_LEN), :]
    lane = lax.broadcasted_iota(jnp.int32, (1, CHUNK), 1)
    bias_qkv = as_row(bias_qkv_ref)
    biases = []
    for pair in range(heads // 2):
        chunks = [slice((3 * pair + c) * CHUNK, (3 * pair + c + 1) * CHUNK) for c in range(3)]
        biases += pair_columns(*(bias_qkv[:, cols] for cols in chunks), lane)
        for cols, value in zip(chunks, pair_columns(*(wqkv_v[:, cols] for cols in chunks), lane)):
            wqkv_v[:, cols] = value

    loads[3].wait()

    def mlp_backward(i, _):
        at = span(i * TILE, TILE, TILE)
        dy = dy_all[at]
        for k in range(hidden // TILE):
            cols = slice(k * TILE, (k + 1) * TILE)
            du = (dot_nt(dy, w2_v[cols, :]) * mixed[at, cols].astype(f32)).astype(bf16)
            mixed[at, cols] = du
            small[5:6, cols] += jnp.sum(du.astype(f32), axis=0, keepdims=True)
        da = dot_nt(mixed[at, :hidden], w1_v[...])
        da_all[at] = da.astype(bf16)
        xhat, _ = row_stats(x_all[at].astype(f32))
        small[2:3] += jnp.sum(da * xhat, axis=0, keepdims=True)
        small[3:4] += jnp.sum(da, axis=0, keepdims=True)
        small[4:5] += jnp.sum(dy.astype(f32), axis=0, keepdims=True)
        move(tiles + hidden // TILE + i)

        @pl.when((lax.rem(i, jnp.int32(2)) == 0) & (i > 0) & (lax.div(i, jnp.int32(2)) < lead))
        def _():
            advance(*sums[0], lax.div(i, jnp.int32(2)) - 1, stop)

        return 0

    lax.fori_loop(0, tiles, mlp_backward, 0)
    for c in deal_da2:
        c.start()

    for c in own:
        c.wait()
    for m, member in enumerate(members):
        where = ring_spot(lax.div(member, jnp.int32(conts)), n_dp)
        slot = lax.rem(member, jnp.int32(conts))
        for a in range(2):
            moved[me_t, a, m] = ring[where, a, slot]
    over_y = [
        remote(moved.at[me_t], moved.at[me_t], y_send.at[k], y_recv.at[k], {"tensor": p})
        for k, p in enumerate(peers)
    ]
    over_core = [
        remote(
            moved.at[2 * j + core], moved.at[2 * j + core], core_send.at[j], core_recv.at[j], {"tensor": sibling}
        )
        for j in range(lines)
    ]
    for c in over_y:
        c.start()

    def up_tile(k, _):
        cols = span(k * TILE, TILE, TILE)
        put_tile(sum1, k, dot_tn(h_all[:, cols], mixed[:, :hidden]), width, n_dp)
        return 0

    lax.fori_loop(0, width // TILE, up_tile, 0)
    sums[1][0].start(jnp.int32(0))
    advance(*sums[0], jnp.int32(lead - 1), stop)

    gain, shift = as_row(gain_one_ref), as_row(shift_one_ref)

    def turned(z, start, sign):
        cos, low, high = (tab[a, pl.ds(start, TILE), :] for a in range(3))
        half = ROT // 2
        return z * cos + (pltpu.roll(z, CHUNK - half, 1) * low + pltpu.roll(z, half, 1) * high) * sign

    def table_start(i):
        return pl.multiple_of(i * TILE + lax.div(i, jnp.int32(prompt_tiles)) * (table_len - prompt_len), CHUNK)

    def project(i):
        at = span(i * TILE, TILE, TILE)
        source = span(i * TILE + cont_total, TILE, TILE)
        xhat, _ = row_stats(x_all[source].astype(f32))
        h = (xhat * gain + shift).astype(bf16)
        h_all[at] = h
        do = dot_nt(dy_all[source], wd_v[...]).astype(bf16)
        for pair in range(heads // 2):
            q, k, v = (
                dot(h, wqkv_v[:, c * CHUNK : (c + 1) * CHUNK]) + biases[c] for c in range(3 * pair, 3 * pair + 3)
            )
            q = turned(q, table_start(i), 1.0)
            qs[2 * pair, at] = jnp.where(lane < HD, q, 0.0).astype(bf16)
            qs[2 * pair + 1, at] = jnp.where(lane < HD, 0.0, q).astype(bf16)
            k = turned(k, table_start(i), 1.0)
            ks[pair, at] = k.astype(bf16)
            k_turned[pair, :, at] = k.T.astype(bf16)
            vs[pair, at] = v.astype(bf16)
            v_turned[pair, :, at] = v.T.astype(bf16)
            both = do[:, pair * CHUNK : (pair + 1) * CHUNK].astype(f32)
            dos[2 * pair, at] = jnp.where(lane < HD, both, 0.0).astype(bf16)
            dos[2 * pair + 1, at] = jnp.where(lane < HD, 0.0, both).astype(bf16)

    def project_prompt(i, _):
        project(i)
        turn_evenly(0, i, prompt_tiles, project_turns)
        return 0

    lax.fori_loop(0, prompt_tiles, project_prompt, 0)
    for c in over_y:
        c.wait()
    for c in over_core:
        c.start()

    query_lane = lax.broadcasted_iota(jnp.int32, (1, TILE), 1)
    reach = jnp.zeros((1, TILE), jnp.int32)
    for m, off in enumerate(offs):
        reach = jnp.where(lax.div(query_lane, jnp.int32(CONT_LEN)) == m, off, reach)

    def attend(pair, _):
        for block in list(range(prompt_tiles - 1, -1, -1)) + [prompt_tiles]:
            first = block * TILE
            seen = first + TILE
            at = slice(first, seen)
            if block == prompt_tiles:
                @pl.when(pair == 0)
                def _():
                    for c in over_core:
                        c.wait()
                    for q in range(n_tensor):
                        for s in range(conts):
                            to = rows + s * CONT_LEN + q * piece
                            x_all[to : to + piece, :] = moved[q, 0, s]
                            dy_all[to : to + piece, :] = moved[q, 1, s]
                    project(jnp.int32(prompt_tiles))

            k, v = ks[pair, :seen], vs[pair, :seen]
            key = lax.broadcasted_iota(jnp.int32, (TILE, TILE), 0)
            query = lax.broadcasted_iota(jnp.int32, (TILE, TILE), 1)
            seen_near = key <= query
            if block == prompt_tiles:
                key_row = lax.broadcasted_iota(jnp.int32, (prompt_len, TILE), 0)
                same = lax.div(key, jnp.int32(CONT_LEN)) == lax.div(query, jnp.int32(CONT_LEN))
                seen_near = seen_near & same
            heads_now = (2 * pair, 2 * pair + 1)
            scores = [dot_nt(k, qs[h, at]) * scale for h in heads_now]
            dprobs = [dot_nt(v, dos[h, at]) for h in heads_now]
            lows, low_slopes, o_turned, dq_turned = [], [], [], []
            for sub in range(2):
                s, dprob = scores[sub], dprobs[sub]
                near = jnp.where(seen_near, s[first:], masked_value)
                if block == prompt_tiles:
                    s = jnp.concatenate([jnp.where(key_row < reach, s[:first], masked_value), near], axis=0)
                else:
                    s = near if first == 0 else jnp.concatenate([s[:first], near], axis=0)
                p = jnp.exp(s - jnp.max(s, axis=0, keepdims=True))
                p = p * (1.0 / jnp.sum(p, axis=0, keepdims=True))
                low = p.astype(bf16)
                delta = jnp.sum(p * dprob, axis=0, keepdims=True)
                ds = (p * (dprob - delta)).astype(bf16)
                part = slice(sub * HD, (sub + 1) * HD)
                o_turned.append(dot(v_turned[pair, part, :seen], low))
                dq_turned.append(dot(k_turned[pair, part, :seen], ds))
                lows.append(low)
                low_slopes.append(ds)
            o_all[at, span(pair * CHUNK, CHUNK, CHUNK)] = jnp.concatenate(o_turned, axis=0).T.astype(bf16)
            dq = jnp.concatenate(dq_turned, axis=0).T * scale
            dq = turned(dq, table_start(jnp.int32(block)), -1.0).astype(bf16)
            cols = span(3 * pair * CHUNK, CHUNK, CHUNK)
            mixed[at, cols] = dq
            small[6:7, cols] += jnp.sum(dq.astype(f32), axis=0, keepdims=True)
            q_both = jnp.concatenate([qs[h, at] for h in heads_now], axis=0)
            do_both = jnp.concatenate([dos[h, at] for h in heads_now], axis=0)
            dk = dot(jnp.concatenate(low_slopes, axis=1), q_both)
            dv = dot(jnp.concatenate(lows, axis=1), do_both)
            if block == prompt_tiles - 1:
                dks[:seen] = dk
                dvs[:seen] = dv
            else:
                old = min(seen, prompt_len)
                dks[:old] += dk[:old]
                dvs[:old] += dv[:old]
                if old < seen:
                    dks[old:seen] = dk[old:]
                    dvs[old:seen] = dv[old:]
            turn_block(pair, prompt_tiles - 1 - block if block < prompt_tiles else block)

        for i in range(tiles):
            at = slice(i * TILE, (i + 1) * TILE)
            dk = turned(dks[at] * scale, table_start(jnp.int32(i)), -1.0).astype(bf16)
            for c, value in ((1, dk), (2, dvs[at].astype(bf16))):
                cols = span((3 * pair + c) * CHUNK, CHUNK, CHUNK)
                mixed[at, cols] = value
                small[6:7, cols] += jnp.sum(value.astype(f32), axis=0, keepdims=True)
        turn_block(pair, 5)
        return 0

    lax.fori_loop(0, heads // 2, attend, 0)
    for c in deal_da2:
        c.wait()

    def weight_tile(k, _):
        cols = span(k * TILE, TILE, TILE)
        put_tile(wg, k, dot_tn(h_all[:, cols], mixed[:, : 3 * local]), width, n_dp, slice(0, 3 * local))
        put_tile(wg, k, dot_tn(dy_all[cont_total:, cols], o_all[...]), width, n_dp, slice(3 * local, 4 * local))
        turn_evenly(back_from, k, width // TILE, all_turns - back_from - back_turns)
        return 0

    lax.fori_loop(0, width // TILE, weight_tile, 0)
    summing = RingSum(wg, got1, x_send, x_recv, n_dp)
    gathering = RingGather(wg, xg_send, xg_recv, n_dp)
    cont_from = 4
    rest_ticks = 2 * stop - all_turns
    all_ticks = max(stop, rest_ticks, cont_from + n_dp - 1)
    summing.start(jnp.int32(0))

    def back(i, _):
        at = span(i * TILE, TILE, TILE)
        da = dot_nt(mixed[at, : 3 * local], wqkv_v[...])
        da_all[at] = da.astype(bf16)
        xhat, _ = row_stats(x_all[span(i * TILE + cont_total, TILE, TILE)].astype(f32))
        small[0:1] += jnp.sum(da * xhat, axis=0, keepdims=True)
        small[1:2] += jnp.sum(da, axis=0, keepdims=True)

        turn_evenly(all_turns - back_turns, i, tiles, back_turns)
        return 0

    lax.fori_loop(0, tiles, back, 0)
    for c in deal_da1:
        c.start()

    def home_steps(k):
        ahead = lax.rem(spot - k + n_dp, jnp.int32(n_dp))
        back = lax.rem(spot + k, jnp.int32(n_dp))
        return (
            remote(ring.at[ahead, 0], ring.at[ahead, 0], home_send.at[0, k], home_recv.at[0, k], {"dp": after}),
            remote(ring.at[back, 1], ring.at[back, 1], home_send.at[1, k], home_recv.at[1, k], {"dp": before}),
            remote(
                small_ring.at[ahead, 0], small_ring.at[ahead, 0], home_send.at[2, k], home_recv.at[2, k], {"dp": after}
            ),
            remote(
                small_ring.at[back, 1], small_ring.at[back, 1], home_send.at[3, k], home_recv.at[3, k], {"dp": before}
            ),
        )

    def run_ticks(begin, end):
        def one(t, _):
            advance(summing, gathering, t, 2 * (n_dp - 1))

            @pl.when(t < rest_ticks)
            def _():
                sum_step(all_turns + t)

            k = t - cont_from

            @pl.when((k >= 0) & (k < n_dp - 1))
            def _():
                for c in home_steps(k):
                    c.wait()

            @pl.when((k >= 0) & (k < n_dp - 2))
            def _():
                for c in home_steps(k + 1):
                    c.start()

            return 0

        lax.fori_loop(begin, end, one, 0)

    line = lax.div(me_t, jnp.int32(2))
    base_one, base_two, base_y = 4 * few, 4 * few + quarter, 4 * few + 2 * quarter
    depth = base_y + quarter
    group_rows = ((0, base_one), (base_one, 2 * quarter), (base_y, quarter))
    room = rows // depth

    def own_part(m, start, size):
        return (h_all, da_all)[m // room].at[pl.ds((m % room) * depth + start, size)]

    def fill(n, m):
        j = lax.rem(line + (m + 1), jnp.int32(lines))
        return pltpu.make_async_copy(
            stack.at[2 * j + core, pl.ds(*group_rows[n])], own_part(m, *group_rows[n]), fill_sem.at[n, m]
        )

    def to_core(n):
        at = pl.ds(*group_rows[n])
        return [
            remote(
                stack.at[2 * j + 1 - core, at], rc.at[j, at], rc_send.at[n, j], rc_recv.at[n, j], {"tensor": sibling}
            )
            for j in range(lines)
        ]

    def to_line(n):
        return [
            remote(
                own_part(k, *group_rows[n]), ry.at[k, pl.ds(*group_rows[n])], ry_send.at[n, k], ry_recv.at[n, k],
                {"tensor": p},
            )
            for k, p in enumerate(peers)
        ]

    def pass_on(n):
        for c in to_core(n):
            c.wait()
        for k in range(lines - 1):
            j = lax.rem(line + (k + 1), jnp.int32(lines))
            mine = own_part(k, *group_rows[n])
            mine[...] = (mine[...].astype(f32) + rc[j, pl.ds(*group_rows[n])].astype(f32)).astype(bf16)
        for c in to_line(n):
            c.start()

    small_to_core = remote(small, small_core, sc_send, sc_recv, {"tensor": sibling})
    small_to_core.start()
    for c in deal_da1:
        c.wait()
    for c in to_core(1):
        c.start()

    def y_tile(i, _):
        at = span(i * TILE, TILE, TILE)
        total = dot(o_all[at], wd_v[...]) + dot(g_all[span(i * TILE + cont_total, TILE, TILE)], w2_v[...])
        da_all[at] = total.astype(bf16)
        return 0

    lax.fori_loop(0, prompt_tiles, y_tile, 0)
    da_all[prompt_len:] = dot(o_all[prompt_len:], wd_v[...]).astype(bf16)
    y_home[...] = dot(g_all[:cont_total], w2_v[...]).astype(bf16)
    for c in deal_y + deal_home:
        c.start()
    run_ticks(0, 1)
    for c in deal_y + deal_home:
        c.wait()
    for n in (0, 2):
        for c in to_core(n):
            c.start()
    fills = [fill(n, m) for n in (0, 1, 2) for m in range(lines)]
    for c in fills:
        c.start()
    small_to_core.wait()
    row = lax.broadcasted_iota(jnp.int32, (8, 1), 0)
    small_y[line] = small[...] + jnp.where(row < 4, small_core[...], 0.0)
    small_to_line = [
        remote(small_y.at[line], small_y.at[line], sy_send.at[k], sy_recv.at[k], {"tensor": p})
        for k, p in enumerate(peers)
    ]
    for c in small_to_line:
        c.start()
    for c in fills:
        c.wait()
    pass_on(0)
    run_ticks(1, 2)
    pass_on(1)
    pass_on(2)
    for c in small_to_line:
        c.wait()
    reduced = small_y[0]
    for j in range(1, lines):
        reduced = reduced + small_y[j]
    reduced = jnp.where(row < 4, reduced, small[...]).astype(bf16)
    fold = width // 4
    for part in range(4):
        small_ring[spot, part // 2, part % 2 * 8 : part % 2 * 8 + 8] = reduced[:, part * fold : (part + 1) * fold]
    run_ticks(2, cont_from)

    def summed(start, size):
        total = own_part(lines - 1, start, size)[...].astype(f32) + rc[line, pl.ds(start, size)].astype(f32)
        for k in range(lines - 1):
            total = total + ry[k, pl.ds(start, size)].astype(f32)
        return total

    def quarter_rows(q):
        return pl.ds(pl.multiple_of(q * quarter, 16), quarter)

    gain_two = as_row(gain_two_ref)
    both = as_row(bias_one_ref) + as_row(bias_two_ref)
    results = (out_p, grad_p)

    def gather_line(a):
        at = quarter_rows(me_t)
        return [pltpu.make_async_copy(own_rows.at[a], results[a].at[at], rows_sem.at[a])] + [
            remote(own_rows.at[a], results[a].at[at], gl_send.at[a, k], gl_recv.at[a, k], {"tensor": p})
            for k, p in enumerate(peers)
        ]

    def to_sibling(a):
        at = quarter_rows(me_t)
        return [remote(own_rows.at[a], results[a].at[at], gc_send.at[a, 0], gc_recv.at[a, 0], {"tensor": sibling})]

    def gather_core(a):
        copies = []
        for k in range(1, lines):
            at = quarter_rows(2 * lax.rem(line + k, jnp.int32(lines)) + core)
            copies.append(
                remote(results[a].at[at], results[a].at[at], gc_send.at[a, k], gc_recv.at[a, k], {"tensor": sibling})
            )
        return copies

    for c in to_line(0):
        c.wait()
    for s in range(conts):
        ring[spot, 0, s] = summed(s * piece, piece).astype(bf16)
        theirs = x_all[span(rows + s * CONT_LEN + me_t * piece, piece, 16)].astype(f32)
        ring[spot, 1, s] = norm_pull(theirs, summed(2 * few + s * piece, piece) * gain).astype(bf16)
        home = span(s * CONT_LEN + me_t * piece, piece, 16)
        x_home = x_all[home].astype(f32)
        keep_y[s] = x_home + summed(few + s * piece, piece) + both
        pulled = norm_pull(x_home, summed(3 * few + s * piece, piece) * gain_two)
        keep_d[s] = dy_all[home].astype(f32) + pulled
    for c in home_steps(jnp.int32(0)):
        c.start()
    run_ticks(cont_from, cont_from + 3)
    quarter_at = span(cont_total + me_t * quarter, quarter, 16)
    for c in to_line(1):
        c.wait()
    e = summed(base_one, quarter) * gain + summed(base_two, quarter) * gain_two
    own_rows[1] = (dy_all[quarter_at].astype(f32) + norm_pull(x_all[quarter_at].astype(f32), e)).astype(bf16)
    for c in gather_line(1) + to_sibling(1):
        c.start()
    run_ticks(cont_from + 3, cont_from + 5)
    for c in to_line(2):
        c.wait()
    own_rows[0] = (x_all[quarter_at].astype(f32) + summed(base_y, quarter) + both).astype(bf16)
    for c in gather_line(0) + to_sibling(0):
        c.start()
    moved_home = cont_from + n_dp - 1
    run_ticks(cont_from + 5, moved_home)
    for part in range(4):
        at = slice(part % 2 * 8, part % 2 * 8 + 8)
        total = small_ring[0, part // 2, at].astype(f32)
        for j in range(1, n_dp):
            total = total + small_ring[j, part // 2, at].astype(f32)
        vec_out[:, part * fold : (part + 1) * fold] = total
    for s in range(conts):
        mine = me_dp * conts + s
        group = group_ref[mine]
        first, _ = find_members(group_ref, group)
        slot = jnp.where(first == mine, jnp.int32(0), jnp.int32(1))
        where = ring_spot(group, n_dp)
        fin[me_t, 0, s] = (keep_y[s] + ring[where, 0, slot].astype(f32)).astype(bf16)
        fin[me_t, 1, s] = (keep_d[s] + ring[where, 1, slot].astype(f32)).astype(bf16)
    fin_line = [
        remote(fin.at[me_t], fin.at[me_t], fin_send.at[k], fin_recv.at[k], {"tensor": p})
        for k, p in enumerate(peers)
    ]
    fin_core = [
        remote(
            fin.at[2 * j + core], fin.at[2 * j + core], finc_send.at[j], finc_recv.at[j], {"tensor": sibling}
        )
        for j in range(lines)
    ]
    for c in fin_line:
        c.start()
    for c in gather_line(1):
        c.wait()
    for c in gather_core(1):
        c.start()
    run_ticks(moved_home, moved_home + 2)
    for c in gather_line(0):
        c.wait()
    for c in gather_core(0):
        c.start()
    if rest_ticks <= moved_home + 2:
        for c in outs[:2]:
            c.start()
    run_ticks(moved_home + 2, max(moved_home + 2, all_ticks))
    for c in outs if rest_ticks > moved_home + 2 else outs[2:]:
        c.start()
    for c in fin_line:
        c.wait()
    for c in fin_core:
        c.start()
    for c in gather_core(0) + to_sibling(0) + gather_core(1) + to_sibling(1) + fin_core:
        c.wait()
    last = [
        pltpu.make_async_copy(
            fin.at[q, a, s], dst.at[pl.ds(s * CONT_LEN + q * piece, piece)], outc_sem.at[a, q, s]
        )
        for a, dst in ((0, out_c), (1, grad_c))
        for q in range(n_tensor)
        for s in range(conts)
    ]
    for c in last:
        c.start()
    for c in last + outs:
        c.wait()


def run_layer(n_dp, n_tensor, early, group_of, offsets, xp, xc, dp, dc, w1, w2, wqkv, wd, *vectors):
    prompt_len, width = xp.shape
    cont_total = xc.shape[0]
    rows = prompt_len + cont_total
    hidden = w1.shape[1]
    local = wd.shape[0]
    heads = local // HD
    piece = CONT_LEN // n_tensor
    lines = n_tensor // 2
    table = jnp.asarray(rotary_table(prompt_len + CONT_LEN))
    table_rows = table.shape[1] + MEMBERS * CONT_LEN
    up, down = ring_shape(width, hidden, n_dp), ring_shape(hidden, width, n_dp)
    third = ring_shape(width, 4 * local, n_dp)
    quarter = prompt_len // n_tensor
    depth = 4 * MEMBERS * piece + 3 * quarter
    shape = jax.ShapeDtypeStruct
    hbm = pl.BlockSpec(memory_space=pl.ANY)
    vmem = pl.BlockSpec(memory_space=pltpu.VMEM)
    smem = pl.BlockSpec(memory_space=pltpu.SMEM)
    sem = pltpu.SemaphoreType.DMA
    return pl.pallas_call(
        functools.partial(layer_kernel, n_dp, n_tensor, early),
        out_shape=(
            shape(xp.shape, bf16),
            shape(xc.shape, bf16),
            shape(xp.shape, bf16),
            shape(xc.shape, bf16),
            shape(up, bf16),
            shape(down, bf16),
            shape(third, bf16),
            shape((n_tensor, depth, width), bf16),
            shape((8, width), f32),
        ),
        in_specs=[smem] * 2 + [hbm] * 9 + [vmem] * 8,
        out_specs=(hbm,) * 8 + (vmem,),
        scratch_shapes=[
            pltpu.VMEM((rows + cont_total, width), bf16),
            pltpu.VMEM((rows + cont_total, width), bf16),
            pltpu.VMEM((width, hidden), bf16),
            pltpu.VMEM((hidden, width), bf16),
            pltpu.VMEM((width, 3 * local), bf16),
            pltpu.VMEM((local, width), bf16),
            pltpu.VMEM((3, table_rows, CHUNK), f32),
            pltpu.VMEM((rows, width), bf16),
            pltpu.VMEM((rows, hidden), bf16),
            pltpu.VMEM((rows, max(hidden, 3 * local)), bf16),
            pltpu.VMEM((rows, width), bf16),
            pltpu.VMEM((n_dp, 2, MEMBERS, piece, width), bf16),
            pltpu.VMEM((n_tensor, 2, MEMBERS, piece, width), bf16),
            pltpu.VMEM(up, bf16),
            pltpu.VMEM(down, bf16),
            pltpu.VMEM((n_dp - 1,) + up[1:], bf16),
            pltpu.VMEM((n_dp - 1,) + down[1:], bf16),
            pltpu.VMEM(third, bf16),
        ]
        + [pltpu.VMEM((heads, rows, CHUNK), bf16)] * 2
        + [pltpu.VMEM((heads // 2, rows, CHUNK), bf16)] * 2
        + [pltpu.VMEM((heads // 2, CHUNK, rows), bf16)] * 2
        + [pltpu.VMEM((rows, CHUNK), f32)] * 2
        + [
            pltpu.VMEM((rows, local), bf16),
            pltpu.VMEM((cont_total, width), bf16),
            pltpu.VMEM((lines, depth, width), bf16),
            pltpu.VMEM((lines - 1, depth, width), bf16),
            pltpu.VMEM((2, quarter, width), bf16),
            pltpu.VMEM((MEMBERS, piece, width), f32),
            pltpu.VMEM((MEMBERS, piece, width), f32),
            pltpu.VMEM((n_tensor, 2, MEMBERS, piece, width), bf16),
            pltpu.VMEM((8, width), f32),
            pltpu.VMEM((8, width), f32),
            pltpu.VMEM((lines, 8, width), f32),
            pltpu.VMEM((n_dp, 2, 16, width // 4), bf16),
            sem((2, MEMBERS)),
            sem((9,)),
            sem((3,)),
            sem((3, n_tensor, MEMBERS + 1)),
            sem((n_tensor, MEMBERS)),
            sem((MEMBERS, 2, 2, n_dp - 1)),
            sem((MEMBERS, 2, 2, n_dp - 1)),
            sem((lines - 1,)),
            sem((lines - 1,)),
            sem((lines,)),
            sem((lines,)),
        ]
        + [sem((2, 2, n_dp - 1))] * 4
        + [sem((3, lines))] * 3
        + [sem((3, lines - 1))] * 2
        + [sem((2, lines - 1))] * 2
        + [sem((2, lines))] * 2
        + [sem((4, n_dp - 1))] * 2
        + [sem] * 2
        + [sem((lines - 1,))] * 4
        + [sem((lines,))] * 2
        + [sem((2,)), sem((2, n_tensor, MEMBERS))]
        + [sem((2, n_dp - 1))] * 4,
        compiler_params=pltpu.CompilerParams(
            collective_id=0, has_side_effects=True, vmem_limit_bytes=63 * 2**20
        ),
        cost_estimate=pl.CostEstimate(flops=34 * 10**9, bytes_accessed=40 * 10**6, transcendentals=5 * 10**6),
        name="layer",
    )(group_of, offsets, xp, xc, dp, dc, w1, w2, wqkv, wd, table, *vectors)


def finish_kernel(
    groups, out_p, out_c, grad_p, grad_c, w1s, w2s, wg, total,
    out_p_out, out_c_out, grad_p_out, grad_c_out, gain_one, shift_one, gain_two, shift_two,
    qkv_out, qkv_bias, dense_out, dense_bias, w1_out, w1_bias, w2_out, w2_bias,
    out_p_v, out_c_v, grad_p_v, grad_c_v, w1s_v, w2s_v, wg_v, qkv_v, dense_v, w1_v, w2_v,
    copy_in, copy_out, piece_in, piece_out, dense_sem,
):
    local3 = qkv_out.shape[1]
    plain = (
        (out_p, out_p_v, out_p_out), (grad_p, grad_p_v, grad_p_out),
        (out_c, out_c_v, out_c_out), (grad_c, grad_c_v, grad_c_out),
    )
    plain_in = [pltpu.make_async_copy(a, b, copy_in.at[i]) for i, (a, b, _) in enumerate(plain)]
    plain_out = [pltpu.make_async_copy(b, c, copy_out.at[i]) for i, (_, b, c) in enumerate(plain)]
    weights = ((w1s, w1s_v, w1_v, w1_out), (w2s, w2s_v, w2_v, w2_out), (wg, wg_v, qkv_v, qkv_out))

    def chunks_of(a, g):
        return pl.ds(g * (a.shape[0] // groups), a.shape[0] // groups)

    def rows_of(a, g):
        return pl.ds(g * (a.shape[0] // groups), a.shape[0] // groups)

    loads = [
        [pltpu.make_async_copy(a.at[chunks_of(a, g)], b.at[chunks_of(a, g)], piece_in.at[i, g]) for g in range(groups)]
        for i, (a, b, _, _) in enumerate(weights)
    ]
    stores = [
        [pltpu.make_async_copy(c.at[rows_of(c, g)], d.at[rows_of(c, g)], piece_out.at[i, g]) for g in range(groups)]
        for i, (_, _, c, d) in enumerate(weights)
    ]
    for c in plain_in[:1] + loads[0] + plain_in[1:2] + loads[1] + plain_in[2:] + loads[2]:
        c.start()
    lane = lax.broadcasted_iota(jnp.int32, (1, CHUNK), 1)
    pairs = [
        [slice((3 * pair + c) * CHUNK, (3 * pair + c + 1) * CHUNK) for c in range(3)]
        for pair in range(local3 // (3 * CHUNK))
    ]
    for n, dst in enumerate((gain_one, shift_one, gain_two, shift_two, dense_bias, w1_bias)):
        dst[...] = total[n, : dst.shape[0]]
    w2_bias[...] = total[4, :]
    for columns in pairs:
        for cols, value in zip(columns, unpair_columns(*(total[6:7, cols] for cols in columns), lane)):
            qkv_bias[cols] = value[0]

    def pieces(src, dst, g):
        per_group = src.shape[0] // groups
        size = dst.shape[0] // (2 * src.shape[0])
        for p in range(2 * per_group):
            first = g * (dst.shape[0] // groups) + p * size
            yield g * per_group + p // 2, p % 2, size, slice(first, first + size)

    for i in range(2):
        plain_in[i].wait()
        plain_out[i].start()
        _, src, dst, _ = weights[i]
        for g in range(groups):
            loads[i][g].wait()
            for chunk, way, size, to in pieces(src, dst, g):
                dst[to, :] = src[chunk, way, :size].astype(f32)
            stores[i][g].start()
    for i in (2, 3):
        plain_in[i].wait()
        plain_out[i].start()
    for g in range(groups):
        loads[2][g].wait()
        dense = []
        for chunk, way, size, to in pieces(wg_v, qkv_v, g):
            for columns in pairs:
                parts = unpair_columns(*(wg_v[chunk, way, :size, cols].astype(f32) for cols in columns), lane)
                for cols, value in zip(columns, parts):
                    qkv_v[to, cols] = value
            dense.append(wg_v[chunk, way, :size, local3:].astype(f32))
        stores[2][g].start()
        size = dense_v.shape[1] // groups
        dense_v[:, g * size : (g + 1) * size] = jnp.concatenate(dense, axis=0).T
    last = pltpu.make_async_copy(dense_v, dense_out, dense_sem)
    last.start()
    for c in plain_out + stores[0] + stores[1] + stores[2] + [last]:
        c.wait()


def run_finish(local3, hidden, out_p, out_c, grad_p, grad_c, w1s, w2s, wg, total):
    width = out_p.shape[1]
    local = local3 // 3
    groups = 4
    shape = jax.ShapeDtypeStruct
    hbm = pl.BlockSpec(memory_space=pl.ANY)
    vmem = pl.BlockSpec(memory_space=pltpu.VMEM)
    sem = pltpu.SemaphoreType.DMA
    moved = (out_p, out_c, grad_p, grad_c)
    return pl.pallas_call(
        functools.partial(finish_kernel, groups),
        out_shape=tuple(shape(a.shape, bf16) for a in moved)
        + (shape((width,), f32),) * 4
        + (
            shape((width, local3), f32), shape((local3,), f32),
            shape((local, width), f32), shape((width,), f32),
            shape((width, hidden), f32), shape((hidden,), f32),
            shape((hidden, width), f32), shape((width,), f32),
        ),
        in_specs=[hbm] * 7 + [vmem],
        out_specs=(hbm,) * 4 + (vmem,) * 4 + (hbm, vmem) * 4,
        scratch_shapes=[pltpu.VMEM(a.shape, bf16) for a in moved + (w1s, w2s, wg)]
        + [
            pltpu.VMEM((width, local3), f32),
            pltpu.VMEM((local, width), f32),
            pltpu.VMEM((width, hidden), f32),
            pltpu.VMEM((hidden, width), f32),
            sem((4,)),
            sem((4,)),
            sem((3, groups)),
            sem((3, groups)),
            sem,
        ],
        compiler_params=pltpu.CompilerParams(vmem_limit_bytes=60 * 2**20),
        name="finish",
    )(out_p, out_c, grad_p, grad_c, w1s, w2s, wg, total)


def per_device(
    n_dp, n_tensor,
    prompt_in, cont_in, prompt_cot, cont_cot, group_of, offsets, ln1_gain, ln1_bias, ln2_gain, ln2_bias,
    qkv_weight, qkv_bias, dense_weight, dense_bias, fc1_weight, fc1_bias, fc2_weight, fc2_bias,
):
    width = prompt_in.shape[1]
    hidden = fc1_weight.shape[1]
    local3 = qkv_weight.shape[1]

    out_p, out_c, grad_p, grad_c, w1g, w2g, wg, _, total = run_layer(
        n_dp, n_tensor, min(n_dp - 1, 1), group_of, offsets, prompt_in, cont_in, prompt_cot, cont_cot,
        fc1_weight, fc2_weight, qkv_weight, dense_weight,
        ln2_gain, ln2_bias, fc1_bias, ln1_gain, ln1_bias, qkv_bias, dense_bias, fc2_bias,
    )
    return run_finish(local3, hidden, out_p, out_c, grad_p, grad_c, w1g, w2g, wg, total)


def solution(mesh):
    rows, whole, columns, segment, depth = P("dp", None), P(), P(None, "tensor"), P("tensor"), P("tensor", None)
    return jax.shard_map(
        functools.partial(per_device, mesh.shape["dp"], mesh.shape["tensor"]),
        mesh=mesh,
        in_specs=(
            rows, rows, rows, rows, whole, whole, whole, whole, whole, whole,
            columns, segment, depth, whole, columns, segment, depth, whole,
        ),
        out_specs=(
            rows, rows, rows, rows, whole, whole, whole, whole,
            columns, segment, depth, whole, columns, segment, depth, whole,
        ),
        check_vma=False,
    )
```

```python
import functools
import math

import jax
import jax.numpy as jnp
import numpy as np
from jax import lax
from jax.experimental import pallas as pl
from jax.experimental.pallas import tpu as pltpu
from jax.sharding import PartitionSpec as P

HD = 64
ROT = 16
CONT_LEN = 128
TILE = 256
CHUNK = 128
MEMBERS = 2

eps_norm = 1e-05
masked_value = -1e30
MESH = pl.DeviceIdType.MESH
bf16 = jnp.bfloat16
f32 = jnp.float32


def dot(a, b):
    return jnp.dot(a, b, preferred_element_type=f32)


def dot_nt(a, b):
    return lax.dot_general(a, b, (((1,), (1,)), ((), ())), preferred_element_type=f32)


def dot_tn(a, b):
    return lax.dot_general(a, b, (((0,), (0,)), ((), ())), preferred_element_type=f32)


def row_stats(x):
    centered = x - jnp.mean(x, axis=-1, keepdims=True)
    scale = lax.rsqrt(jnp.mean(centered * centered, axis=-1, keepdims=True) + eps_norm)
    return centered * scale, scale


def norm_pull(x, e):
    xhat, scale = row_stats(x)
    return scale * (
        e
        - jnp.mean(e, axis=-1, keepdims=True)
        - xhat * jnp.mean(e * xhat, axis=-1, keepdims=True)
    )


def gelu_and_slope(u):
    t = 1.0 / (1.0 + jnp.abs(u) * (0.3275911 / math.sqrt(2.0)))
    bell = jnp.exp(-0.5 * u * u)
    poly = t * (
        0.127414796
        + t * (-0.142248368 + t * (0.7107068705 + t * (-0.7265760135 + t * 0.5307027145)))
    )
    tail = poly * bell
    cdf = jnp.where(u >= 0, 1.0 - tail, tail)
    return u * cdf, cdf + u * bell * (1.0 / math.sqrt(2.0 * math.pi))


def rotary_table(length):
    half = ROT // 2
    frequencies = np.exp(
        -np.arange(half, dtype=np.float32) * np.float32(2.0 * math.log(10000.0) / ROT)
    ).astype(np.float32)
    angles = np.arange(length, dtype=np.float32)[:, None] * frequencies[None, :]
    angles = np.concatenate([angles, angles], axis=1).astype(np.float32)
    cos = np.ones((length, HD), np.float32)
    low = np.zeros((length, HD), np.float32)
    high = np.zeros((length, HD), np.float32)
    cos[:, :ROT] = np.cos(angles)
    low[:, :half] = -np.sin(angles)[:, :half]
    high[:, half:ROT] = np.sin(angles)[:, half:]
    return np.stack([np.concatenate([t, t], axis=1) for t in (cos, low, high)])


def ring_spot(device, n):
    odd = lax.rem(device, jnp.int32(2))
    half = lax.div(device, jnp.int32(2))
    return (1 - odd) * half + odd * (n - 1 - half)


def ring_device(spot, n):
    far = lax.div(spot, jnp.int32(n // 2))
    return (1 - far) * (2 * spot) + far * (2 * (n - 1 - spot) + 1)


def ring_neighbours(n):
    spot = ring_spot(lax.axis_index("dp"), n)
    after = ring_device(lax.rem(spot + 1, jnp.int32(n)), n)
    before = ring_device(lax.rem(spot + n - 1, jnp.int32(n)), n)
    return spot, after, before


def find_members(group_ref, wanted):
    count = group_ref.shape[0]
    first = jnp.int32(count)
    last = jnp.int32(-1)
    for j in range(count):
        hit = group_ref[j] == wanted
        first = jnp.minimum(first, jnp.where(hit, jnp.int32(j), jnp.int32(count)))
        last = jnp.maximum(last, jnp.where(hit, jnp.int32(j), jnp.int32(-1)))
    return jnp.minimum(first, count - 1), jnp.maximum(last, 0)


def remote(src, dst, send, recv, device):
    return pltpu.make_async_remote_copy(
        src_ref=src, dst_ref=dst, send_sem=send, recv_sem=recv, device_id=device, device_id_type=MESH
    )


def as_row(ref):
    return ref[...].astype(f32).reshape(1, ref.shape[0])


def span(start, size, step):
    return pl.ds(pl.multiple_of(start, step), size)


def piece_rows(rows, n):
    return rows // (2 * n), max(16, rows // (2 * n))


def ring_shape(rows, width, n):
    return (n, 2, piece_rows(rows, n)[1], width)


def put_tile(buffer, k, value, rows, n, cols=slice(None)):
    size = piece_rows(rows, n)[0]
    pieces = TILE // size
    for p in range(pieces):
        buffer[k * (pieces // 2) + p // 2, p % 2, :size, cols] = value[p * size : (p + 1) * size].astype(bf16)


def pair_columns(c0, c1, c2, lane):
    low = lane < HD
    crossed = jnp.where(low, c2, c0)
    return jnp.where(low, c0, c1), pltpu.roll(crossed, HD, 1), jnp.where(low, c1, c2)


def unpair_columns(q, k, v, lane):
    low = lane < HD
    crossed = pltpu.roll(k, HD, 1)
    return jnp.where(low, q, crossed), jnp.where(low, v, q), jnp.where(low, crossed, v)


class RingSum:
    def __init__(self, buffer, arrived, send, recv, n):
        self.buffer, self.arrived, self.send, self.recv, self.n = buffer, arrived, send, recv, n
        self.spot, self.after, self.before = ring_neighbours(n)

    def copy(self, k, way):
        n = self.n
        chunk, device = (
            (lax.rem(self.spot + (2 * n - 1) - k, jnp.int32(n)), self.after),
            (lax.rem(self.spot + 1 + k, jnp.int32(n)), self.before),
        )[way]
        return remote(
            self.buffer.at[chunk, way], self.arrived.at[k, way], self.send.at[way, k], self.recv.at[way, k],
            {"dp": device},
        )

    def start(self, k, ways=(0, 1)):
        for way in ways:
            self.copy(k, way).start()

    def finish(self, k, ways=(0, 1)):
        n = self.n
        for way in ways:
            self.copy(k, way).wait()
            chunk = lax.rem(self.spot + ((2 * n - 2) - k, 2 + k)[way], jnp.int32(n))
            self.buffer[chunk, way] += self.arrived[k, way]


class RingGather:
    def __init__(self, buffer, send, recv, n, part=()):
        self.buffer, self.send, self.recv, self.n, self.part = buffer, send, recv, n, part
        self.spot, self.after, self.before = ring_neighbours(n)

    def copy(self, k, way):
        n = self.n
        chunk, device = (
            (lax.rem(self.spot + n - k, jnp.int32(n)), self.after),
            (lax.rem(self.spot + k, jnp.int32(n)), self.before),
        )[way]
        place = self.buffer.at[(chunk, way) + self.part]
        return remote(place, place, self.send.at[way, k], self.recv.at[way, k], {"dp": device})

    def start(self, k, ways=(0, 1)):
        for way in ways:
            self.copy(k, way).start()

    def finish(self, k, ways=(0, 1)):
        for way in ways:
            self.copy(k, way).wait()


def advance(summing, gathering, t, stop):
    n = summing.n
    for way in ((0,), (1,)):

        @pl.when(t < n - 1)
        def _():
            summing.finish(t, way)

        @pl.when(t < n - 2)
        def _():
            summing.start(t + 1, way)

        @pl.when((t == n - 2) & (stop > n - 1))
        def _():
            gathering.start(jnp.int32(0), way)

        @pl.when((t >= n - 1) & (t < stop))
        def _():
            gathering.finish(t - (n - 1), way)

        @pl.when((t >= n - 1) & (t < stop - 1))
        def _():
            gathering.start(t - (n - 2), way)


def layer_kernel(
    n_dp, n_tensor, early, group_ref, offsets, xp, xc, dp, dc, w1, w2, wqkv, wd, table,
    gain_two_ref, shift_two_ref, bias1_ref, gain_one_ref, shift_one_ref, bias_qkv_ref, bias_one_ref, bias_two_ref,
    out_p, out_c, grad_p, grad_c, w1s_out, w2s_out, wg_out, stack, vec_out,
    x_all, dy_all, w1_v, w2_v, wqkv_v, wd_v, tab, h_all, g_all, mixed, da_all, ring, moved,
    sum1, sum2, got1, got2, wg, qs, dos, ks, vs, k_turned, v_turned, dks, dvs, o_all, y_home,
    rc, ry, own_rows, keep_y, keep_d, fin, small, small_core, small_y, small_ring,
    own_sem, load_sem, out_sem, part_sem, home_sem, ring_send, ring_recv, y_send, y_recv, core_send, core_recv,
    rs_send, rs_recv, ag_send, ag_recv,
    fill_sem, rc_send, rc_recv, ry_send, ry_recv, gl_send, gl_recv, gc_send, gc_recv,
    home_send, home_recv, sc_send, sc_recv, sy_send, sy_recv, fin_send, fin_recv, finc_send, finc_recv,
    rows_sem, outc_sem, x_send, x_recv, xg_send, xg_recv,
):
    prompt_len, width = xp.shape
    cont_total = xc.shape[0]
    conts = MEMBERS
    rows = prompt_len + cont_total
    tiles = rows // TILE
    prompt_tiles = prompt_len // TILE
    hidden = w1.shape[1]
    local = wd.shape[0]
    heads = local // HD
    piece = CONT_LEN // n_tensor
    lines = n_tensor // 2
    table_len = table.shape[1]
    scale = 1.0 / math.sqrt(HD)
    me_dp, me_t = lax.axis_index("dp"), lax.axis_index("tensor")
    core = lax.rem(me_t, jnp.int32(2))
    sibling = me_t + 1 - 2 * core
    peers = [lax.rem(me_t + 2 * k, jnp.int32(n_tensor)) for k in range(1, lines)]
    spot, after, before = ring_neighbours(n_dp)

    own = [
        pltpu.make_async_copy(
            src.at[span(s * CONT_LEN + me_t * piece, piece, 16)], ring.at[spot, a, s], own_sem.at[a, s]
        )
        for a, src in enumerate((xc, dc))
        for s in range(conts)
    ]
    loads = [
        pltpu.make_async_copy(src, dst, load_sem.at[i])
        for i, (src, dst) in enumerate(
            (
                (xc, x_all.at[pl.ds(0, cont_total)]),
                (w1, w1_v),
                (dc, dy_all.at[pl.ds(0, cont_total)]),
                (w2, w2_v),
                (xp, x_all.at[pl.ds(cont_total, prompt_len)]),
                (dp, dy_all.at[pl.ds(cont_total, prompt_len)]),
                (wqkv, wqkv_v),
                (wd, wd_v),
                (table, tab.at[:, pl.ds(0, table_len)]),
            )
        )
    ]
    partners = [{"dp": after}, {"dp": before}, {"tensor": sibling}] + [{"tensor": p} for p in peers]
    barrier = pltpu.get_barrier_semaphore()
    for partner in partners:
        pl.semaphore_signal(barrier, inc=1, device_id=partner, device_id_type=MESH)
    for c in own + [loads[i] for i in (1, 0, 4, 2, 5, 3, 6, 7, 8)]:
        c.start()
    pl.semaphore_wait(barrier, len(partners))

    halves = min(2, piece // 16)
    moving = [
        RingGather(
            ring, ring_send.at[s, b], ring_recv.at[s, b], n_dp, (s, pl.ds(b * (piece // halves), piece // halves))
        )
        for s in range(conts)
        for b in range(halves)
    ]
    for s in range(conts):
        for b in range(halves):
            for way, (src, device) in enumerate(((xc, after), (dc, before))):
                at = span(s * CONT_LEN + me_t * piece + b * (piece // halves), piece // halves, 16)
                part = pl.ds(b * (piece // halves), piece // halves)
                remote(
                    src.at[at], ring.at[spot, way, s, part], ring_send.at[s, b, way, 0], ring_recv.at[s, b, way, 0],
                    {"dp": device},
                ).start()
    sums = [
        (
            RingSum(buffer, got, rs_send.at[i], rs_recv.at[i], n_dp),
            RingGather(buffer, ag_send.at[i], ag_recv.at[i], n_dp),
        )
        for i, (buffer, got) in enumerate(((sum2, got2), (sum1, got1)))
    ]

    def spread(point, points, total, step):
        begin = lax.div(point * total, jnp.int32(points))
        end = lax.div((point + 1) * total, jnp.int32(points))

        def one(t, _):
            step(t)
            return 0

        lax.fori_loop(begin, end, one, 0)

    def move_step(t):
        k = lax.div(t, jnp.int32(len(moving)))
        for s, m in enumerate(moving):
            mine = lax.rem(t, jnp.int32(len(moving))) == s

            for way in ((0,), (1,)):

                @pl.when(mine)
                def _():
                    m.finish(k, way)

                @pl.when(mine & (k < n_dp - 2))
                def _():
                    m.start(k + 1, way)

    move_points = 2 * tiles + hidden // TILE

    def move(point):
        spread(point, move_points, len(moving) * (n_dp - 1), move_step)

    stop = 2 * (n_dp - 1)
    lead = 3
    all_turns = 2 * (n_dp - 1 + early) - 1
    pair_turns = all_turns * 2 // (3 * heads // 2)
    project_turns = all_turns // 9
    back_turns = (all_turns - project_turns - pair_turns * (heads // 2)) // 2
    back_from = project_turns + pair_turns * (heads // 2)
    block_ends = (8, 14, 19, 22, 32, 35)

    def sum_step(t):
        k = lax.div(t, jnp.int32(2))

        @pl.when(lax.rem(t, jnp.int32(2)) == 0)
        def _():
            advance(*sums[1], k, stop)

        @pl.when((lax.rem(t, jnp.int32(2)) == 1) & (k + lead < stop))
        def _():
            advance(*sums[0], k + lead, stop)

    def turn(begin, end):
        def one(t, _):
            sum_step(t)
            return 0

        lax.fori_loop(begin, end, one, 0)

    def turn_evenly(base, point, points, total):
        spread(point, points, total, lambda t: sum_step(base + t))

    def turn_block(pair, place):
        base = project_turns + pair * pair_turns
        ends = [pair_turns * b // block_ends[-1] for b in (0,) + block_ends]
        if ends[place] < ends[place + 1]:
            turn(base + ends[place], base + ends[place + 1])

    few = conts * piece
    quarter = prompt_len // n_tensor

    def deal(src, prompt_row, cont_row, prompt_base, cont_base, which):
        copies = []
        for q in range(n_tensor):
            copies.append(
                pltpu.make_async_copy(
                    src.at[pl.ds(prompt_row + q * quarter, quarter)], stack.at[q, pl.ds(prompt_base, quarter)],
                    part_sem.at[which, q, conts],
                )
            )
            for s in range(conts):
                copies.append(
                    pltpu.make_async_copy(
                        src.at[pl.ds(cont_row + s * CONT_LEN + q * piece, piece)],
                        stack.at[q, pl.ds(cont_base + s * piece, piece)], part_sem.at[which, q, s],
                    )
                )
        return copies

    deal_da2 = deal(da_all, cont_total, 0, 4 * few + quarter, 3 * few, 0)
    deal_da1 = deal(da_all, 0, prompt_len, 4 * few, 2 * few, 1)
    deal_y = deal(da_all, 0, prompt_len, 4 * few + 2 * quarter, 0, 2)
    deal_home = [
        pltpu.make_async_copy(
            y_home.at[pl.ds(s * CONT_LEN + q * piece, piece)], stack.at[q, pl.ds(few + s * piece, piece)],
            home_sem.at[q, s],
        )
        for q in range(n_tensor)
        for s in range(conts)
    ]
    outs = [
        pltpu.make_async_copy(src, dst, out_sem.at[i])
        for i, (src, dst) in enumerate(((sum1, w1s_out), (sum2, w2s_out), (wg, wg_out)))
    ]
    small[...] = jnp.zeros_like(small)

    gain, shift, bias = as_row(gain_two_ref), as_row(shift_two_ref), as_row(bias1_ref)
    loads[0].wait()
    loads[1].wait()

    def mlp_forward(i, _):
        @pl.when(i == 1)
        def _():
            loads[4].wait()

        at = span(i * TILE, TILE, TILE)
        xhat, _ = row_stats(x_all[at].astype(f32))
        h = (xhat * gain + shift).astype(bf16)
        h_all[at] = h
        for k in range(hidden // TILE):
            cols = slice(k * TILE, (k + 1) * TILE)
            value, slope = gelu_and_slope(dot(h, w1_v[:, cols]) + bias[:, cols])
            g_all[at, cols] = value.astype(bf16)
            mixed[at, cols] = slope.astype(bf16)
        move(i)
        return 0

    lax.fori_loop(0, tiles, mlp_forward, 0)
    loads[2].wait()
    loads[5].wait()

    def down_tile(k, _):
        cols = span(k * TILE, TILE, TILE)
        put_tile(sum2, k, dot_tn(g_all[:, cols], dy_all[:rows]), hidden, n_dp)
        move(tiles + k)
        return 0

    lax.fori_loop(0, hidden // TILE, down_tile, 0)
    sums[0][0].start(jnp.int32(0))
    members = find_members(group_ref, me_dp)
    offs = [offsets[m] for m in members]
    for c in loads[6:]:
        c.wait()
    for m, off in enumerate(offs):
        for a in range(3):
            tab[a, table_len + m * CONT_LEN : table_len + (m + 1) * CONT_LEN, :] = tab[a, pl.ds(off, CONT_LEN), :]
    lane = lax.broadcasted_iota(jnp.int32, (1, CHUNK), 1)
    bias_qkv = as_row(bias_qkv_ref)
    biases = []
    for pair in range(heads // 2):
        chunks = [slice((3 * pair + c) * CHUNK, (3 * pair + c + 1) * CHUNK) for c in range(3)]
        biases += pair_columns(*(bias_qkv[:, cols] for cols in chunks), lane)
        for cols, value in zip(chunks, pair_columns(*(wqkv_v[:, cols] for cols in chunks), lane)):
            wqkv_v[:, cols] = value

    loads[3].wait()

    def mlp_backward(i, _):
        at = span(i * TILE, TILE, TILE)
        dy = dy_all[at]
        for k in range(hidden // TILE):
            cols = slice(k * TILE, (k + 1) * TILE)
            du = (dot_nt(dy, w2_v[cols, :]) * mixed[at, cols].astype(f32)).astype(bf16)
            mixed[at, cols] = du
            small[5:6, cols] += jnp.sum(du.astype(f32), axis=0, keepdims=True)
        da = dot_nt(mixed[at, :hidden], w1_v[...])
        da_all[at] = da.astype(bf16)
        xhat, _ = row_stats(x_all[at].astype(f32))
        small[2:3] += jnp.sum(da * xhat, axis=0, keepdims=True)
        small[3:4] += jnp.sum(da, axis=0, keepdims=True)
        small[4:5] += jnp.sum(dy.astype(f32), axis=0, keepdims=True)
        move(tiles + hidden // TILE + i)

        @pl.when((lax.rem(i, jnp.int32(2)) == 0) & (i > 0) & (lax.div(i, jnp.int32(2)) < lead))
        def _():
            advance(*sums[0], lax.div(i, jnp.int32(2)) - 1, stop)

        return 0

    lax.fori_loop(0, tiles, mlp_backward, 0)
    for c in deal_da2:
        c.start()

    for c in own:
        c.wait()
    for m, member in enumerate(members):
        where = ring_spot(lax.div(member, jnp.int32(conts)), n_dp)
        slot = lax.rem(member, jnp.int32(conts))
        for a in range(2):
            moved[me_t, a, m] = ring[where, a, slot]
    over_y = [
        remote(moved.at[me_t], moved.at[me_t], y_send.at[k], y_recv.at[k], {"tensor": p})
        for k, p in enumerate(peers)
    ]
    over_core = [
        remote(
            moved.at[2 * j + core], moved.at[2 * j + core], core_send.at[j], core_recv.at[j], {"tensor": sibling}
        )
        for j in range(lines)
    ]
    for c in over_y:
        c.start()

    def up_tile(k, _):
        cols = span(k * TILE, TILE, TILE)
        put_tile(sum1, k, dot_tn(h_all[:, cols], mixed[:, :hidden]), width, n_dp)
        return 0

    lax.fori_loop(0, width // TILE, up_tile, 0)
    sums[1][0].start(jnp.int32(0))
    advance(*sums[0], jnp.int32(lead - 1), stop)

    gain, shift = as_row(gain_one_ref), as_row(shift_one_ref)

    def turned(z, start, sign):
        cos, low, high = (tab[a, pl.ds(start, TILE), :] for a in range(3))
        half = ROT // 2
        return z * cos + (pltpu.roll(z, CHUNK - half, 1) * low + pltpu.roll(z, half, 1) * high) * sign

    def table_start(i):
        return pl.multiple_of(i * TILE + lax.div(i, jnp.int32(prompt_tiles)) * (table_len - prompt_len), CHUNK)

    def project(i):
        at = span(i * TILE, TILE, TILE)
        source = span(i * TILE + cont_total, TILE, TILE)
        xhat, _ = row_stats(x_all[source].astype(f32))
        h = (xhat * gain + shift).astype(bf16)
        h_all[at] = h
        do = dot_nt(dy_all[source], wd_v[...]).astype(bf16)
        for pair in range(heads // 2):
            q, k, v = (
                dot(h, wqkv_v[:, c * CHUNK : (c + 1) * CHUNK]) + biases[c] for c in range(3 * pair, 3 * pair + 3)
            )
            q = turned(q, table_start(i), 1.0)
            qs[2 * pair, at] = jnp.where(lane < HD, q, 0.0).astype(bf16)
            qs[2 * pair + 1, at] = jnp.where(lane < HD, 0.0, q).astype(bf16)
            k = turned(k, table_start(i), 1.0)
            ks[pair, at] = k.astype(bf16)
            k_turned[pair, :, at] = k.T.astype(bf16)
            vs[pair, at] = v.astype(bf16)
            v_turned[pair, :, at] = v.T.astype(bf16)
            both = do[:, pair * CHUNK : (pair + 1) * CHUNK].astype(f32)
            dos[2 * pair, at] = jnp.where(lane < HD, both, 0.0).astype(bf16)
            dos[2 * pair + 1, at] = jnp.where(lane < HD, 0.0, both).astype(bf16)

    def project_prompt(i, _):
        project(i)
        turn_evenly(0, i, prompt_tiles, project_turns)
        return 0

    lax.fori_loop(0, prompt_tiles, project_prompt, 0)
    for c in over_y:
        c.wait()
    for c in over_core:
        c.start()

    query_lane = lax.broadcasted_iota(jnp.int32, (1, TILE), 1)
    reach = jnp.zeros((1, TILE), jnp.int32)
    for m, off in enumerate(offs):
        reach = jnp.where(lax.div(query_lane, jnp.int32(CONT_LEN)) == m, off, reach)

    def attend(pair, _):
        for block in list(range(prompt_tiles - 1, -1, -1)) + [prompt_tiles]:
            first = block * TILE
            seen = first + TILE
            at = slice(first, seen)
            if block == prompt_tiles:
                @pl.when(pair == 0)
                def _():
                    for c in over_core:
                        c.wait()
                    for q in range(n_tensor):
                        for s in range(conts):
                            to = rows + s * CONT_LEN + q * piece
                            x_all[to : to + piece, :] = moved[q, 0, s]
                            dy_all[to : to + piece, :] = moved[q, 1, s]
                    project(jnp.int32(prompt_tiles))

            k, v = ks[pair, :seen], vs[pair, :seen]
            key = lax.broadcasted_iota(jnp.int32, (TILE, TILE), 0)
            query = lax.broadcasted_iota(jnp.int32, (TILE, TILE), 1)
            seen_near = key <= query
            if block == prompt_tiles:
                key_row = lax.broadcasted_iota(jnp.int32, (prompt_len, TILE), 0)
                same = lax.div(key, jnp.int32(CONT_LEN)) == lax.div(query, jnp.int32(CONT_LEN))
                seen_near = seen_near & same
            heads_now = (2 * pair, 2 * pair + 1)
            scores = [dot_nt(k, qs[h, at]) * scale for h in heads_now]
            dprobs = [dot_nt(v, dos[h, at]) for h in heads_now]
            lows, low_slopes, o_turned, dq_turned = [], [], [], []
            for sub in range(2):
                s, dprob = scores[sub], dprobs[sub]
                near = jnp.where(seen_near, s[first:], masked_value)
                if block == prompt_tiles:
                    s = jnp.concatenate([jnp.where(key_row < reach, s[:first], masked_value), near], axis=0)
                else:
                    s = near if first == 0 else jnp.concatenate([s[:first], near], axis=0)
                p = jnp.exp(s - jnp.max(s, axis=0, keepdims=True))
                p = p * (1.0 / jnp.sum(p, axis=0, keepdims=True))
                low = p.astype(bf16)
                delta = jnp.sum(p * dprob, axis=0, keepdims=True)
                ds = (p * (dprob - delta)).astype(bf16)
                part = slice(sub * HD, (sub + 1) * HD)
                o_turned.append(dot(v_turned[pair, part, :seen], low))
                dq_turned.append(dot(k_turned[pair, part, :seen], ds))
                lows.append(low)
                low_slopes.append(ds)
            o_all[at, span(pair * CHUNK, CHUNK, CHUNK)] = jnp.concatenate(o_turned, axis=0).T.astype(bf16)
            dq = jnp.concatenate(dq_turned, axis=0).T * scale
            dq = turned(dq, table_start(jnp.int32(block)), -1.0).astype(bf16)
            cols = span(3 * pair * CHUNK, CHUNK, CHUNK)
            mixed[at, cols] = dq
            small[6:7, cols] += jnp.sum(dq.astype(f32), axis=0, keepdims=True)
            q_both = jnp.concatenate([qs[h, at] for h in heads_now], axis=0)
            do_both = jnp.concatenate([dos[h, at] for h in heads_now], axis=0)
            dk = dot(jnp.concatenate(low_slopes, axis=1), q_both)
            dv = dot(jnp.concatenate(lows, axis=1), do_both)
            if block == prompt_tiles - 1:
                dks[:seen] = dk
                dvs[:seen] = dv
            else:
                old = min(seen, prompt_len)
                dks[:old] += dk[:old]
                dvs[:old] += dv[:old]
                if old < seen:
                    dks[old:seen] = dk[old:]
                    dvs[old:seen] = dv[old:]
            turn_block(pair, prompt_tiles - 1 - block if block < prompt_tiles else block)

        for i in range(tiles):
            at = slice(i * TILE, (i + 1) * TILE)
            dk = turned(dks[at] * scale, table_start(jnp.int32(i)), -1.0).astype(bf16)
            for c, value in ((1, dk), (2, dvs[at].astype(bf16))):
                cols = span((3 * pair + c) * CHUNK, CHUNK, CHUNK)
                mixed[at, cols] = value
                small[6:7, cols] += jnp.sum(value.astype(f32), axis=0, keepdims=True)
        turn_block(pair, 5)
        return 0

    lax.fori_loop(0, heads // 2, attend, 0)
    for c in deal_da2:
        c.wait()

    def weight_tile(k, _):
        cols = span(k * TILE, TILE, TILE)
        put_tile(wg, k, dot_tn(h_all[:, cols], mixed[:, : 3 * local]), width, n_dp, slice(0, 3 * local))
        put_tile(wg, k, dot_tn(dy_all[cont_total:, cols], o_all[...]), width, n_dp, slice(3 * local, 4 * local))
        turn_evenly(back_from, k, width // TILE, all_turns - back_from - back_turns)
        return 0

    lax.fori_loop(0, width // TILE, weight_tile, 0)
    summing = RingSum(wg, got1, x_send, x_recv, n_dp)
    gathering = RingGather(wg, xg_send, xg_recv, n_dp)
    cont_from = 4
    rest_ticks = 2 * stop - all_turns
    all_ticks = max(stop, rest_ticks, cont_from + n_dp - 1)
    summing.start(jnp.int32(0))

    def back(i, _):
        at = span(i * TILE, TILE, TILE)
        da = dot_nt(mixed[at, : 3 * local], wqkv_v[...])
        da_all[at] = da.astype(bf16)
        xhat, _ = row_stats(x_all[span(i * TILE + cont_total, TILE, TILE)].astype(f32))
        small[0:1] += jnp.sum(da * xhat, axis=0, keepdims=True)
        small[1:2] += jnp.sum(da, axis=0, keepdims=True)

        turn_evenly(all_turns - back_turns, i, tiles, back_turns)
        return 0

    lax.fori_loop(0, tiles, back, 0)
    for c in deal_da1:
        c.start()

    def home_steps(k):
        ahead = lax.rem(spot - k + n_dp, jnp.int32(n_dp))
        back = lax.rem(spot + k, jnp.int32(n_dp))
        return (
            remote(ring.at[ahead, 0], ring.at[ahead, 0], home_send.at[0, k], home_recv.at[0, k], {"dp": after}),
            remote(ring.at[back, 1], ring.at[back, 1], home_send.at[1, k], home_recv.at[1, k], {"dp": before}),
            remote(
                small_ring.at[ahead, 0], small_ring.at[ahead, 0], home_send.at[2, k], home_recv.at[2, k], {"dp": after}
            ),
            remote(
                small_ring.at[back, 1], small_ring.at[back, 1], home_send.at[3, k], home_recv.at[3, k], {"dp": before}
            ),
        )

    def run_ticks(begin, end):
        def one(t, _):
            advance(summing, gathering, t, 2 * (n_dp - 1))

            @pl.when(t < rest_ticks)
            def _():
                sum_step(all_turns + t)

            k = t - cont_from

            @pl.when((k >= 0) & (k < n_dp - 1))
            def _():
                for c in home_steps(k):
                    c.wait()

            @pl.when((k >= 0) & (k < n_dp - 2))
            def _():
                for c in home_steps(k + 1):
                    c.start()

            return 0

        lax.fori_loop(begin, end, one, 0)

    line = lax.div(me_t, jnp.int32(2))
    base_one, base_two, base_y = 4 * few, 4 * few + quarter, 4 * few + 2 * quarter
    depth = base_y + quarter
    group_rows = ((0, base_one), (base_one, 2 * quarter), (base_y, quarter))
    room = rows // depth

    def own_part(m, start, size):
        return (h_all, da_all)[m // room].at[pl.ds((m % room) * depth + start, size)]

    def fill(n, m):
        j = lax.rem(line + (m + 1), jnp.int32(lines))
        return pltpu.make_async_copy(
            stack.at[2 * j + core, pl.ds(*group_rows[n])], own_part(m, *group_rows[n]), fill_sem.at[n, m]
        )

    def to_core(n):
        at = pl.ds(*group_rows[n])
        return [
            remote(
                stack.at[2 * j + 1 - core, at], rc.at[j, at], rc_send.at[n, j], rc_recv.at[n, j], {"tensor": sibling}
            )
            for j in range(lines)
        ]

    def to_line(n):
        return [
            remote(
                own_part(k, *group_rows[n]), ry.at[k, pl.ds(*group_rows[n])], ry_send.at[n, k], ry_recv.at[n, k],
                {"tensor": p},
            )
            for k, p in enumerate(peers)
        ]

    def pass_on(n):
        for c in to_core(n):
            c.wait()
        for k in range(lines - 1):
            j = lax.rem(line + (k + 1), jnp.int32(lines))
            mine = own_part(k, *group_rows[n])
            mine[...] = (mine[...].astype(f32) + rc[j, pl.ds(*group_rows[n])].astype(f32)).astype(bf16)
        for c in to_line(n):
            c.start()

    small_to_core = remote(small, small_core, sc_send, sc_recv, {"tensor": sibling})
    small_to_core.start()
    for c in deal_da1:
        c.wait()
    for c in to_core(1):
        c.start()

    def y_tile(i, _):
        at = span(i * TILE, TILE, TILE)
        total = dot(o_all[at], wd_v[...]) + dot(g_all[span(i * TILE + cont_total, TILE, TILE)], w2_v[...])
        da_all[at] = total.astype(bf16)
        return 0

    lax.fori_loop(0, prompt_tiles, y_tile, 0)
    da_all[prompt_len:] = dot(o_all[prompt_len:], wd_v[...]).astype(bf16)
    y_home[...] = dot(g_all[:cont_total], w2_v[...]).astype(bf16)
    for c in deal_y + deal_home:
        c.start()
    run_ticks(0, 1)
    for c in deal_y + deal_home:
        c.wait()
    for n in (0, 2):
        for c in to_core(n):
            c.start()
    fills = [fill(n, m) for n in (0, 1, 2) for m in range(lines)]
    for c in fills:
        c.start()
    small_to_core.wait()
    row = lax.broadcasted_iota(jnp.int32, (8, 1), 0)
    small_y[line] = small[...] + jnp.where(row < 4, small_core[...], 0.0)
    small_to_line = [
        remote(small_y.at[line], small_y.at[line], sy_send.at[k], sy_recv.at[k], {"tensor": p})
        for k, p in enumerate(peers)
    ]
    for c in small_to_line:
        c.start()
    for c in fills:
        c.wait()
    pass_on(0)
    run_ticks(1, 2)
    pass_on(1)
    pass_on(2)
    for c in small_to_line:
        c.wait()
    reduced = small_y[0]
    for j in range(1, lines):
        reduced = reduced + small_y[j]
    reduced = jnp.where(row < 4, reduced, small[...]).astype(bf16)
    fold = width // 4
    for part in range(4):
        small_ring[spot, part // 2, part % 2 * 8 : part % 2 * 8 + 8] = reduced[:, part * fold : (part + 1) * fold]
    run_ticks(2, cont_from)

    def summed(start, size):
        total = own_part(lines - 1, start, size)[...].astype(f32) + rc[line, pl.ds(start, size)].astype(f32)
        for k in range(lines - 1):
            total = total + ry[k, pl.ds(start, size)].astype(f32)
        return total

    def quarter_rows(q):
        return pl.ds(pl.multiple_of(q * quarter, 16), quarter)

    gain_two = as_row(gain_two_ref)
    both = as_row(bias_one_ref) + as_row(bias_two_ref)
    results = (out_p, grad_p)

    def gather_line(a):
        at = quarter_rows(me_t)
        return [pltpu.make_async_copy(own_rows.at[a], results[a].at[at], rows_sem.at[a])] + [
            remote(own_rows.at[a], results[a].at[at], gl_send.at[a, k], gl_recv.at[a, k], {"tensor": p})
            for k, p in enumerate(peers)
        ]

    def to_sibling(a):
        at = quarter_rows(me_t)
        return [remote(own_rows.at[a], results[a].at[at], gc_send.at[a, 0], gc_recv.at[a, 0], {"tensor": sibling})]

    def gather_core(a):
        copies = []
        for k in range(1, lines):
            at = quarter_rows(2 * lax.rem(line + k, jnp.int32(lines)) + core)
            copies.append(
                remote(results[a].at[at], results[a].at[at], gc_send.at[a, k], gc_recv.at[a, k], {"tensor": sibling})
            )
        return copies

    for c in to_line(0):
        c.wait()
    for s in range(conts):
        ring[spot, 0, s] = summed(s * piece, piece).astype(bf16)
        theirs = x_all[span(rows + s * CONT_LEN + me_t * piece, piece, 16)].astype(f32)
        ring[spot, 1, s] = norm_pull(theirs, summed(2 * few + s * piece, piece) * gain).astype(bf16)
        home = span(s * CONT_LEN + me_t * piece, piece, 16)
        x_home = x_all[home].astype(f32)
        keep_y[s] = x_home + summed(few + s * piece, piece) + both
        pulled = norm_pull(x_home, summed(3 * few + s * piece, piece) * gain_two)
        keep_d[s] = dy_all[home].astype(f32) + pulled
    for c in home_steps(jnp.int32(0)):
        c.start()
    run_ticks(cont_from, cont_from + 3)
    quarter_at = span(cont_total + me_t * quarter, quarter, 16)
    for c in to_line(1):
        c.wait()
    e = summed(base_one, quarter) * gain + summed(base_two, quarter) * gain_two
    own_rows[1] = (dy_all[quarter_at].astype(f32) + norm_pull(x_all[quarter_at].astype(f32), e)).astype(bf16)
    for c in gather_line(1) + to_sibling(1):
        c.start()
    run_ticks(cont_from + 3, cont_from + 5)
    for c in to_line(2):
        c.wait()
    own_rows[0] = (x_all[quarter_at].astype(f32) + summed(base_y, quarter) + both).astype(bf16)
    for c in gather_line(0) + to_sibling(0):
        c.start()
    moved_home = cont_from + n_dp - 1
    run_ticks(cont_from + 5, moved_home)
    for part in range(4):
        at = slice(part % 2 * 8, part % 2 * 8 + 8)
        total = small_ring[0, part // 2, at].astype(f32)
        for j in range(1, n_dp):
            total = total + small_ring[j, part // 2, at].astype(f32)
        vec_out[:, part * fold : (part + 1) * fold] = total
    for s in range(conts):
        mine = me_dp * conts + s
        group = group_ref[mine]
        first, _ = find_members(group_ref, group)
        slot = jnp.where(first == mine, jnp.int32(0), jnp.int32(1))
        where = ring_spot(group, n_dp)
        fin[me_t, 0, s] = (keep_y[s] + ring[where, 0, slot].astype(f32)).astype(bf16)
        fin[me_t, 1, s] = (keep_d[s] + ring[where, 1, slot].astype(f32)).astype(bf16)
    fin_line = [
        remote(fin.at[me_t], fin.at[me_t], fin_send.at[k], fin_recv.at[k], {"tensor": p})
        for k, p in enumerate(peers)
    ]
    fin_core = [
        remote(
            fin.at[2 * j + core], fin.at[2 * j + core], finc_send.at[j], finc_recv.at[j], {"tensor": sibling}
        )
        for j in range(lines)
    ]
    for c in fin_line:
        c.start()
    for c in gather_line(1):
        c.wait()
    for c in gather_core(1):
        c.start()
    run_ticks(moved_home, moved_home + 2)
    for c in gather_line(0):
        c.wait()
    for c in gather_core(0):
        c.start()
    if rest_ticks <= moved_home + 2:
        for c in outs[:2]:
            c.start()
    run_ticks(moved_home + 2, max(moved_home + 2, all_ticks))
    for c in outs if rest_ticks > moved_home + 2 else outs[2:]:
        c.start()
    for c in fin_line:
        c.wait()
    for c in fin_core:
        c.start()
    for c in gather_core(0) + to_sibling(0) + gather_core(1) + to_sibling(1) + fin_core:
        c.wait()
    last = [
        pltpu.make_async_copy(
            fin.at[q, a, s], dst.at[pl.ds(s * CONT_LEN + q * piece, piece)], outc_sem.at[a, q, s]
        )
        for a, dst in ((0, out_c), (1, grad_c))
        for q in range(n_tensor)
        for s in range(conts)
    ]
    for c in last:
        c.start()
    for c in last + outs:
        c.wait()


def run_layer(n_dp, n_tensor, early, group_of, offsets, xp, xc, dp, dc, w1, w2, wqkv, wd, *vectors):
    prompt_len, width = xp.shape
    cont_total = xc.shape[0]
    rows = prompt_len + cont_total
    hidden = w1.shape[1]
    local = wd.shape[0]
    heads = local // HD
    piece = CONT_LEN // n_tensor
    lines = n_tensor // 2
    table = jnp.asarray(rotary_table(prompt_len + CONT_LEN))
    table_rows = table.shape[1] + MEMBERS * CONT_LEN
    up, down = ring_shape(width, hidden, n_dp), ring_shape(hidden, width, n_dp)
    third = ring_shape(width, 4 * local, n_dp)
    quarter = prompt_len // n_tensor
    depth = 4 * MEMBERS * piece + 3 * quarter
    shape = jax.ShapeDtypeStruct
    hbm = pl.BlockSpec(memory_space=pl.ANY)
    vmem = pl.BlockSpec(memory_space=pltpu.VMEM)
    smem = pl.BlockSpec(memory_space=pltpu.SMEM)
    sem = pltpu.SemaphoreType.DMA
    return pl.pallas_call(
        functools.partial(layer_kernel, n_dp, n_tensor, early),
        out_shape=(
            shape(xp.shape, bf16),
            shape(xc.shape, bf16),
            shape(xp.shape, bf16),
            shape(xc.shape, bf16),
            shape(up, bf16),
            shape(down, bf16),
            shape(third, bf16),
            shape((n_tensor, depth, width), bf16),
            shape((8, width), f32),
        ),
        in_specs=[smem] * 2 + [hbm] * 9 + [vmem] * 8,
        out_specs=(hbm,) * 8 + (vmem,),
        scratch_shapes=[
            pltpu.VMEM((rows + cont_total, width), bf16),
            pltpu.VMEM((rows + cont_total, width), bf16),
            pltpu.VMEM((width, hidden), bf16),
            pltpu.VMEM((hidden, width), bf16),
            pltpu.VMEM((width, 3 * local), bf16),
            pltpu.VMEM((local, width), bf16),
            pltpu.VMEM((3, table_rows, CHUNK), f32),
            pltpu.VMEM((rows, width), bf16),
            pltpu.VMEM((rows, hidden), bf16),
            pltpu.VMEM((rows, max(hidden, 3 * local)), bf16),
            pltpu.VMEM((rows, width), bf16),
            pltpu.VMEM((n_dp, 2, MEMBERS, piece, width), bf16),
            pltpu.VMEM((n_tensor, 2, MEMBERS, piece, width), bf16),
            pltpu.VMEM(up, bf16),
            pltpu.VMEM(down, bf16),
            pltpu.VMEM((n_dp - 1,) + up[1:], bf16),
            pltpu.VMEM((n_dp - 1,) + down[1:], bf16),
            pltpu.VMEM(third, bf16),
        ]
        + [pltpu.VMEM((heads, rows, CHUNK), bf16)] * 2
        + [pltpu.VMEM((heads // 2, rows, CHUNK), bf16)] * 2
        + [pltpu.VMEM((heads // 2, CHUNK, rows), bf16)] * 2
        + [pltpu.VMEM((rows, CHUNK), f32)] * 2
        + [
            pltpu.VMEM((rows, local), bf16),
            pltpu.VMEM((cont_total, width), bf16),
            pltpu.VMEM((lines, depth, width), bf16),
            pltpu.VMEM((lines - 1, depth, width), bf16),
            pltpu.VMEM((2, quarter, width), bf16),
            pltpu.VMEM((MEMBERS, piece, width), f32),
            pltpu.VMEM((MEMBERS, piece, width), f32),
            pltpu.VMEM((n_tensor, 2, MEMBERS, piece, width), bf16),
            pltpu.VMEM((8, width), f32),
            pltpu.VMEM((8, width), f32),
            pltpu.VMEM((lines, 8, width), f32),
            pltpu.VMEM((n_dp, 2, 16, width // 4), bf16),
            sem((2, MEMBERS)),
            sem((9,)),
            sem((3,)),
            sem((3, n_tensor, MEMBERS + 1)),
            sem((n_tensor, MEMBERS)),
            sem((MEMBERS, 2, 2, n_dp - 1)),
            sem((MEMBERS, 2, 2, n_dp - 1)),
            sem((lines - 1,)),
            sem((lines - 1,)),
            sem((lines,)),
            sem((lines,)),
        ]
        + [sem((2, 2, n_dp - 1))] * 4
        + [sem((3, lines))] * 3
        + [sem((3, lines - 1))] * 2
        + [sem((2, lines - 1))] * 2
        + [sem((2, lines))] * 2
        + [sem((4, n_dp - 1))] * 2
        + [sem] * 2
        + [sem((lines - 1,))] * 4
        + [sem((lines,))] * 2
        + [sem((2,)), sem((2, n_tensor, MEMBERS))]
        + [sem((2, n_dp - 1))] * 4,
        compiler_params=pltpu.CompilerParams(
            collective_id=0, has_side_effects=True, vmem_limit_bytes=63 * 2**20
        ),
        cost_estimate=pl.CostEstimate(flops=34 * 10**9, bytes_accessed=40 * 10**6, transcendentals=5 * 10**6),
        name="layer",
    )(group_of, offsets, xp, xc, dp, dc, w1, w2, wqkv, wd, table, *vectors)


def finish_kernel(
    groups, out_p, out_c, grad_p, grad_c, w1s, w2s, wg, total,
    out_p_out, out_c_out, grad_p_out, grad_c_out, gain_one, shift_one, gain_two, shift_two,
    qkv_out, qkv_bias, dense_out, dense_bias, w1_out, w1_bias, w2_out, w2_bias,
    out_p_v, out_c_v, grad_p_v, grad_c_v, w1s_v, w2s_v, wg_v, qkv_v, dense_v, w1_v, w2_v,
    copy_in, copy_out, piece_in, piece_out, dense_sem,
):
    local3 = qkv_out.shape[1]
    plain = (
        (out_p, out_p_v, out_p_out), (grad_p, grad_p_v, grad_p_out),
        (out_c, out_c_v, out_c_out), (grad_c, grad_c_v, grad_c_out),
    )
    plain_in = [pltpu.make_async_copy(a, b, copy_in.at[i]) for i, (a, b, _) in enumerate(plain)]
    plain_out = [pltpu.make_async_copy(b, c, copy_out.at[i]) for i, (_, b, c) in enumerate(plain)]
    weights = ((w1s, w1s_v, w1_v, w1_out), (w2s, w2s_v, w2_v, w2_out), (wg, wg_v, qkv_v, qkv_out))

    def chunks_of(a, g):
        return pl.ds(g * (a.shape[0] // groups), a.shape[0] // groups)

    def rows_of(a, g):
        return pl.ds(g * (a.shape[0] // groups), a.shape[0] // groups)

    loads = [
        [pltpu.make_async_copy(a.at[chunks_of(a, g)], b.at[chunks_of(a, g)], piece_in.at[i, g]) for g in range(groups)]
        for i, (a, b, _, _) in enumerate(weights)
    ]
    stores = [
        [pltpu.make_async_copy(c.at[rows_of(c, g)], d.at[rows_of(c, g)], piece_out.at[i, g]) for g in range(groups)]
        for i, (_, _, c, d) in enumerate(weights)
    ]
    for c in plain_in[:1] + loads[0] + plain_in[1:2] + loads[1] + plain_in[2:] + loads[2]:
        c.start()
    lane = lax.broadcasted_iota(jnp.int32, (1, CHUNK), 1)
    pairs = [
        [slice((3 * pair + c) * CHUNK, (3 * pair + c + 1) * CHUNK) for c in range(3)]
        for pair in range(local3 // (3 * CHUNK))
    ]
    for n, dst in enumerate((gain_one, shift_one, gain_two, shift_two, dense_bias, w1_bias)):
        dst[...] = total[n, : dst.shape[0]]
    w2_bias[...] = total[4, :]
    for columns in pairs:
        for cols, value in zip(columns, unpair_columns(*(total[6:7, cols] for cols in columns), lane)):
            qkv_bias[cols] = value[0]

    def pieces(src, dst, g):
        per_group = src.shape[0] // groups
        size = dst.shape[0] // (2 * src.shape[0])
        for p in range(2 * per_group):
            first = g * (dst.shape[0] // groups) + p * size
            yield g * per_group + p // 2, p % 2, size, slice(first, first + size)

    for i in range(2):
        plain_in[i].wait()
        plain_out[i].start()
        _, src, dst, _ = weights[i]
        for g in range(groups):
            loads[i][g].wait()
            for chunk, way, size, to in pieces(src, dst, g):
                dst[to, :] = src[chunk, way, :size].astype(f32)
            stores[i][g].start()
    for i in (2, 3):
        plain_in[i].wait()
        plain_out[i].start()
    for g in range(groups):
        loads[2][g].wait()
        dense = []
        for chunk, way, size, to in pieces(wg_v, qkv_v, g):
            for columns in pairs:
                parts = unpair_columns(*(wg_v[chunk, way, :size, cols].astype(f32) for cols in columns), lane)
                for cols, value in zip(columns, parts):
                    qkv_v[to, cols] = value
            dense.append(wg_v[chunk, way, :size, local3:].astype(f32))
        stores[2][g].start()
        size = dense_v.shape[1] // groups
        dense_v[:, g * size : (g + 1) * size] = jnp.concatenate(dense, axis=0).T
    last = pltpu.make_async_copy(dense_v, dense_out, dense_sem)
    last.start()
    for c in plain_out + stores[0] + stores[1] + stores[2] + [last]:
        c.wait()


def run_finish(local3, hidden, out_p, out_c, grad_p, grad_c, w1s, w2s, wg, total):
    width = out_p.shape[1]
    local = local3 // 3
    groups = 4
    shape = jax.ShapeDtypeStruct
    hbm = pl.BlockSpec(memory_space=pl.ANY)
    vmem = pl.BlockSpec(memory_space=pltpu.VMEM)
    sem = pltpu.SemaphoreType.DMA
    moved = (out_p, out_c, grad_p, grad_c)
    return pl.pallas_call(
        functools.partial(finish_kernel, groups),
        out_shape=tuple(shape(a.shape, bf16) for a in moved)
        + (shape((width,), f32),) * 4
        + (
            shape((width, local3), f32), shape((local3,), f32),
            shape((local, width), f32), shape((width,), f32),
            shape((width, hidden), f32), shape((hidden,), f32),
            shape((hidden, width), f32), shape((width,), f32),
        ),
        in_specs=[hbm] * 7 + [vmem],
        out_specs=(hbm,) * 4 + (vmem,) * 4 + (hbm, vmem) * 4,
        scratch_shapes=[pltpu.VMEM(a.shape, bf16) for a in moved + (w1s, w2s, wg)]
        + [
            pltpu.VMEM((width, local3), f32),
            pltpu.VMEM((local, width), f32),
            pltpu.VMEM((width, hidden), f32),
            pltpu.VMEM((hidden, width), f32),
            sem((4,)),
            sem((4,)),
            sem((3, groups)),
            sem((3, groups)),
            sem,
        ],
        compiler_params=pltpu.CompilerParams(vmem_limit_bytes=60 * 2**20),
        name="finish",
    )(out_p, out_c, grad_p, grad_c, w1s, w2s, wg, total)


def per_device(
    n_dp, n_tensor,
    prompt_in, cont_in, prompt_cot, cont_cot, group_of, offsets, ln1_gain, ln1_bias, ln2_gain, ln2_bias,
    qkv_weight, qkv_bias, dense_weight, dense_bias, fc1_weight, fc1_bias, fc2_weight, fc2_bias,
):
    width = prompt_in.shape[1]
    hidden = fc1_weight.shape[1]
    local3 = qkv_weight.shape[1]

    out_p, out_c, grad_p, grad_c, w1g, w2g, wg, _, total = run_layer(
        n_dp, n_tensor, min(n_dp - 1, 1), group_of, offsets, prompt_in, cont_in, prompt_cot, cont_cot,
        fc1_weight, fc2_weight, qkv_weight, dense_weight,
        ln2_gain, ln2_bias, fc1_bias, ln1_gain, ln1_bias, qkv_bias, dense_bias, fc2_bias,
    )
    return run_finish(local3, hidden, out_p, out_c, grad_p, grad_c, w1g, w2g, wg, total)


def solution(mesh):
    rows, whole, columns, segment, depth = P("dp", None), P(), P(None, "tensor"), P("tensor"), P("tensor", None)
    return jax.shard_map(
        functools.partial(per_device, mesh.shape["dp"], mesh.shape["tensor"]),
        mesh=mesh,
        in_specs=(
            rows, rows, rows, rows, whole, whole, whole, whole, whole, whole,
            columns, segment, depth, whole, columns, segment, depth, whole,
        ),
        out_specs=(
            rows, rows, rows, rows, whole, whole, whole, whole,
            columns, segment, depth, whole, columns, segment, depth, whole,
        ),
        check_vma=False,
    )
```
